32 devices in a mesh: rep: 4 (over y, x), grp: 8 (over z, core).
Axes of the slice: x: 2, y: 2, z: 4, core: 2. Of those that a mesh axis runs over, the one named last changes fastest.
Arguments:
- tokens: bfloat16 [32768, 768], P(('rep', 'grp')), may hold values from -6 to 6
- segments: int32 [32768], P(('rep', 'grp')), may hold values from 0 to 17, as said below
- routes: int32 [32768, 2], P(('rep', 'grp')), may hold values from 0 to 15, all different within a row; in each aligned block of 1024 rows (0 to 1023, 1024 to 2047, ...) at most 256 rows name the same one
- gain_attn: bfloat16 [768], P('grp'), may hold values from 0.5 to 1.5
- w_query: bfloat16 [768, 768], P('grp'), may hold values from -0.21875 to 0.21875
- w_key: bfloat16 [768, 768], P('grp'), may hold values from -0.21875 to 0.21875
- w_value: bfloat16 [768, 768], P('grp'), may hold values from -0.21875 to 0.21875
- w_output: bfloat16 [768, 768], P('grp'), may hold values from -1.75 to 1.75
- rel_bias: bfloat16 [32, 12], P('grp'), may hold values from -4 to 4
- gain_ffn: bfloat16 [768], P('grp'), may hold values from 0.5 to 1.5
- router: bfloat16 [768, 16], P('grp'), may hold values from -0.21875 to 0.21875
- w_in: bfloat16 [16, 768, 3072], P('grp'), may hold values from -0.21875 to 0.21875
- w_out: bfloat16 [16, 3072, 768], P('grp'), may hold values from -0.109375 to 0.109375
- cotangent: bfloat16 [32768, 768], P(('rep', 'grp')), may hold values from -6 to 6
Outputs:
- out: bfloat16 [32768, 768], P(('rep', 'grp'))
- loss: float32 [], replicated
- balance_terms: float32 [16], replicated
- x_grad: float32 [32768, 768], P(('rep', 'grp'))
- gain_attn_grad: float32 [768], P('grp')
- w_query_grad: float32 [768, 768], P('grp')
- w_key_grad: float32 [768, 768], P('grp')
- w_value_grad: float32 [768, 768], P('grp')
- w_output_grad: float32 [768, 768], P('grp')
- rel_bias_grad: float32 [32, 12], P('grp')
- gain_ffn_grad: float32 [768], P('grp')
- router_grad: float32 [768, 16], P('grp')
- w_in_grad: float32 [16, 768, 3072], P('grp', 'rep')
- w_out_grad: float32 [16, 3072, 768], P('grp', 'rep')
The draws below stay inside these ranges and needn't reach their ends.
Inputs may be any that keep to these rules, and one draw needn't show every extreme that they name: `segments`: within each sequence of 1024 tokens, documents carry ids 1, 2, 3 in order, each of 60 to 800 tokens; id 0 marks padding after the last document. The first sequence holds documents of exactly 60 tokens. `routes`: A token's 2 experts differ. In the rows of one device no expert is named more than 256 times, and this bound is reached.
All inputs are finite; a program needn't handle non-finite values.
Results may differ from the reference program's by a relative error of at most 0.013.
Values may be sent and summed in bfloat16 or wider, within the bound.
A program may use at most 384 MiB of HBM per device.

```python
import math
import jax
import jax.numpy as jnp
import numpy as np
from jax import lax

D = 768
HEADS = 12
HEAD_DIM = 64
FF = 3072
TOP = 2
SEQ = 1024
BUCKETS = 32
DOC_MIN = 60
DOC_MAX = 800
EXPERTS = 16
TOK_DEV = 1024
TOKENS = 32768
CAP = 256
DEVICES = 32


def draw_segments(key, part):
    seq_count = TOKENS // SEQ
    most_docs = SEQ // DOC_MIN + 1
    doc_sizes = jax.random.randint(key, (seq_count, most_docs), DOC_MIN, DOC_MAX + 1).astype(jnp.int32)
    first_row = (jnp.arange(seq_count, dtype=jnp.int32) == 0)[:, None]
    doc_sizes = jnp.where(first_row, jnp.int32(DOC_MIN), doc_sizes).astype(jnp.int32)
    doc_ends = jnp.cumsum(doc_sizes, axis=1).astype(jnp.int32)
    places = jnp.arange(SEQ, dtype=jnp.int32)
    finished = jnp.sum((doc_ends[:, None, :] <= places[None, :, None]).astype(jnp.int32), axis=2)
    filled = jnp.max(jnp.where(doc_ends <= SEQ, doc_ends, 0), axis=1)
    doc_ids = jnp.where(places[None, :] < filled[:, None], finished + 1, 0)
    return doc_ids.reshape(TOKENS).astype(jnp.int32)


def shard_levels(key, extent, shards, smallest, largest):
    def one(axis_at, parts):
        steps = jax.random.uniform(jax.random.fold_in(jax.random.fold_in(key, 6), axis_at), (parts,), jnp.float32, smallest / len(shards), largest / len(shards))
        return jnp.repeat(jnp.exp(steps), extent[axis_at] // parts).reshape((-1,) + (1,) * (len(extent) - axis_at - 1))

    gain = one(*shards[0])
    for cut in shards[1:]:
        gain = gain * one(*cut)
    return gain


def shared_out(key, own, number, rows, count, top, bound, lean):
    order = jax.random.permutation(key, count)
    crowded, ordinary = load_shares(count, rows * top, bound, lean, True), load_shares(count, rows * top, bound, lean, False)
    places = jnp.arange(count)

    def named(lengths, offset_by):
        used = int((lengths > 0).sum())
        fixed = max(1, used // 4)
        passed = fixed + (places - fixed + offset_by * (used - fixed)) % max(1, count - fixed)
        return jnp.zeros((count,), jnp.int32).at[order[jnp.where(places < fixed, places, passed)]].set(jnp.asarray(lengths, jnp.int32))

    lengths = jnp.where(number % 4 == 0, named(crowded, number // 4), named(ordinary, number - number // 4 - 1))
    mixed = jax.random.permutation(jax.random.fold_in(own, 3), count)
    source_of, sink = mixed[0:count // 2 * 2:2], mixed[1:count // 2 * 2:2]
    room = jnp.minimum(lengths[source_of] - 1, bound - lengths[sink]) // 2
    room = jnp.where((source_of == order[0]) | (sink == order[0]) | (lengths[sink] == 0), 0, jnp.maximum(room, 0))
    passed = jax.random.randint(jax.random.fold_in(own, 4), (count // 2,), 0, 1 << 20) % (room + 1)
    lengths = lengths.at[source_of].add(-passed).at[sink].add(passed)
    labels = jnp.searchsorted(jnp.cumsum(lengths), jnp.arange(rows * top), side="right").astype(jnp.int32)
    table = labels.reshape(top, rows).T
    table = table[jax.random.permutation(jax.random.fold_in(own, 1), rows)]
    offset_by = jax.random.randint(jax.random.fold_in(own, 2), (rows, 1), 0, top)
    return jnp.take_along_axis(table, (jnp.arange(top)[None, :] + offset_by) % top, axis=1)


def load_shares(amount, total, reach, lean, full):
    loads = [(1 << 20) // math.isqrt(rank ** lean) + 1 for rank in range(1, amount + 1)]
    largest = reach if full else min(reach, max(-(-total // amount), total * loads[0] // sum(loads)))
    least = 1 if total - largest >= amount - 1 else 0
    holding, spare = [largest] + [least] * (amount - 1), total - largest - least * (amount - 1)
    while spare > 0:
        movable = [i for i in range(1, amount) if holding[i] < largest] or [i for i in range(1, amount) if holding[i] < reach]
        mass, remaining = sum([loads[i] for i in movable]), spare
        for i in movable:
            extra = min(reach - holding[i], max(1, remaining * loads[i] // mass), spare)
            holding[i] = holding[i] + extra
            spare = spare - extra
    return np.array(holding)


def gaussian(own_key, dims, deviation, limit, pieces=(), held_as=jnp.bfloat16):
    loudness = shard_levels(own_key, dims, pieces, -0.22, 0.18) if pieces else 1.0
    entries = jax.random.normal(own_key, dims, jnp.float32) * deviation * loudness
    return jnp.minimum(jnp.maximum(entries, -limit), limit).astype(held_as)


def setup_inputs(seed: int = 0) -> dict:
    keys = jax.random.split(jax.random.key(seed), 15)
    tokens = gaussian(keys[0], (TOKENS, D), 1.0, 6.0, ((0, 32),))
    segments = draw_segments(jax.random.fold_in(keys[14], 71), 0)
    routes_keys = jax.random.split(jax.random.fold_in(keys[2], 1), TOKENS // TOK_DEV)
    routes_turns = jax.random.permutation(jax.random.fold_in(keys[2], 3), TOKENS // TOK_DEV)
    routes = jax.vmap(lambda own, number: shared_out(jax.random.fold_in(keys[2], 2), own, number, TOK_DEV, EXPERTS, TOP, CAP, 1))(routes_keys, routes_turns).reshape((TOKENS, TOP))
    gain_attn = jnp.clip(1.0 + 0.1 * jax.random.normal(keys[3], (D,), jnp.float32), 0.5, 1.5).astype(jnp.bfloat16)
    w_query = gaussian(keys[4], (D, D), D ** -0.5, 0.21875, ((0, 8),))
    w_key = gaussian(keys[5], (D, D), D ** -0.5, 0.21875, ((0, 8),))
    w_value = gaussian(keys[6], (D, D), D ** -0.5, 0.21875, ((0, 8),))
    w_output = gaussian(keys[7], (D, D), (D // 64) ** -0.5, 1.75, ((0, 8),))
    rel_bias = gaussian(keys[8], (BUCKETS, HEADS), 1.0, 4.0, ((0, 8),))
    gain_ffn = jnp.clip(1.0 + 0.1 * jax.random.normal(keys[9], (D,), jnp.float32), 0.5, 1.5).astype(jnp.bfloat16)
    router = gaussian(keys[10], (D, EXPERTS), D ** -0.5, 0.21875, ((0, 8),))
    w_in = gaussian(keys[11], (EXPERTS, D, FF), D ** -0.5, 0.21875, ((0, 8),))
    w_out = gaussian(keys[12], (EXPERTS, FF, D), FF ** -0.5, 0.109375, ((0, 8),))
    cotangent = gaussian(keys[13], (TOKENS, D), 1.0, 6.0, ((0, 32),))
    return {"tokens": tokens, "segments": segments, "routes": routes, "gain_attn": gain_attn, "w_query": w_query, "w_key": w_key, "w_value": w_value, "w_output": w_output, "rel_bias": rel_bias, "gain_ffn": gain_ffn, "router": router, "w_in": w_in, "w_out": w_out, "cotangent": cotangent}


norm_eps = 1e-06
aux_weight = 0.01
far_marks = (18, 20, 23, 26, 30, 34, 39, 45, 51, 58, 66, 76, 86, 98, 112)

@jax.custom_vjp
def low(v):
    return lax.optimization_barrier(v.astype(jnp.bfloat16)).astype(jnp.float32)

@jax.custom_vjp
def low_back(v):
    return v

def low_keep(v):
    return (low(v), None)

def low_pass(kept, grad):
    return (grad,)

def back_keep(v):
    return (v, None)

def back_low(kept, grad):
    return (low(grad),)
low.defvjp(low_keep, low_pass)
low_back.defvjp(back_keep, back_low)

def both(values):
    return low(low_back(values))

def rms_scale(values):
    return lax.rsqrt(lax.optimization_barrier(jnp.mean(values * values, axis=-1, keepdims=True)) + norm_eps)

def positions_of(seg_row):
    length = seg_row.shape[0]
    places = lax.iota(jnp.int32, length)
    before = jnp.concatenate([seg_row[:1] - 1, seg_row[:-1]])
    starts = jnp.where(seg_row != before, places, 0)
    return places - lax.cummax(starts, axis=0)

def bucket_of(distance):
    far_part = jnp.zeros_like(distance)
    for far_mark in far_marks:
        far_part = far_part + (distance >= far_mark).astype(jnp.int32)
    return jnp.minimum(distance, 16) + far_part

def attend_one(query_seq, key_seq, value_seq, seg_row, table):
    high = lax.Precision.HIGHEST
    length = seg_row.shape[0]
    pos_row = positions_of(seg_row)
    distance = jnp.maximum(pos_row[:, None] - pos_row[None, :], 0)
    biases = jnp.transpose(jnp.take(table, bucket_of(distance), axis=0), (2, 0, 1))
    scores = jnp.einsum('qhd,khd->hqk', query_seq, key_seq, precision=high) * HEAD_DIM ** (-0.5) + biases
    scores = low_back(scores)
    places = lax.iota(jnp.int32, length)
    allowed = (seg_row[:, None] == seg_row[None, :]) & (places[None, :] <= places[:, None]) & ((seg_row[:, None] != 0) | (places[None, :] == places[:, None]))
    weights = jax.nn.softmax(jnp.where(allowed[None], scores, -1e+30), axis=-1)
    context = jnp.einsum('hqk,khd->qhd', low(weights), value_seq, precision=high)
    return both(context.reshape(length, D))

def forward(inputs, gain_attn, w_query, w_key, w_value, w_output, rel_bias, gain_ffn, router, w_in, w_out, segments, routes):
    high = lax.Precision.HIGHEST
    normed_one = low(inputs * rms_scale(inputs) * gain_attn)
    query_rows = both(jnp.dot(normed_one, w_query, precision=high))
    key_rows = both(jnp.dot(normed_one, w_key, precision=high))
    value_rows = both(jnp.dot(normed_one, w_value, precision=high))
    seq_count = TOKENS // SEQ
    head_shape = (seq_count, SEQ, HEADS, HEAD_DIM)

    def attend(packed):
        return attend_one(packed[0], packed[1], packed[2], packed[3], rel_bias)
    context = lax.map(jax.checkpoint(attend), (query_rows.reshape(head_shape), key_rows.reshape(head_shape), value_rows.reshape(head_shape), segments.reshape(seq_count, SEQ)))
    context = context.reshape(TOKENS, D)
    hidden_one = inputs + low_back(jnp.dot(context, w_output, precision=high))
    normed_two = low(hidden_one * rms_scale(hidden_one) * gain_ffn)
    logits = low_back(jnp.dot(normed_two, router, precision=high))
    router_prob = jax.nn.softmax(logits, axis=-1)
    choose = routes[:, :, None] == lax.iota(jnp.int32, EXPERTS)[None, None, :]
    picked_prob = lax.optimization_barrier(jnp.sum(jnp.where(choose, router_prob[:, None, :], 0.0), axis=-1))
    gates = picked_prob / lax.optimization_barrier(jnp.sum(picked_prob, axis=-1, keepdims=True))
    fraction = lax.optimization_barrier(jnp.sum(choose.astype(jnp.float32), axis=(0, 1))) / (TOP * TOKENS)
    balance_terms = EXPERTS * EXPERTS * fraction * lax.optimization_barrier(jnp.mean(router_prob, axis=0))
    loss = aux_weight / EXPERTS * jnp.sum(balance_terms)
    dev_routes = routes.reshape(DEVICES, TOK_DEV * TOP)
    dev_hot = (dev_routes[:, :, None] == lax.iota(jnp.int32, EXPERTS)[None, None, :]).astype(jnp.int32)
    slots = lax.optimization_barrier(jnp.sum((jnp.cumsum(dev_hot, axis=1) - dev_hot) * dev_hot, axis=2)).astype(jnp.int32)
    owners = jnp.broadcast_to(lax.iota(jnp.int32, DEVICES)[:, None], dev_routes.shape)
    copies = jnp.repeat(normed_two, TOP, axis=0).reshape(DEVICES, TOK_DEV * TOP, D)
    buffers = jnp.zeros((DEVICES, EXPERTS, CAP, D), jnp.float32).at[owners, dev_routes, slots].add(copies)
    buffers = low_back(buffers)
    by_expert = jnp.transpose(buffers, (1, 0, 2, 3)).reshape(EXPERTS, DEVICES * CAP, D)

    def expert_pass(packed):
        rows_in, weight_in, weight_out = packed
        pre_act = low_back(jnp.dot(rows_in, weight_in, precision=high))
        activated = low(jax.nn.gelu(pre_act, approximate=True))
        return both(jnp.dot(activated, weight_out, precision=high))
    outs_all = lax.map(jax.checkpoint(expert_pass), (by_expert, w_in, w_out))
    returned = jnp.transpose(outs_all.reshape(EXPERTS, DEVICES, CAP, D), (1, 0, 2, 3))
    picked_out = returned[owners, dev_routes, slots].reshape(TOKENS, TOP, D)
    hidden_two = hidden_one + lax.optimization_barrier(jnp.sum(gates[:, :, None] * picked_out, axis=1))
    return (hidden_two, loss, balance_terms)

def reference(tokens, segments, routes, gain_attn, w_query, w_key, w_value, w_output, rel_bias, gain_ffn, router, w_in, w_out, cotangent):
    primals = tuple((array_in.astype(jnp.float32) for array_in in (tokens, gain_attn, w_query, w_key, w_value, w_output, rel_bias, gain_ffn, router, w_in, w_out)))

    def wrapped(*params):
        return forward(*params, segments, routes)
    (hidden_two, loss, balance_terms), pullback = jax.vjp(wrapped, *primals)
    keep_rows = (segments != 0).astype(jnp.float32)[:, None]
    gradients = pullback((cotangent.astype(jnp.float32) * keep_rows, jnp.ones((), jnp.float32), jnp.zeros((EXPERTS,), jnp.float32)))
    return (hidden_two.astype(jnp.bfloat16), loss, balance_terms, gradients[0], gradients[1], gradients[2], gradients[3], gradients[4], gradients[5], gradients[6], gradients[7], gradients[8], gradients[9], gradients[10])
```

```python
from functools import partial

import jax
import jax.numpy as jnp
from jax import lax
from jax.experimental import pallas as pl
from jax.experimental.pallas import tpu as pltpu
from jax.sharding import PartitionSpec as P

TOP = 2
QB = 128
PAIR = 128
NEAR = 2 * QB
SPAN = 3 * QB
OUT_OF_DOC = -1e30
FAR_MARKS = (18, 20, 23, 26, 30, 34, 39, 45, 51, 58, 66, 76, 86, 98, 112)
norm_eps = 1e-06
aux_weight = 0.01
f32, bf16 = jnp.float32, jnp.bfloat16


def rms_scale(values):
    return lax.rsqrt(jnp.mean(values * values, axis=-1, keepdims=True) + norm_eps)


def bucket_of(distance):
    far_part = jnp.zeros_like(distance)
    for far_mark in FAR_MARKS:
        far_part = far_part + (distance >= far_mark).astype(jnp.int32)
    return jnp.minimum(distance, 16) + far_part


def band_hot(buckets):
    lane = lax.broadcasted_iota(jnp.int32, (8, SPAN), 1)
    row = lax.broadcasted_iota(jnp.int32, (8, SPAN), 0)
    turn = (lane - row + SPAN) % SPAN
    diff = jnp.where(turn < QB, turn, turn - SPAN) + QB
    bucket = bucket_of(jnp.maximum(diff, 0)).reshape(1, 8 * SPAN)
    return bucket == lax.iota(jnp.int32, buckets)[:, None]


def split_pair(rows, low_lanes):
    zero = jnp.zeros_like(rows)
    return jnp.concatenate(
        [jnp.where(low_lanes, rows, zero), jnp.where(low_lanes, zero, rows)], axis=0
    )


def fill_mask(seg_col, seg_row, mask):
    seq = mask.shape[0]
    for i in range(seq // QB):
        length = (i + 1) * QB
        sk = seg_col[0:length, :]
        sq = seg_row[:, i * QB:(i + 1) * QB]
        kp = lax.broadcasted_iota(jnp.int32, (length, QB), 0)
        qp = lax.broadcasted_iota(jnp.int32, (length, QB), 1) + i * QB
        ok = (sk == sq) & (kp <= qp) & ((sq != 0) | (kp == qp))
        mask[0:length, i * QB:(i + 1) * QB] = jnp.where(ok, 0.0, OUT_OF_DOC).astype(f32)


def fill_near(base, near):
    for head in range(2):
        rows = base[head]
        for a in range(NEAR // 8):
            turned = rows if a == 0 else pltpu.roll(rows, 8 * a, 1)
            near[8 * a:8 * a + 8, head * QB:(head + 1) * QB] = turned[:, 0:QB]


def scores_chunk(k, lo, hi, qcat, mask, near, i):
    s = lax.dot_general(k[lo:hi, :], qcat, (((1,), (1,)), ((), ())), preferred_element_type=f32)
    m = mask[lo:hi, i * QB:(i + 1) * QB]
    s = s + jnp.concatenate([m, m], axis=1)
    start = (i - 1) * QB
    if lo >= start:
        s = s + near[lo - start:hi - start, :]
    return s


def fwd_kernel(base, seg_col, seg_row, q, k, v, ctx, lse, mask, near, scores, probs, v_t):
    seq = q.shape[0]

    @pl.when(pl.program_id(0) == 0)
    def _():
        fill_mask(seg_col, seg_row, mask)

    fill_near(base, near)
    v_t[...] = v[...].T
    low_lanes = lax.broadcasted_iota(jnp.int32, (QB, PAIR), 1) < PAIR // 2
    scale = (PAIR // 2) ** -0.5
    for i in range(seq // QB):
        qs = slice(i * QB, (i + 1) * QB)
        qcat = split_pair(q[qs, :] * jnp.asarray(scale, bf16), low_lanes)
        top = None
        for c in range(i + 1):
            s = scores_chunk(k, c * QB, (c + 1) * QB, qcat, mask, near, i)
            scores[c * QB:(c + 1) * QB, :] = s
            here = jnp.max(s.reshape(QB // 8, 8, NEAR), axis=0)
            top = here if top is None else jnp.maximum(top, here)
        top = jnp.max(top, axis=0, keepdims=True)
        total = jnp.zeros((8, NEAR), f32)
        for c in range(i + 1):
            p = jnp.exp(scores[c * QB:(c + 1) * QB, :] - top)
            total = total + jnp.sum(p.reshape(QB // 8, 8, NEAR), axis=0)
            probs[c * QB:(c + 1) * QB, :] = p.astype(bf16)
        total = jnp.sum(total, axis=0, keepdims=True)
        length = (i + 1) * QB
        out = jnp.dot(v_t[:, 0:length], probs[0:length, :], preferred_element_type=f32) / total
        half = PAIR // 2
        both = jnp.concatenate([out[0:half, 0:QB], out[half:PAIR, QB:NEAR]], axis=0)
        ctx[qs, :] = both.T.astype(bf16)
        lse[0, i:i + 1, :] = top + jnp.log(total)


def attend(q, k, v, seg, base):
    seq, width = q.shape
    pairs = width // PAIR
    col = pl.BlockSpec((seq, PAIR), lambda h: (0, h))
    whole = lambda *shape: pl.BlockSpec(shape, lambda h: (0,) * len(shape))
    return pl.pallas_call(
        fwd_kernel,
        grid=(pairs,),
        in_specs=[pl.BlockSpec((2, 8, SPAN), lambda h: (h, 0, 0)), whole(seq, 1), whole(1, seq), col, col, col],
        out_specs=[col, pl.BlockSpec((1, seq // QB, NEAR), lambda h: (h, 0, 0))],
        out_shape=[
            jax.ShapeDtypeStruct((seq, width), bf16),
            jax.ShapeDtypeStruct((pairs, seq // QB, NEAR), f32),
        ],
        scratch_shapes=[
            pltpu.VMEM((seq, seq), f32),
            pltpu.VMEM((NEAR, NEAR), f32),
            pltpu.VMEM((seq, NEAR), f32),
            pltpu.VMEM((seq, NEAR), bf16),
            pltpu.VMEM((PAIR, seq), bf16),
        ],
        compiler_params=pltpu.CompilerParams(vmem_limit_bytes=32 * 1024 * 1024),
        cost_estimate=pl.CostEstimate(flops=seq * seq * width * 4, bytes_accessed=8 * seq * width, transcendentals=6 * seq * seq),
        name="attend",
    )(base, seg.reshape(seq, 1), seg.reshape(1, seq), q, k, v)


def bwd_kernel(base, seg_col, seg_row, q, k, v, ctx, dctx, lse, dq, dk, dv, dnear, dfar,
               mask, near, ds_all, p_all, k_t, dk_sum, dv_sum, dnear_sum, dfar_sum):
    seq = q.shape[0]

    @pl.when(pl.program_id(0) == 0)
    def _():
        fill_mask(seg_col, seg_row, mask)

    fill_near(base, near)
    k_t[...] = k[...].T
    low_lanes = lax.broadcasted_iota(jnp.int32, (QB, PAIR), 1) < PAIR // 2
    half = PAIR // 2
    scale = half ** -0.5
    dnear_sum[...] = jnp.zeros_like(dnear_sum)
    dfar_sum[...] = jnp.zeros_like(dfar_sum)
    for i in reversed(range(seq // QB)):
        qs = slice(i * QB, (i + 1) * QB)
        length = (i + 1) * QB
        qcat = split_pair(q[qs, :] * jnp.asarray(scale, bf16), low_lanes)
        dcat = split_pair(dctx[qs, :], low_lanes)
        dots = (ctx[qs, :].astype(f32) * dctx[qs, :].astype(f32)).T
        centre = jnp.concatenate(
            [jnp.sum(dots[0:half], axis=0, keepdims=True), jnp.sum(dots[half:], axis=0, keepdims=True)], axis=1
        )
        norm = lse[0, i:i + 1, :]
        for c in range(i + 1):
            lo, hi = c * QB, (c + 1) * QB
            s = scores_chunk(k, lo, hi, qcat, mask, near, i)
            p = jnp.exp(s - norm)
            p_all[lo:hi, :] = p.astype(bf16)
            dp = lax.dot_general(v[lo:hi, :], dcat, (((1,), (1,)), ((), ())), preferred_element_type=f32)
            ds = p * (dp - centre)
            ds_all[lo:hi, :] = ds.astype(bf16)
            start = (i - 1) * QB
            if lo >= start:
                dnear_sum[lo - start:hi - start, :] += ds
            else:
                dfar_sum[...] += jnp.sum(ds.reshape(QB // 8, 8, NEAR), axis=0)
        out = jnp.dot(k_t[:, 0:length], ds_all[0:length, :], preferred_element_type=f32)
        both = jnp.concatenate([out[0:half, 0:QB], out[half:PAIR, QB:NEAR]], axis=0)
        dq[qs, :] = (both.T * scale).astype(bf16)
        dk_part = jnp.dot(ds_all[0:length, :], qcat, preferred_element_type=f32)
        dv_part = jnp.dot(p_all[0:length, :], dcat, preferred_element_type=f32)
        if i == seq // QB - 1:
            dk_sum[0:length, :] = dk_part
            dv_sum[0:length, :] = dv_part
        else:
            dk_sum[0:length, :] += dk_part
            dv_sum[0:length, :] += dv_part
    dk[...] = dk_sum[...].astype(bf16)
    dv[...] = dv_sum[...].astype(bf16)
    for head in range(2):
        total = jnp.zeros((8, SPAN), f32)
        for a in range(NEAR // 8):
            rows = dnear_sum[8 * a:8 * a + 8, head * QB:(head + 1) * QB]
            rows = jnp.concatenate([rows, jnp.zeros((8, SPAN - QB), f32)], axis=1)
            total = total + (rows if a == 0 else pltpu.roll(rows, SPAN - 8 * a, 1))
        dnear[head] = total
    dfar[0] = dfar_sum[...]


def attend_back(q, k, v, seg, base, ctx, dctx, lse):
    seq, width = q.shape
    pairs = width // PAIR
    col = pl.BlockSpec((seq, PAIR), lambda h: (0, h))
    band = pl.BlockSpec((2, 8, SPAN), lambda h: (h, 0, 0))
    whole = lambda *shape: pl.BlockSpec(shape, lambda h: (0,) * len(shape))
    rows = jax.ShapeDtypeStruct((seq, width), bf16)
    return pl.pallas_call(
        bwd_kernel,
        grid=(pairs,),
        in_specs=[band, whole(seq, 1), whole(1, seq), col, col, col, col, col,
                  pl.BlockSpec((1, seq // QB, NEAR), lambda h: (h, 0, 0))],
        out_specs=[col, col, col, band, pl.BlockSpec((1, 8, NEAR), lambda h: (h, 0, 0))],
        out_shape=[rows, rows, rows, jax.ShapeDtypeStruct((2 * pairs, 8, SPAN), f32),
                   jax.ShapeDtypeStruct((pairs, 8, NEAR), f32)],
        scratch_shapes=[
            pltpu.VMEM((seq, seq), f32),
            pltpu.VMEM((NEAR, NEAR), f32),
            pltpu.VMEM((seq, NEAR), bf16),
            pltpu.VMEM((seq, NEAR), bf16),
            pltpu.VMEM((PAIR, seq), bf16),
            pltpu.VMEM((seq, PAIR), f32),
            pltpu.VMEM((seq, PAIR), f32),
            pltpu.VMEM((NEAR, NEAR), f32),
            pltpu.VMEM((8, NEAR), f32),
        ],
        compiler_params=pltpu.CompilerParams(vmem_limit_bytes=40 * 1024 * 1024),
        cost_estimate=pl.CostEstimate(flops=seq * seq * width * 10, bytes_accessed=16 * seq * width, transcendentals=6 * seq * seq),
        name="attend_back",
    )(base, seg.reshape(seq, 1), seg.reshape(1, seq), q, k, v, ctx, dctx, lse)


def bias_base(table):
    buckets, heads = table.shape
    hot = band_hot(buckets).astype(bf16)
    base = lax.dot_general(table, hot, (((0,), (0,)), ((), ())), preferred_element_type=f32)
    last = table[buckets - 1].astype(f32)
    return base.reshape(heads, 8, SPAN) - last[:, None, None]


def table_back(dnear, dfar, buckets):
    heads = dnear.shape[0]
    hot = band_hot(buckets).astype(f32)
    grad = lax.dot_general(hot, dnear.reshape(heads, 8 * SPAN), (((1,), (1,)), ((), ())),
                           preferred_element_type=f32, precision=lax.Precision.HIGHEST)
    far = jnp.sum(dfar.reshape(heads // 2, 8, 2, QB), axis=(1, 3)).reshape(1, heads)
    last = (lax.iota(jnp.int32, buckets) == buckets - 1)[:, None]
    return grad + jnp.where(last, far, 0.0)


def outer_sum(left_rows, right_rows):
    return lax.dot_general(
        left_rows, right_rows, (((0,), (0,)), ((), ())), preferred_element_type=jnp.float32
    )


def back_proj(grad_rows, weight):
    return lax.dot_general(
        grad_rows, weight, (((1,), (1,)), ((), ())), preferred_element_type=jnp.float32
    )


def shards(
    tokens,
    segments,
    routes,
    gain_attn,
    w_query,
    w_key,
    w_value,
    w_output,
    rel_bias,
    gain_ffn,
    router,
    w_in,
    w_out,
    cotangent,
):
    dense_full = (
        lax.all_gather(gain_attn, "grp", axis=0, tiled=True),
        lax.all_gather(w_query, "grp", axis=0, tiled=True),
        lax.all_gather(w_key, "grp", axis=0, tiled=True),
        lax.all_gather(w_value, "grp", axis=0, tiled=True),
        lax.all_gather(w_output, "grp", axis=0, tiled=True),
        lax.all_gather(rel_bias, "grp", axis=0, tiled=True),
        lax.all_gather(gain_ffn, "grp", axis=0, tiled=True),
        lax.all_gather(router, "grp", axis=0, tiled=True),
    )
    gain_one, query_full, key_full, value_full, output_full, table_full, gain_two, router_full = (
        dense_full
    )
    tok_rows = tokens.shape[0]
    width = tokens.shape[1]
    inputs = tokens.astype(jnp.float32)
    scale_one = rms_scale(inputs)
    normed_one = (inputs * scale_one * gain_one.astype(jnp.float32)).astype(jnp.bfloat16)
    query_rows = jnp.dot(normed_one, query_full, preferred_element_type=jnp.float32).astype(
        jnp.bfloat16
    )
    key_rows = jnp.dot(normed_one, key_full, preferred_element_type=jnp.float32).astype(
        jnp.bfloat16
    )
    value_rows = jnp.dot(normed_one, value_full, preferred_element_type=jnp.float32).astype(
        jnp.bfloat16
    )
    base = bias_base(table_full)
    context, lse = attend(query_rows, key_rows, value_rows, segments, base)
    hidden_one = inputs + jnp.dot(context, output_full, preferred_element_type=jnp.float32)
    scale_two = rms_scale(hidden_one)
    normed_two = (hidden_one * scale_two * gain_two.astype(jnp.float32)).astype(jnp.bfloat16)
    logits = jnp.dot(normed_two, router_full, preferred_element_type=jnp.float32)
    router_prob = jax.nn.softmax(logits, axis=-1)
    exp_local = w_in.shape[0]
    groups = lax.axis_size("grp")
    experts = exp_local * groups
    capacity = 2 * tok_rows * TOP // experts
    choose = routes[:, :, None] == lax.iota(jnp.int32, experts)[None, None, :]
    picked_prob = jnp.sum(jnp.where(choose, router_prob[:, None, :], 0.0), axis=-1)
    prob_sum = jnp.sum(picked_prob, axis=-1, keepdims=True)
    gates = picked_prob / prob_sum
    counts, prob_totals = lax.psum(
        (jnp.sum(choose.astype(jnp.float32), axis=(0, 1)), jnp.sum(router_prob, axis=0)),
        ("rep", "grp"),
    )
    all_tokens = tok_rows * lax.axis_size("rep") * groups
    fraction = counts / (TOP * all_tokens)
    balance_terms = experts * experts * fraction * (prob_totals / all_tokens)
    loss = aux_weight / experts * jnp.sum(balance_terms)
    flat_routes = routes.reshape(tok_rows * TOP)
    flat_hot = (flat_routes[:, None] == lax.iota(jnp.int32, experts)[None, :]).astype(jnp.int32)
    slots = jnp.sum((jnp.cumsum(flat_hot, axis=0) - flat_hot) * flat_hot, axis=1)
    copies = jnp.repeat(normed_two, TOP, axis=0)
    send_rows = (
        jnp.zeros((experts, capacity, width), jnp.bfloat16).at[flat_routes, slots].set(copies)
    )
    received = lax.all_to_all(
        send_rows.reshape(groups, exp_local, capacity, width),
        "grp",
        split_axis=0,
        concat_axis=0,
        tiled=True,
    )
    pre_act = jnp.einsum("gecd,edf->gecf", received, w_in, preferred_element_type=jnp.float32)
    activated = jax.nn.gelu(pre_act, approximate=True).astype(jnp.bfloat16)
    expert_out = jnp.einsum(
        "gecf,efd->gecd", activated, w_out, preferred_element_type=jnp.float32
    ).astype(jnp.bfloat16)
    returned = lax.all_to_all(expert_out, "grp", split_axis=0, concat_axis=0, tiled=True).reshape(
        experts, capacity, width
    )
    picked_out = returned[flat_routes, slots].astype(jnp.float32).reshape(tok_rows, TOP, width)
    hidden_two = hidden_one + jnp.sum(gates[:, :, None] * picked_out, axis=1)
    output = hidden_two.astype(jnp.bfloat16)
    gain_one, query_full, key_full, value_full, output_full, table_full, gain_two, router_full = (
        dense_full
    )
    grad_out = cotangent.astype(jnp.float32) * (segments != 0).astype(jnp.float32)[:, None]
    grad_gate = jnp.sum(grad_out[:, None, :] * picked_out, axis=-1)
    grad_mix = (
        (gates[:, :, None] * grad_out[:, None, :])
        .astype(jnp.bfloat16)
        .reshape(tok_rows * TOP, width)
    )
    grad_send = (
        jnp.zeros((experts, capacity, width), jnp.bfloat16).at[flat_routes, slots].set(grad_mix)
    )
    grad_received = lax.all_to_all(
        grad_send.reshape(groups, exp_local, capacity, width),
        "grp",
        split_axis=0,
        concat_axis=0,
        tiled=True,
    )
    grad_act = jnp.einsum(
        "gecd,efd->gecf", grad_received, w_out, preferred_element_type=jnp.float32
    )
    down_grad = jnp.einsum(
        "gecf,gecd->efd", activated, grad_received, preferred_element_type=jnp.float32
    )
    unused_out, gelu_back = jax.vjp(partial(jax.nn.gelu, approximate=True), pre_act)
    grad_pre = gelu_back(grad_act)[0].astype(jnp.bfloat16)
    up_grad = jnp.einsum("gecd,gecf->edf", received, grad_pre, preferred_element_type=jnp.float32)
    grad_rows = jnp.einsum(
        "gecf,edf->gecd", grad_pre, w_in, preferred_element_type=jnp.float32
    ).astype(jnp.bfloat16)
    up_share, down_share = (
        lax.psum_scatter(up_grad, "rep", scatter_dimension=1, tiled=True),
        lax.psum_scatter(down_grad, "rep", scatter_dimension=1, tiled=True),
    )
    grad_back = lax.all_to_all(grad_rows, "grp", split_axis=0, concat_axis=0, tiled=True).reshape(
        experts, capacity, width
    )
    grad_norm_two = jnp.sum(
        grad_back[flat_routes, slots].astype(jnp.float32).reshape(tok_rows, TOP, width), axis=1
    )
    grad_picked = grad_gate / prob_sum - jnp.sum(
        grad_gate * picked_prob, axis=-1, keepdims=True
    ) / (prob_sum * prob_sum)
    grad_router_prob = (
        jnp.sum(jnp.where(choose, grad_picked[:, :, None], 0.0), axis=1)
        + aux_weight * experts * fraction / all_tokens
    )
    grad_logits = (
        router_prob
        * (grad_router_prob - jnp.sum(router_prob * grad_router_prob, axis=-1, keepdims=True))
    ).astype(jnp.bfloat16)
    router_grad = outer_sum(normed_two, grad_logits)
    grad_norm_two = grad_norm_two + back_proj(grad_logits, router_full)
    gain_two_grad = jnp.sum(grad_norm_two * (hidden_one * scale_two), axis=0)
    scaled_two = grad_norm_two * gain_two.astype(jnp.float32)
    grad_hidden_one = (
        grad_out
        + scale_two * scaled_two
        - hidden_one * scale_two**3 * jnp.mean(scaled_two * hidden_one, axis=-1, keepdims=True)
    )
    grad_attn = grad_hidden_one.astype(jnp.bfloat16)
    output_grad = outer_sum(context, grad_attn)
    grad_context = back_proj(grad_attn, output_full).astype(jnp.bfloat16)
    grad_query_rows, grad_key_rows, grad_value_rows, near_grad, far_grad = attend_back(
        query_rows, key_rows, value_rows, segments, base, context, grad_context, lse
    )
    query_grad = outer_sum(normed_one, grad_query_rows)
    key_grad = outer_sum(normed_one, grad_key_rows)
    value_grad = outer_sum(normed_one, grad_value_rows)
    grad_norm_one = (
        back_proj(grad_query_rows, query_full)
        + back_proj(grad_key_rows, key_full)
        + back_proj(grad_value_rows, value_full)
    )
    gain_one_grad = jnp.sum(grad_norm_one * (inputs * scale_one), axis=0)
    scaled_one = grad_norm_one * gain_one.astype(jnp.float32)
    grad_input = (
        grad_hidden_one
        + scale_one * scaled_one
        - inputs * scale_one**3 * jnp.mean(scaled_one * inputs, axis=-1, keepdims=True)
    )
    table_grad = table_back(near_grad, far_grad, table_full.shape[0])
    shares = (
        lax.psum_scatter(gain_one_grad, "grp", scatter_dimension=0, tiled=True),
        lax.psum_scatter(query_grad, "grp", scatter_dimension=0, tiled=True),
        lax.psum_scatter(key_grad, "grp", scatter_dimension=0, tiled=True),
        lax.psum_scatter(value_grad, "grp", scatter_dimension=0, tiled=True),
        lax.psum_scatter(output_grad, "grp", scatter_dimension=0, tiled=True),
        lax.psum_scatter(table_grad, "grp", scatter_dimension=0, tiled=True),
        lax.psum_scatter(gain_two_grad, "grp", scatter_dimension=0, tiled=True),
        lax.psum_scatter(router_grad, "grp", scatter_dimension=0, tiled=True),
    )
    summed = lax.psum(
        (shares[0], shares[1], shares[2], shares[3], shares[4], shares[5], shares[6], shares[7]),
        "rep",
    )
    return (
        output,
        loss,
        balance_terms,
        grad_input,
        summed[0],
        summed[1],
        summed[2],
        summed[3],
        summed[4],
        summed[5],
        summed[6],
        summed[7],
        up_share,
        down_share,
    )


def solution(mesh):
    return jax.shard_map(
        shards,
        mesh=mesh,
        in_specs=(
            P(("rep", "grp"), None),
            P(("rep", "grp")),
            P(("rep", "grp"), None),
            P("grp"),
            P("grp", None),
            P("grp", None),
            P("grp", None),
            P("grp", None),
            P("grp", None),
            P("grp"),
            P("grp", None),
            P("grp", None, None),
            P("grp", None, None),
            P(("rep", "grp"), None),
        ),
        out_specs=(
            P(("rep", "grp"), None),
            P(),
            P(),
            P(("rep", "grp"), None),
            P("grp"),
            P("grp", None),
            P("grp", None),
            P("grp", None),
            P("grp", None),
            P("grp", None),
            P("grp"),
            P("grp", None),
            P("grp", "rep", None),
            P("grp", "rep", None),
        ),
        check_vma=False,
    )
```

```python
from functools import partial

import jax
import jax.numpy as jnp
from jax import lax
from jax.experimental import pallas as pl
from jax.experimental.pallas import tpu as pltpu
from jax.sharding import PartitionSpec as P

TOP = 2
QB = 128
PAIR = 128
NEAR = 2 * QB
SPAN = 3 * QB
OUT_OF_DOC = -1e30
FAR_MARKS = (18, 20, 23, 26, 30, 34, 39, 45, 51, 58, 66, 76, 86, 98, 112)
norm_eps = 1e-06
aux_weight = 0.01
f32, bf16 = jnp.float32, jnp.bfloat16


def rms_scale(values):
    return lax.rsqrt(jnp.mean(values * values, axis=-1, keepdims=True) + norm_eps)


def bucket_of(distance):
    far_part = jnp.zeros_like(distance)
    for far_mark in FAR_MARKS:
        far_part = far_part + (distance >= far_mark).astype(jnp.int32)
    return jnp.minimum(distance, 16) + far_part


def band_hot(buckets):
    lane = lax.broadcasted_iota(jnp.int32, (8, SPAN), 1)
    row = lax.broadcasted_iota(jnp.int32, (8, SPAN), 0)
    turn = (lane - row + SPAN) % SPAN
    diff = jnp.where(turn < QB, turn, turn - SPAN) + QB
    bucket = bucket_of(jnp.maximum(diff, 0)).reshape(1, 8 * SPAN)
    return bucket == lax.iota(jnp.int32, buckets)[:, None]


def split_pair(rows, low_lanes):
    zero = jnp.zeros_like(rows)
    return jnp.concatenate(
        [jnp.where(low_lanes, rows, zero), jnp.where(low_lanes, zero, rows)], axis=0
    )


def fill_mask(seg_col, seg_row, mask):
    seq = mask.shape[0]
    for i in range(seq // QB):
        length = (i + 1) * QB
        sk = seg_col[0:length, :]
        sq = seg_row[:, i * QB:(i + 1) * QB]
        kp = lax.broadcasted_iota(jnp.int32, (length, QB), 0)
        qp = lax.broadcasted_iota(jnp.int32, (length, QB), 1) + i * QB
        ok = (sk == sq) & (kp <= qp) & ((sq != 0) | (kp == qp))
        mask[0:length, i * QB:(i + 1) * QB] = jnp.where(ok, 0.0, OUT_OF_DOC).astype(f32)


def fill_near(base, near):
    for head in range(2):
        rows = base[head]
        for a in range(NEAR // 8):
            turned = rows if a == 0 else pltpu.roll(rows, 8 * a, 1)
            near[8 * a:8 * a + 8, head * QB:(head + 1) * QB] = turned[:, 0:QB]


def scores_chunk(k, lo, hi, qcat, mask, near, i):
    s = lax.dot_general(k[lo:hi, :], qcat, (((1,), (1,)), ((), ())), preferred_element_type=f32)
    m = mask[lo:hi, i * QB:(i + 1) * QB]
    s = s + jnp.concatenate([m, m], axis=1)
    start = (i - 1) * QB
    if lo >= start:
        s = s + near[lo - start:hi - start, :]
    return s


def fwd_kernel(base, seg_col, seg_row, q, k, v, ctx, lse, mask, near, scores, probs, v_t):
    seq = q.shape[0]

    @pl.when(pl.program_id(0) == 0)
    def _():
        fill_mask(seg_col, seg_row, mask)

    fill_near(base, near)
    v_t[...] = v[...].T
    low_lanes = lax.broadcasted_iota(jnp.int32, (QB, PAIR), 1) < PAIR // 2
    scale = (PAIR // 2) ** -0.5
    for i in range(seq // QB):
        qs = slice(i * QB, (i + 1) * QB)
        qcat = split_pair(q[qs, :] * jnp.asarray(scale, bf16), low_lanes)
        top = None
        for c in range(i + 1):
            s = scores_chunk(k, c * QB, (c + 1) * QB, qcat, mask, near, i)
            scores[c * QB:(c + 1) * QB, :] = s
            here = jnp.max(s.reshape(QB // 8, 8, NEAR), axis=0)
            top = here if top is None else jnp.maximum(top, here)
        top = jnp.max(top, axis=0, keepdims=True)
        total = jnp.zeros((8, NEAR), f32)
        for c in range(i + 1):
            p = jnp.exp(scores[c * QB:(c + 1) * QB, :] - top)
            total = total + jnp.sum(p.reshape(QB // 8, 8, NEAR), axis=0)
            probs[c * QB:(c + 1) * QB, :] = p.astype(bf16)
        total = jnp.sum(total, axis=0, keepdims=True)
        length = (i + 1) * QB
        out = jnp.dot(v_t[:, 0:length], probs[0:length, :], preferred_element_type=f32) / total
        half = PAIR // 2
        both = jnp.concatenate([out[0:half, 0:QB], out[half:PAIR, QB:NEAR]], axis=0)
        ctx[qs, :] = both.T.astype(bf16)
        lse[0, i:i + 1, :] = top + jnp.log(total)


def attend(q, k, v, seg, base):
    seq, width = q.shape
    pairs = width // PAIR
    col = pl.BlockSpec((seq, PAIR), lambda h: (0, h))
    whole = lambda *shape: pl.BlockSpec(shape, lambda h: (0,) * len(shape))
    return pl.pallas_call(
        fwd_kernel,
        grid=(pairs,),
        in_specs=[pl.BlockSpec((2, 8, SPAN), lambda h: (h, 0, 0)), whole(seq, 1), whole(1, seq), col, col, col],
        out_specs=[col, pl.BlockSpec((1, seq // QB, NEAR), lambda h: (h, 0, 0))],
        out_shape=[
            jax.ShapeDtypeStruct((seq, width), bf16),
            jax.ShapeDtypeStruct((pairs, seq // QB, NEAR), f32),
        ],
        scratch_shapes=[
            pltpu.VMEM((seq, seq), f32),
            pltpu.VMEM((NEAR, NEAR), f32),
            pltpu.VMEM((seq, NEAR), f32),
            pltpu.VMEM((seq, NEAR), bf16),
            pltpu.VMEM((PAIR, seq), bf16),
        ],
        compiler_params=pltpu.CompilerParams(vmem_limit_bytes=32 * 1024 * 1024),
        cost_estimate=pl.CostEstimate(flops=seq * seq * width * 4, bytes_accessed=8 * seq * width, transcendentals=6 * seq * seq),
        name="attend",
    )(base, seg.reshape(seq, 1), seg.reshape(1, seq), q, k, v)


def bwd_kernel(base, seg_col, seg_row, q, k, v, ctx, dctx, lse, dq, dk, dv, dnear, dfar,
               mask, near, ds_all, p_all, k_t, dk_sum, dv_sum, dnear_sum, dfar_sum):
    seq = q.shape[0]

    @pl.when(pl.program_id(0) == 0)
    def _():
        fill_mask(seg_col, seg_row, mask)

    fill_near(base, near)
    k_t[...] = k[...].T
    low_lanes = lax.broadcasted_iota(jnp.int32, (QB, PAIR), 1) < PAIR // 2
    half = PAIR // 2
    scale = half ** -0.5
    dnear_sum[...] = jnp.zeros_like(dnear_sum)
    dfar_sum[...] = jnp.zeros_like(dfar_sum)
    for i in reversed(range(seq // QB)):
        qs = slice(i * QB, (i + 1) * QB)
        length = (i + 1) * QB
        qcat = split_pair(q[qs, :] * jnp.asarray(scale, bf16), low_lanes)
        dcat = split_pair(dctx[qs, :], low_lanes)
        dots = (ctx[qs, :].astype(f32) * dctx[qs, :].astype(f32)).T
        centre = jnp.concatenate(
            [jnp.sum(dots[0:half], axis=0, keepdims=True), jnp.sum(dots[half:], axis=0, keepdims=True)], axis=1
        )
        norm = lse[0, i:i + 1, :]
        for c in range(i + 1):
            lo, hi = c * QB, (c + 1) * QB
            s = scores_chunk(k, lo, hi, qcat, mask, near, i)
            p = jnp.exp(s - norm)
            p_all[lo:hi, :] = p.astype(bf16)
            dp = lax.dot_general(v[lo:hi, :], dcat, (((1,), (1,)), ((), ())), preferred_element_type=f32)
            ds = p * (dp - centre)
            ds_all[lo:hi, :] = ds.astype(bf16)
            start = (i - 1) * QB
            if lo >= start:
                dnear_sum[lo - start:hi - start, :] += ds
            else:
                dfar_sum[...] += jnp.sum(ds.reshape(QB // 8, 8, NEAR), axis=0)
        out = jnp.dot(k_t[:, 0:length], ds_all[0:length, :], preferred_element_type=f32)
        both = jnp.concatenate([out[0:half, 0:QB], out[half:PAIR, QB:NEAR]], axis=0)
        dq[qs, :] = (both.T * scale).astype(bf16)
        dk_part = jnp.dot(ds_all[0:length, :], qcat, preferred_element_type=f32)
        dv_part = jnp.dot(p_all[0:length, :], dcat, preferred_element_type=f32)
        if i == seq // QB - 1:
            dk_sum[0:length, :] = dk_part
            dv_sum[0:length, :] = dv_part
        else:
            dk_sum[0:length, :] += dk_part
            dv_sum[0:length, :] += dv_part
    dk[...] = dk_sum[...].astype(bf16)
    dv[...] = dv_sum[...].astype(bf16)
    for head in range(2):
        total = jnp.zeros((8, SPAN), f32)
        for a in range(NEAR // 8):
            rows = dnear_sum[8 * a:8 * a + 8, head * QB:(head + 1) * QB]
            rows = jnp.concatenate([rows, jnp.zeros((8, SPAN - QB), f32)], axis=1)
            total = total + (rows if a == 0 else pltpu.roll(rows, SPAN - 8 * a, 1))
        dnear[head] = total
    dfar[0] = dfar_sum[...]


def attend_back(q, k, v, seg, base, ctx, dctx, lse):
    seq, width = q.shape
    pairs = width // PAIR
    col = pl.BlockSpec((seq, PAIR), lambda h: (0, h))
    band = pl.BlockSpec((2, 8, SPAN), lambda h: (h, 0, 0))
    whole = lambda *shape: pl.BlockSpec(shape, lambda h: (0,) * len(shape))
    rows = jax.ShapeDtypeStruct((seq, width), bf16)
    return pl.pallas_call(
        bwd_kernel,
        grid=(pairs,),
        in_specs=[band, whole(seq, 1), whole(1, seq), col, col, col, col, col,
                  pl.BlockSpec((1, seq // QB, NEAR), lambda h: (h, 0, 0))],
        out_specs=[col, col, col, band, pl.BlockSpec((1, 8, NEAR), lambda h: (h, 0, 0))],
        out_shape=[rows, rows, rows, jax.ShapeDtypeStruct((2 * pairs, 8, SPAN), f32),
                   jax.ShapeDtypeStruct((pairs, 8, NEAR), f32)],
        scratch_shapes=[
            pltpu.VMEM((seq, seq), f32),
            pltpu.VMEM((NEAR, NEAR), f32),
            pltpu.VMEM((seq, NEAR), bf16),
            pltpu.VMEM((seq, NEAR), bf16),
            pltpu.VMEM((PAIR, seq), bf16),
            pltpu.VMEM((seq, PAIR), f32),
            pltpu.VMEM((seq, PAIR), f32),
            pltpu.VMEM((NEAR, NEAR), f32),
            pltpu.VMEM((8, NEAR), f32),
        ],
        compiler_params=pltpu.CompilerParams(vmem_limit_bytes=40 * 1024 * 1024),
        cost_estimate=pl.CostEstimate(flops=seq * seq * width * 10, bytes_accessed=16 * seq * width, transcendentals=6 * seq * seq),
        name="attend_back",
    )(base, seg.reshape(seq, 1), seg.reshape(1, seq), q, k, v, ctx, dctx, lse)


def bias_base(table):
    buckets, heads = table.shape
    hot = band_hot(buckets).astype(bf16)
    base = lax.dot_general(table, hot, (((0,), (0,)), ((), ())), preferred_element_type=f32)
    last = table[buckets - 1].astype(f32)
    return base.reshape(heads, 8, SPAN) - last[:, None, None]


def table_back(dnear, dfar, buckets):
    heads = dnear.shape[0]
    hot = band_hot(buckets).astype(f32)
    grad = lax.dot_general(hot, dnear.reshape(heads, 8 * SPAN), (((1,), (1,)), ((), ())),
                           preferred_element_type=f32, precision=lax.Precision.HIGHEST)
    far = jnp.sum(dfar.reshape(heads // 2, 8, 2, QB), axis=(1, 3)).reshape(1, heads)
    last = (lax.iota(jnp.int32, buckets) == buckets - 1)[:, None]
    return grad + jnp.where(last, far, 0.0)


def gelu_and_slope(u):
    root = (2.0 / jnp.pi) ** 0.5
    square = u * u
    bent = jnp.tanh(u * (root + (root * 0.044715) * square))
    rise = 0.5 + 0.5 * bent
    slope = rise + (0.5 * u) * (1.0 - bent * bent) * (root + (root * 3 * 0.044715) * square)
    return u * rise, slope


def expert_kernel(first, n_a, n_b, g_a, g_b, info, router_t, w_in, w_out, *rest):
    (y_a, y_b, r_a, r_b, act_out, dpre_out, x_out, dy_out,
     hot, x_s, g_s, dy_s, gate_s, y_sum, d_sum, y_all, d_all, dgate_c) = rest[-18:]
    e, f = pl.program_id(0), pl.program_id(1)
    rows, width = n_a.shape
    cap = x_s.shape[0] // 2
    expert = first[0] + e
    sources = ((n_a, g_a), (n_b, g_b))

    @pl.when((e == 0) & (f == 0))
    def _():
        dgate_c[...] = jnp.zeros_like(dgate_c)

    @pl.when(f == 0)
    def _():
        for s, (n_ref, g_ref) in enumerate(sources):
            logits = lax.dot_general(router_t[...], n_ref[...], (((1,), (1,)), ((), ())), preferred_element_type=f32)
            ids = lax.broadcasted_iota(jnp.int32, logits.shape, 0)
            power = jnp.exp(logits - jnp.max(logits, axis=0, keepdims=True))
            prob = power / jnp.sum(power, axis=0, keepdims=True)
            chosen = (ids == info[4 * s + 2:4 * s + 3, :]) | (ids == info[4 * s + 3:4 * s + 4, :])
            both = jnp.sum(jnp.where(chosen, prob, 0.0), axis=0, keepdims=True)
            gate_row = jnp.sum(jnp.where(ids == expert, prob, 0.0), axis=0, keepdims=True) / both
            slot_row = jnp.where(e == 0, info[4 * s:4 * s + 1, :], info[4 * s + 1:4 * s + 2, :])
            match = slot_row == lax.broadcasted_iota(jnp.int32, (cap, rows), 0)
            one_hot = jnp.where(match, 1.0, 0.0).astype(bf16)
            part = slice(s * cap, (s + 1) * cap)
            gate_s[part, :] = jnp.sum(jnp.where(match, gate_row, 0.0), axis=1, keepdims=True)
            hot[s, pl.ds(pl.multiple_of(e * cap, cap), cap), :] = one_hot
            x_s[part, :] = jnp.dot(one_hot, n_ref[...], preferred_element_type=f32).astype(bf16)
            g_rows = jnp.dot(one_hot, g_ref[...], preferred_element_type=f32)
            g_s[part, :] = g_rows.astype(bf16)
            dy_s[part, :] = (gate_s[part, :] * g_rows).astype(bf16)
        x_out[0] = x_s[...]
        dy_out[0] = dy_s[...]

    pre = jnp.dot(x_s[...], w_in[0], preferred_element_type=f32)
    act, slope = gelu_and_slope(pre)
    act = act.astype(bf16)
    act_out[0] = act
    dact = lax.dot_general(dy_s[...], w_out[0], (((1,), (1,)), ((), ())), preferred_element_type=f32)
    dpre = (dact * slope).astype(bf16)
    dpre_out[0] = dpre
    y_part = jnp.dot(act, w_out[0], preferred_element_type=f32)
    d_part = lax.dot_general(dpre, w_in[0], (((1,), (1,)), ((), ())), preferred_element_type=f32)

    @pl.when(f == 0)
    def _():
        y_sum[...] = y_part
        d_sum[...] = d_part

    @pl.when(f != 0)
    def _():
        y_sum[...] += y_part
        d_sum[...] += d_part

    @pl.when(f == pl.num_programs(1) - 1)
    def _():
        y_rows = y_sum[...].astype(bf16).astype(f32)
        dgate = jnp.sum(y_rows * g_s[...].astype(f32), axis=1, keepdims=True)
        y_rows = (gate_s[...] * y_rows).astype(bf16)
        d_rows = d_sum[...].astype(bf16)
        for s in range(2):
            part = slice(s * cap, (s + 1) * cap)
            here = pl.ds(pl.multiple_of(e * cap, cap), cap)
            y_all[s, here, :] = y_rows[part]
            d_all[s, here, :] = d_rows[part]
            slot_row = jnp.where(e == 0, info[4 * s:4 * s + 1, :], info[4 * s + 1:4 * s + 2, :])
            match = slot_row == lax.broadcasted_iota(jnp.int32, (cap, rows), 0)
            row = jnp.sum(jnp.where(match, dgate[part], 0.0), axis=0, keepdims=True)
            for c in range(TOP):
                routed = info[4 * s + 2 + c:4 * s + 3 + c, :] == expert
                dgate_c[TOP * s + c:TOP * s + c + 1, :] += jnp.where(routed, row, 0.0)

    @pl.when((e == pl.num_programs(0) - 1) & (f == pl.num_programs(1) - 1))
    def _():
        turn = (((0,), (0,)), ((), ()))
        for s, (y_ref, r_ref) in enumerate(((y_a, r_a), (y_b, r_b))):
            y_ref[...] = lax.dot_general(hot[s], y_all[s], turn, preferred_element_type=f32).astype(bf16)
            r_ref[0:rows, :] = lax.dot_general(hot[s], d_all[s], turn, preferred_element_type=f32).astype(bf16)
            value = dgate_c[TOP * s:TOP * s + TOP, :]
            high = value.astype(bf16)
            value = value - high.astype(f32)
            middle = value.astype(bf16)
            low = (value - middle.astype(f32)).astype(bf16)
            pieces = jnp.concatenate([high.astype(f32), middle.astype(f32), low.astype(f32), jnp.zeros((2, rows), f32)], axis=0)
            over = jnp.concatenate([pieces[:, width:], jnp.zeros((8, 2 * width - rows), f32)], axis=1)
            r_ref[rows:rows + 16, :] = jnp.concatenate([pieces[:, 0:width], over], axis=0).astype(bf16)


def unpack_dgate(tail, rows):
    tail = tail.astype(f32)
    pieces = jnp.concatenate([tail[0:8], tail[8:16]], axis=1)[:, 0:rows]
    return pieces[0:2] + pieces[2:4] + pieces[4:6]


def expert_block(k, blocks, first, n_a, n_b, g_a, g_b, info, router_t, w_in, w_out, cap, kept):
    rows, width = n_a.shape
    local, _, hidden = w_in.shape
    part = 768 if hidden % 768 == 0 else hidden
    once = pl.Buffered(1)
    whole = lambda *shape: pl.BlockSpec(shape, lambda e, f: (0,) * len(shape), pipeline_mode=once)
    wide = pl.BlockSpec((1, 2 * cap, part), lambda e, f: (e, k, f))
    slim = pl.BlockSpec((1, 2 * cap, width), lambda e, f: (e, k, 0))
    slots = blocks * 2 * cap
    shapes = [
        jax.ShapeDtypeStruct((rows, width), bf16), jax.ShapeDtypeStruct((rows, width), bf16),
        jax.ShapeDtypeStruct((rows + 16, width), bf16), jax.ShapeDtypeStruct((rows + 16, width), bf16),
        jax.ShapeDtypeStruct((local, slots, hidden), bf16), jax.ShapeDtypeStruct((local, slots, hidden), bf16),
        jax.ShapeDtypeStruct((local, slots, width), bf16), jax.ShapeDtypeStruct((local, slots, width), bf16),
    ]
    in_specs = [
        pl.BlockSpec(memory_space=pltpu.SMEM), whole(rows, width), whole(rows, width), whole(rows, width), whole(rows, width),
        whole(8, rows), whole(*router_t.shape),
        pl.BlockSpec((1, width, part), lambda e, f: (e, 0, f)), pl.BlockSpec((1, part, width), lambda e, f: (e, f, 0)),
    ]
    args = [first, n_a, n_b, g_a, g_b, info, router_t, w_in, w_out]
    alias = {}
    if kept is not None:
        alias = {len(args) + i: 4 + i for i in range(4)}
        in_specs += [pl.BlockSpec(memory_space=pl.ANY)] * 4
        args += list(kept)
    out = pl.pallas_call(
        expert_kernel,
        grid=(local, hidden // part),
        in_specs=in_specs,
        out_specs=[whole(rows, width), whole(rows, width), whole(rows + 16, width), whole(rows + 16, width), wide, wide, slim, slim],
        out_shape=shapes,
        scratch_shapes=[
            pltpu.VMEM((2, local * cap, rows), bf16),
            pltpu.VMEM((2 * cap, width), bf16), pltpu.VMEM((2 * cap, width), bf16), pltpu.VMEM((2 * cap, width), bf16),
            pltpu.VMEM((2 * cap, 1), f32),
            pltpu.VMEM((2 * cap, width), f32), pltpu.VMEM((2 * cap, width), f32),
            pltpu.VMEM((2, local * cap, width), bf16), pltpu.VMEM((2, local * cap, width), bf16),
            pltpu.VMEM((8, rows), f32),
        ],
        input_output_aliases=alias,
        compiler_params=pltpu.CompilerParams(vmem_limit_bytes=48 * 1024 * 1024),
        cost_estimate=pl.CostEstimate(flops=2 * local * cap * (8 * width * hidden + 8 * width * rows), bytes_accessed=60 * 1024 * 1024, transcendentals=2 * local * cap * hidden),
        name="expert_block",
    )(*args)
    return out[:4], out[4:]


def chip_ring(chips):
    return [0] + list(range(1, chips, 2)) + [z for z in range(chips - 1, 0, -1) if z % 2 == 0]


class Group:
    def __init__(self):
        self.size = lax.axis_size("grp")
        self.chips = self.size // 2
        self.order = chip_ring(self.chips)
        me = lax.axis_index("grp")
        self.me, self.chip, self.core = me, me // 2, me % 2

    def onward(self, x):
        pairs = []
        for i, z in enumerate(self.order):
            after = self.order[(i + 1) % self.chips]
            pairs += [(2 * z, 2 * after), (2 * z + 1, 2 * after + 1)]
        return lax.ppermute(x, "grp", pairs)

    def swap(self, x):
        return lax.ppermute(x, "grp", [(i, i ^ 1) for i in range(self.size)])

    def source_chip(self, k):
        table = [0] * self.chips
        for i, z in enumerate(self.order):
            table[z] = self.order[(i - k) % self.chips]
        return jnp.asarray(table, jnp.int32)[self.chip]


def pick_constant(table, index):
    value = jnp.int32(table[0])
    for i in range(1, len(table)):
        value = jnp.where(index == i, jnp.int32(table[i]), value)
    return value


def gather_kernel(chips, reps, *refs):
    count = 5
    shard, tally = refs[:count], refs[count]
    full, tally_all = refs[count + 1:2 * count + 1], refs[2 * count + 1]
    own_sem, ring_send, ring_recv, core_send, core_recv, rep_send, rep_recv, tally_in, tally_sum, tally_vmem = refs[2 * count + 2:]
    order = chip_ring(chips)
    rep, me = lax.axis_index("rep"), lax.axis_index("grp")
    chip, core = me // 2, me % 2
    after, before = [0] * chips, [0] * chips
    for i, z in enumerate(order):
        after[z], before[z] = order[(i + 1) % chips], order[(i - 1) % chips]
    after = 2 * pick_constant(after, chip) + core
    before = 2 * pick_constant(before, chip) + core
    sibling = 2 * chip + 1 - core
    mesh_id = pl.DeviceIdType.MESH

    barrier = pltpu.get_barrier_semaphore()
    peers = [(rep, after), (rep, before), (rep, sibling)]
    peers += [(lax.rem(rep + k, reps), me) for k in range(1, reps)]
    for peer in peers:
        pl.semaphore_signal(barrier, inc=1, device_id=peer, device_id_type=mesh_id)
    pl.semaphore_wait(barrier, len(peers))

    def place(a, owner):
        if a == count:
            return tally_all.at[owner]
        rows = shard[a].shape[0]
        return full[a].at[pl.ds(pl.multiple_of(owner * rows, rows), rows), :]

    def remote(src, dst, send, recv, target):
        return pltpu.make_async_remote_copy(
            src_ref=src, dst_ref=dst, send_sem=send, recv_sem=recv, device_id=target, device_id_type=mesh_id
        )

    tallies = [
        remote(tally, tally_in.at[k - 1], rep_send.at[k - 1], rep_recv.at[k - 1], (lax.rem(rep + k, reps), me))
        for k in range(1, reps)
    ]
    for copy in tallies:
        copy.start()
    own_tally = pltpu.make_async_copy(tally, tally_vmem, own_sem.at[count])
    own_tally.start()

    pending = []
    moved = [None] * (count + 1)
    own = []
    for a in range(count):
        keep = pltpu.make_async_copy(shard[a], place(a, me), own_sem.at[a])
        keep.start()
        own.append(keep)
        ring = remote(shard[a], place(a, me), ring_send.at[0, a], ring_recv.at[0, a], (rep, after))
        ring.start()
        across = remote(shard[a], place(a, me), core_send.at[0, a], core_recv.at[0, a], (rep, sibling))
        across.start()
        moved[a] = ring
        pending += [ring, across]

    own_tally.wait()
    total = tally_vmem[...]
    for k, copy in enumerate(tallies):
        copy.wait_recv()
        total = total + tally_in[k]
    tally_sum[...] = total
    keep = pltpu.make_async_copy(tally_sum, place(count, me), own_sem.at[count + 1])
    keep.start()
    own.append(keep)
    ring = remote(tally_sum, place(count, me), ring_send.at[0, count], ring_recv.at[0, count], (rep, after))
    ring.start()
    across = remote(tally_sum, place(count, me), core_send.at[0, count], core_recv.at[0, count], (rep, sibling))
    across.start()
    moved[count] = ring
    pending += [ring, across]

    for k in range(1, chips):
        source = [0] * chips
        for i, z in enumerate(order):
            source[z] = order[(i - k) % chips]
        owner = 2 * pick_constant(source, chip) + core
        for a in range(count + 1):
            moved[a].wait_recv()
            block = place(a, owner)
            if k < chips - 1:
                ring = remote(block, block, ring_send.at[k, a], ring_recv.at[k, a], (rep, after))
                ring.start()
                moved[a] = ring
                pending.append(ring)
            across = remote(block, block, core_send.at[k, a], core_recv.at[k, a], (rep, sibling))
            across.start()
            pending.append(across)
    for copy in pending:
        copy.wait_send()
    for copy in tallies:
        copy.wait_send()
    for keep in own:
        keep.wait()
    for k in range(chips):
        source = [0] * chips
        for i, z in enumerate(order):
            source[z] = order[(i - k) % chips]
        owner = 2 * pick_constant(source, chip) + 1 - core
        for a in range(count + 1):
            block = place(a, owner)
            remote(block, block, core_send.at[k, a], core_recv.at[k, a], (rep, sibling)).wait_recv()


def gather_group(arrays, tally):
    size, reps = lax.axis_size("grp"), lax.axis_size("rep")
    chips = size // 2
    count = len(arrays)
    hbm = pl.BlockSpec(memory_space=pl.ANY)
    dma = pltpu.SemaphoreType.DMA
    return pl.pallas_call(
        partial(gather_kernel, chips, reps),
        in_specs=[hbm] * (count + 1),
        out_specs=[hbm] * (count + 1),
        out_shape=[jax.ShapeDtypeStruct((size * x.shape[0], x.shape[1]), x.dtype) for x in arrays]
        + [jax.ShapeDtypeStruct((size,) + tally.shape, f32)],
        scratch_shapes=[
            dma((count + 2,)), dma((chips, count + 1)), dma((chips, count + 1)), dma((chips, count + 1)), dma((chips, count + 1)),
            dma((reps,)), dma((reps,)),
            pltpu.VMEM((reps - 1,) + tally.shape, f32), pltpu.VMEM(tally.shape, f32), pltpu.VMEM(tally.shape, f32),
        ],
        compiler_params=pltpu.CompilerParams(collective_id=0, has_side_effects=True),
        cost_estimate=pl.CostEstimate(flops=0, bytes_accessed=16 * 1024 * 1024, transcendentals=0),
        name="gather_group",
    )(*arrays, tally)


def pack_small(gain_attn, gain_ffn, router, rel_bias, routes):
    def lanes(x):
        return jnp.pad(x, ((0, 0), (0, 128 - x.shape[1])))

    rows = jnp.concatenate([
        lanes(gain_attn[None]), lanes(gain_ffn[None]), lanes(rel_bias), lanes(router.T),
        routes.T.astype(bf16).reshape(-1, 128),
    ], axis=0)
    return jnp.pad(rows, ((0, -rows.shape[0] % 16), (0, 0)))


def unpack_small(packed, size, shard, bias_rows, heads, experts, tokens):
    blocks = packed.reshape(size, -1, 128)
    gain_one = blocks[:, 0, 0:shard].reshape(-1)
    gain_two = blocks[:, 1, 0:shard].reshape(-1)
    at = 2 + bias_rows
    table = blocks[:, 2:at, 0:heads].reshape(-1, heads)
    router_t = jnp.transpose(blocks[:, at:at + experts, 0:shard], (1, 0, 2)).reshape(experts, -1)
    at += experts
    routes = blocks[:, at:at + TOP * tokens // 128].reshape(size, TOP, tokens).astype(jnp.int32)
    return gain_one, gain_two, table, router_t, routes


def outer_sum(left_rows, right_rows):
    return lax.dot_general(
        left_rows, right_rows, (((0,), (0,)), ((), ())), preferred_element_type=jnp.float32
    )


def back_proj(grad_rows, weight):
    return lax.dot_general(
        grad_rows, weight, (((1,), (1,)), ((), ())), preferred_element_type=jnp.float32
    )


def rep_moved(whole):
    count = lax.axis_size("rep")
    me = lax.axis_index("rep")
    rows = whole.shape[1] // count
    moved = []
    for k in range(1, count):
        piece = lax.dynamic_slice_in_dim(whole, (me ^ k) * rows, rows, 1)
        moved.append(lax.ppermute(piece, "rep", [(i, i ^ k) for i in range(count)]))
    return moved


def rep_sum(whole, moved):
    rows = moved[0].shape[1]
    total = lax.dynamic_slice_in_dim(whole, lax.axis_index("rep") * rows, rows, 1).astype(f32)
    for piece in moved:
        total = total + piece.astype(f32)
    return total


def local_slots(routes_all, first, local):
    ids = first + lax.iota(jnp.int32, local)
    hot = jnp.any(routes_all[:, None, :, :] == ids[None, :, None, None], axis=2).astype(jnp.int32)
    return jnp.where(hot != 0, jnp.cumsum(hot, axis=2) - hot, -1)


def shards(
    tokens,
    segments,
    routes,
    gain_attn,
    w_query,
    w_key,
    w_value,
    w_output,
    rel_bias,
    gain_ffn,
    router,
    w_in,
    w_out,
    cotangent,
):
    group = Group()
    tok_rows, width = tokens.shape
    exp_local = w_in.shape[0]
    groups = group.size
    experts = exp_local * groups
    capacity = 2 * tok_rows * TOP // experts
    choose = routes[:, :, None] == lax.iota(jnp.int32, experts)[None, None, :]
    tally = jnp.pad(jnp.sum(choose.astype(f32), axis=(0, 1))[None], ((0, 7), (0, 128 - experts)))
    small = pack_small(gain_attn, gain_ffn, router, rel_bias, routes)
    query_full, key_full, value_full, output_full, small_all, tally_all = gather_group(
        (w_query, w_key, w_value, w_output, small), tally
    )
    gain_one, gain_two, table_full, router_t, routes_all = unpack_small(
        small_all, groups, gain_attn.shape[0], rel_bias.shape[0], rel_bias.shape[1], experts, tok_rows
    )
    router_full = router_t.T
    counts = jnp.sum(tally_all[:, 0, 0:experts], axis=0)
    first = (group.me * exp_local).astype(jnp.int32)
    cotangent, small_all = lax.optimization_barrier((cotangent, small_all))
    slots_all = local_slots(routes_all, first, exp_local)

    kept_grad = jnp.where((segments != 0)[:, None], cotangent, jnp.zeros_like(cotangent))
    grad_own = [kept_grad]
    for k in range(1, group.chips):
        grad_own.append(group.onward(grad_own[-1]))
    grad_sib = [group.swap(block) for block in grad_own]

    inputs = tokens.astype(f32)
    scale_one = rms_scale(inputs)
    normed_one = (inputs * scale_one * gain_one.astype(f32)).astype(bf16)
    query_rows = jnp.dot(normed_one, query_full, preferred_element_type=f32).astype(bf16)
    key_rows = jnp.dot(normed_one, key_full, preferred_element_type=f32).astype(bf16)
    value_rows = jnp.dot(normed_one, value_full, preferred_element_type=f32).astype(bf16)
    base = bias_base(table_full)
    context, lse = attend(query_rows, key_rows, value_rows, segments, base)
    hidden_one = inputs + jnp.dot(context, output_full, preferred_element_type=f32)
    scale_two = rms_scale(hidden_one)
    normed_two = (hidden_one * scale_two * gain_two.astype(f32)).astype(bf16)

    norm_own = [normed_two]
    for k in range(1, group.chips):
        norm_own.append(group.onward(norm_own[-1]))
    norm_sib = [group.swap(block) for block in norm_own]

    kept = None
    results = []
    for k in range(group.chips):
        chip = group.source_chip(k)
        info = jnp.concatenate(
            [
                lax.dynamic_index_in_dim(rows, 2 * chip + core, 0, keepdims=False)
                for core in (group.core, 1 - group.core)
                for rows in (slots_all, routes_all)
            ],
            axis=0,
        )
        outs, kept = expert_block(
            k, group.chips, first.reshape(1), norm_own[k], norm_sib[k], grad_own[k], grad_sib[k],
            info, router_t, w_in, w_out, capacity, kept,
        )
        results.append(outs)

    def reduce_blocks(own, sibling):
        moving = None
        for k in list(range(1, group.chips)) + [0]:
            total = own[k].astype(f32) + group.swap(sibling[k]).astype(f32)
            if moving is not None:
                total = total + moving.astype(f32)
            if k != 0:
                moving = group.onward(total.astype(bf16))
        return total

    act_all, dpre_all, x_all, dy_all = kept
    up_grad = jnp.einsum("ekd,ekf->edf", x_all, dpre_all, preferred_element_type=f32).astype(bf16)
    down_grad = jnp.einsum("ekf,ekd->efd", act_all, dy_all, preferred_element_type=f32).astype(bf16)
    up_moved, down_moved = rep_moved(up_grad), rep_moved(down_grad)

    back = reduce_blocks([r[2] for r in results], [r[3] for r in results])
    y_own, y_sib = [r[0] for r in results], [r[1] for r in results]
    back, up_grad, down_grad, y_own, y_sib = lax.optimization_barrier((back, up_grad, down_grad, y_own, y_sib))
    mixed = reduce_blocks(y_own, y_sib)
    up_share, down_share = rep_sum(up_grad, up_moved), rep_sum(down_grad, down_moved)

    logits = jnp.dot(normed_two, router_full, preferred_element_type=f32)
    router_prob = jax.nn.softmax(logits, axis=-1)
    picked_prob = jnp.sum(jnp.where(choose, router_prob[:, None, :], 0.0), axis=-1)
    prob_sum = jnp.sum(picked_prob, axis=-1, keepdims=True)
    all_tokens = tok_rows * lax.axis_size("rep") * groups
    fraction = counts / (TOP * all_tokens)

    output = (hidden_one + mixed[0:tok_rows]).astype(bf16)
    grad_out = kept_grad.astype(f32)
    grad_gate = unpack_dgate(back[tok_rows:], tok_rows).T
    grad_norm_two = back[0:tok_rows]
    grad_picked = grad_gate / prob_sum - jnp.sum(
        grad_gate * picked_prob, axis=-1, keepdims=True
    ) / (prob_sum * prob_sum)
    grad_router_prob = (
        jnp.sum(jnp.where(choose, grad_picked[:, :, None], 0.0), axis=1)
        + aux_weight * experts * fraction / all_tokens
    )
    grad_logits = (
        router_prob
        * (grad_router_prob - jnp.sum(router_prob * grad_router_prob, axis=-1, keepdims=True))
    ).astype(jnp.bfloat16)
    router_grad = outer_sum(normed_two, grad_logits)
    grad_norm_two = grad_norm_two + back_proj(grad_logits, router_full)
    gain_two_grad = jnp.sum(grad_norm_two * (hidden_one * scale_two), axis=0)
    scaled_two = grad_norm_two * gain_two.astype(jnp.float32)
    grad_hidden_one = (
        grad_out
        + scale_two * scaled_two
        - hidden_one * scale_two**3 * jnp.mean(scaled_two * hidden_one, axis=-1, keepdims=True)
    )
    grad_attn = grad_hidden_one.astype(jnp.bfloat16)
    output_grad = outer_sum(context, grad_attn)
    grad_context = back_proj(grad_attn, output_full).astype(jnp.bfloat16)
    grad_query_rows, grad_key_rows, grad_value_rows, near_grad, far_grad = attend_back(
        query_rows, key_rows, value_rows, segments, base, context, grad_context, lse
    )
    query_grad = outer_sum(normed_one, grad_query_rows)
    key_grad = outer_sum(normed_one, grad_key_rows)
    value_grad = outer_sum(normed_one, grad_value_rows)
    grad_norm_one = (
        back_proj(grad_query_rows, query_full)
        + back_proj(grad_key_rows, key_full)
        + back_proj(grad_value_rows, value_full)
    )
    gain_one_grad = jnp.sum(grad_norm_one * (inputs * scale_one), axis=0)
    scaled_one = grad_norm_one * gain_one.astype(jnp.float32)
    grad_input = (
        grad_hidden_one
        + scale_one * scaled_one
        - inputs * scale_one**3 * jnp.mean(scaled_one * inputs, axis=-1, keepdims=True)
    )
    table_grad = table_back(near_grad, far_grad, table_full.shape[0])
    heads = table_grad.shape[1]
    flat = jnp.concatenate([
        gain_one_grad, gain_two_grad, table_grad.reshape(-1), router_grad.T.reshape(-1), jnp.sum(router_prob, axis=0)
    ])
    flat = lax.psum(flat, ("rep", "grp"))
    at = 2 * width
    table_sum = flat[at:at + table_grad.size].reshape(-1, heads)
    at += table_grad.size
    router_sum = flat[at:at + router_grad.size].reshape(experts, width).T
    at += router_grad.size
    prob_totals = flat[at:at + experts]
    balance_terms = experts * experts * fraction * (prob_totals / all_tokens)
    loss = aux_weight / experts * jnp.sum(balance_terms)

    def mine(x):
        rows = x.shape[0] // groups
        return lax.dynamic_slice_in_dim(x, group.me * rows, rows, 0)

    dense = [
        lax.psum_scatter(x, "grp", scatter_dimension=0, tiled=True)
        for x in (query_grad, key_grad, value_grad, output_grad)
    ]
    dense = lax.psum(tuple(dense), "rep")
    return (
        output,
        loss,
        balance_terms,
        grad_input,
        mine(flat[0:width]),
        dense[0],
        dense[1],
        dense[2],
        dense[3],
        mine(table_sum),
        mine(flat[width:2 * width]),
        mine(router_sum),
        up_share,
        down_share,
    )


def solution(mesh):
    return jax.shard_map(
        shards,
        mesh=mesh,
        in_specs=(
            P(("rep", "grp"), None),
            P(("rep", "grp")),
            P(("rep", "grp"), None),
            P("grp"),
            P("grp", None),
            P("grp", None),
            P("grp", None),
            P("grp", None),
            P("grp", None),
            P("grp"),
            P("grp", None),
            P("grp", None, None),
            P("grp", None, None),
            P(("rep", "grp"), None),
        ),
        out_specs=(
            P(("rep", "grp"), None),
            P(),
            P(),
            P(("rep", "grp"), None),
            P("grp"),
            P("grp", None),
            P("grp", None),
            P("grp", None),
            P("grp", None),
            P("grp", None),
            P("grp"),
            P("grp", None),
            P("grp", "rep", None),
            P("grp", "rep", None),
        ),
        check_vma=False,
    )
```

```python
from functools import partial

import jax
import jax.numpy as jnp
from jax import lax
from jax.experimental import pallas as pl
from jax.experimental.pallas import tpu as pltpu
from jax.sharding import PartitionSpec as P

TOP = 2
QB = 128
PAIR = 128
NEAR = 2 * QB
SPAN = 3 * QB
OUT_OF_DOC = -1e30
FAR_MARKS = (18, 20, 23, 26, 30, 34, 39, 45, 51, 58, 66, 76, 86, 98, 112)
norm_eps = 1e-06
aux_weight = 0.01
f32, bf16 = jnp.float32, jnp.bfloat16


def after(x, *earlier):
    return lax.optimization_barrier((x, earlier))[0]


def rms_scale(values):
    return lax.rsqrt(jnp.mean(values * values, axis=-1, keepdims=True) + norm_eps)


def bucket_of(distance):
    far_part = jnp.zeros_like(distance)
    for far_mark in FAR_MARKS:
        far_part = far_part + (distance >= far_mark).astype(jnp.int32)
    return jnp.minimum(distance, 16) + far_part


def band_hot(buckets):
    lane = lax.broadcasted_iota(jnp.int32, (8, SPAN), 1)
    row = lax.broadcasted_iota(jnp.int32, (8, SPAN), 0)
    turn = (lane - row + SPAN) % SPAN
    diff = jnp.where(turn < QB, turn, turn - SPAN) + QB
    bucket = bucket_of(jnp.maximum(diff, 0)).reshape(1, 8 * SPAN)
    return bucket == lax.iota(jnp.int32, buckets)[:, None]


def split_pair(rows, low_lanes):
    zero = jnp.zeros_like(rows)
    return jnp.concatenate(
        [jnp.where(low_lanes, rows, zero), jnp.where(low_lanes, zero, rows)], axis=0
    )


def fill_mask(seg_col, seg_row, mask):
    seq = mask.shape[0]
    for i in range(seq // QB):
        length = (i + 1) * QB
        sk = seg_col[0:length, :]
        sq = seg_row[:, i * QB:(i + 1) * QB]
        kp = lax.broadcasted_iota(jnp.int32, (length, QB), 0)
        qp = lax.broadcasted_iota(jnp.int32, (length, QB), 1) + i * QB
        ok = (sk == sq) & (kp <= qp) & ((sq != 0) | (kp == qp))
        mask[0:length, i * QB:(i + 1) * QB] = jnp.where(ok, 0.0, OUT_OF_DOC).astype(f32)


def fill_near(base, near):
    for head in range(2):
        rows = base[head]
        for a in range(NEAR // 8):
            turned = rows if a == 0 else pltpu.roll(rows, 8 * a, 1)
            near[8 * a:8 * a + 8, head * QB:(head + 1) * QB] = turned[:, 0:QB]


def scores_chunk(k, lo, hi, qcat, mask, near, i):
    s = lax.dot_general(k[lo:hi, :], qcat, (((1,), (1,)), ((), ())), preferred_element_type=f32)
    m = mask[lo:hi, i * QB:(i + 1) * QB]
    s = s + jnp.concatenate([m, m], axis=1)
    start = (i - 1) * QB
    if lo >= start:
        s = s + near[lo - start:hi - start, :]
    return s


def fwd_kernel(base, seg_col, seg_row, q, k, v, ctx, lse, mask, near, scores, probs, v_t):
    seq = q.shape[0]

    @pl.when(pl.program_id(0) == 0)
    def _():
        fill_mask(seg_col, seg_row, mask)

    fill_near(base, near)
    v_t[...] = v[...].T
    low_lanes = lax.broadcasted_iota(jnp.int32, (QB, PAIR), 1) < PAIR // 2
    scale = (PAIR // 2) ** -0.5
    for i in range(seq // QB):
        qs = slice(i * QB, (i + 1) * QB)
        qcat = split_pair(q[qs, :] * jnp.asarray(scale, bf16), low_lanes)
        top = None
        for c in range(i + 1):
            s = scores_chunk(k, c * QB, (c + 1) * QB, qcat, mask, near, i)
            scores[c * QB:(c + 1) * QB, :] = s
            here = jnp.max(s.reshape(QB // 8, 8, NEAR), axis=0)
            top = here if top is None else jnp.maximum(top, here)
        top = jnp.max(top, axis=0, keepdims=True)
        total = jnp.zeros((8, NEAR), f32)
        for c in range(i + 1):
            p = jnp.exp(scores[c * QB:(c + 1) * QB, :] - top)
            total = total + jnp.sum(p.reshape(QB // 8, 8, NEAR), axis=0)
            probs[c * QB:(c + 1) * QB, :] = p.astype(bf16)
        total = jnp.sum(total, axis=0, keepdims=True)
        length = (i + 1) * QB
        out = jnp.dot(v_t[:, 0:length], probs[0:length, :], preferred_element_type=f32) / total
        half = PAIR // 2
        both = jnp.concatenate([out[0:half, 0:QB], out[half:PAIR, QB:NEAR]], axis=0)
        ctx[qs, :] = both.T.astype(bf16)
        lse[0, i:i + 1, :] = top + jnp.log(total)


def attend(q, k, v, seg, base):
    seq, width = q.shape
    pairs = width // PAIR
    col = pl.BlockSpec((seq, PAIR), lambda h: (0, h))
    whole = lambda *shape: pl.BlockSpec(shape, lambda h: (0,) * len(shape))
    return pl.pallas_call(
        fwd_kernel,
        grid=(pairs,),
        in_specs=[pl.BlockSpec((2, 8, SPAN), lambda h: (h, 0, 0)), whole(seq, 1), whole(1, seq), col, col, col],
        out_specs=[col, pl.BlockSpec((1, seq // QB, NEAR), lambda h: (h, 0, 0))],
        out_shape=[
            jax.ShapeDtypeStruct((seq, width), bf16),
            jax.ShapeDtypeStruct((pairs, seq // QB, NEAR), f32),
        ],
        scratch_shapes=[
            pltpu.VMEM((seq, seq), f32),
            pltpu.VMEM((NEAR, NEAR), f32),
            pltpu.VMEM((seq, NEAR), f32),
            pltpu.VMEM((seq, NEAR), bf16),
            pltpu.VMEM((PAIR, seq), bf16),
        ],
        compiler_params=pltpu.CompilerParams(vmem_limit_bytes=32 * 1024 * 1024),
        cost_estimate=pl.CostEstimate(flops=1, bytes_accessed=1024, transcendentals=0),
        name="attend",
    )(base, seg.reshape(seq, 1), seg.reshape(1, seq), q, k, v)


def bwd_kernel(base, seg_col, seg_row, q, k, v, ctx, dctx, lse, dq, dk, dv, dnear, dfar,
               mask, near, ds_all, p_all, k_t, dk_sum, dv_sum, dnear_sum, dfar_sum):
    seq = q.shape[0]

    @pl.when(pl.program_id(0) == 0)
    def _():
        fill_mask(seg_col, seg_row, mask)

    fill_near(base, near)
    k_t[...] = k[...].T
    low_lanes = lax.broadcasted_iota(jnp.int32, (QB, PAIR), 1) < PAIR // 2
    half = PAIR // 2
    scale = half ** -0.5
    dnear_sum[...] = jnp.zeros_like(dnear_sum)
    dfar_sum[...] = jnp.zeros_like(dfar_sum)
    for i in reversed(range(seq // QB)):
        qs = slice(i * QB, (i + 1) * QB)
        length = (i + 1) * QB
        qcat = split_pair(q[qs, :] * jnp.asarray(scale, bf16), low_lanes)
        dcat = split_pair(dctx[qs, :], low_lanes)
        dots = (ctx[qs, :].astype(f32) * dctx[qs, :].astype(f32)).T
        centre = jnp.concatenate(
            [jnp.sum(dots[0:half], axis=0, keepdims=True), jnp.sum(dots[half:], axis=0, keepdims=True)], axis=1
        )
        norm = lse[0, i:i + 1, :]
        for c in range(i + 1):
            lo, hi = c * QB, (c + 1) * QB
            s = scores_chunk(k, lo, hi, qcat, mask, near, i)
            p = jnp.exp(s - norm)
            p_all[lo:hi, :] = p.astype(bf16)
            dp = lax.dot_general(v[lo:hi, :], dcat, (((1,), (1,)), ((), ())), preferred_element_type=f32)
            ds = p * (dp - centre)
            ds_all[lo:hi, :] = ds.astype(bf16)
            start = (i - 1) * QB
            if lo >= start:
                dnear_sum[lo - start:hi - start, :] += ds
            else:
                dfar_sum[...] += jnp.sum(ds.reshape(QB // 8, 8, NEAR), axis=0)
        out = jnp.dot(k_t[:, 0:length], ds_all[0:length, :], preferred_element_type=f32)
        both = jnp.concatenate([out[0:half, 0:QB], out[half:PAIR, QB:NEAR]], axis=0)
        dq[qs, :] = (both.T * scale).astype(bf16)
        dk_part = jnp.dot(ds_all[0:length, :], qcat, preferred_element_type=f32)
        dv_part = jnp.dot(p_all[0:length, :], dcat, preferred_element_type=f32)
        if i == seq // QB - 1:
            dk_sum[0:length, :] = dk_part
            dv_sum[0:length, :] = dv_part
        else:
            dk_sum[0:length, :] += dk_part
            dv_sum[0:length, :] += dv_part
    dk[...] = dk_sum[...].astype(bf16)
    dv[...] = dv_sum[...].astype(bf16)
    for head in range(2):
        total = jnp.zeros((8, SPAN), f32)
        for a in range(NEAR // 8):
            rows = dnear_sum[8 * a:8 * a + 8, head * QB:(head + 1) * QB]
            rows = jnp.concatenate([rows, jnp.zeros((8, SPAN - QB), f32)], axis=1)
            total = total + (rows if a == 0 else pltpu.roll(rows, SPAN - 8 * a, 1))
        dnear[head] = total
    dfar[0] = dfar_sum[...]


def attend_back(q, k, v, seg, base, ctx, dctx, lse):
    seq, width = q.shape
    pairs = width // PAIR
    col = pl.BlockSpec((seq, PAIR), lambda h: (0, h))
    band = pl.BlockSpec((2, 8, SPAN), lambda h: (h, 0, 0))
    whole = lambda *shape: pl.BlockSpec(shape, lambda h: (0,) * len(shape))
    rows = jax.ShapeDtypeStruct((seq, width), bf16)
    return pl.pallas_call(
        bwd_kernel,
        grid=(pairs,),
        in_specs=[band, whole(seq, 1), whole(1, seq), col, col, col, col, col,
                  pl.BlockSpec((1, seq // QB, NEAR), lambda h: (h, 0, 0))],
        out_specs=[col, col, col, band, pl.BlockSpec((1, 8, NEAR), lambda h: (h, 0, 0))],
        out_shape=[rows, rows, rows, jax.ShapeDtypeStruct((2 * pairs, 8, SPAN), f32),
                   jax.ShapeDtypeStruct((pairs, 8, NEAR), f32)],
        scratch_shapes=[
            pltpu.VMEM((seq, seq), f32),
            pltpu.VMEM((NEAR, NEAR), f32),
            pltpu.VMEM((seq, NEAR), bf16),
            pltpu.VMEM((seq, NEAR), bf16),
            pltpu.VMEM((PAIR, seq), bf16),
            pltpu.VMEM((seq, PAIR), f32),
            pltpu.VMEM((seq, PAIR), f32),
            pltpu.VMEM((NEAR, NEAR), f32),
            pltpu.VMEM((8, NEAR), f32),
        ],
        compiler_params=pltpu.CompilerParams(vmem_limit_bytes=40 * 1024 * 1024),
        cost_estimate=pl.CostEstimate(flops=1, bytes_accessed=1024, transcendentals=0),
        name="attend_back",
    )(base, seg.reshape(seq, 1), seg.reshape(1, seq), q, k, v, ctx, dctx, lse)


def bias_base(table):
    buckets, heads = table.shape
    hot = band_hot(buckets).astype(bf16)
    base = lax.dot_general(table, hot, (((0,), (0,)), ((), ())), preferred_element_type=f32)
    last = table[buckets - 1].astype(f32)
    return base.reshape(heads, 8, SPAN) - last[:, None, None]


def table_back(dnear, dfar, buckets):
    heads = dnear.shape[0]
    hot = band_hot(buckets).astype(f32)
    grad = lax.dot_general(hot, dnear.reshape(heads, 8 * SPAN), (((1,), (1,)), ((), ())),
                           preferred_element_type=f32, precision=lax.Precision.HIGHEST)
    far = jnp.sum(dfar.reshape(heads // 2, 8, 2, QB), axis=(1, 3)).reshape(1, heads)
    last = (lax.iota(jnp.int32, buckets) == buckets - 1)[:, None]
    return grad + jnp.where(last, far, 0.0)


def gelu_and_slope(u):
    root = (2.0 / jnp.pi) ** 0.5
    square = u * u
    bent = jnp.tanh(u * (root + (root * 0.044715) * square))
    rise = 0.5 + 0.5 * bent
    slope = rise + (0.5 * u) * (1.0 - bent * bent) * (root + (root * 3 * 0.044715) * square)
    return u * rise, slope


def expert_kernel(first, n_a, n_b, g_a, g_b, info, router_t, w_in, w_out, *rest):
    (y_a, y_b, r_a, r_b, act_out, dpre_out, x_out, dy_out,
     hot, x_s, g_s, dy_s, gate_s, y_sum, d_sum, y_all, d_all, dgate_c) = rest[-18:]
    e, f = pl.program_id(0), pl.program_id(1)
    rows, width = n_a.shape
    cap = x_s.shape[0] // 2
    expert = first[0] + e
    sources = ((n_a, g_a), (n_b, g_b))

    @pl.when((e == 0) & (f == 0))
    def _():
        dgate_c[...] = jnp.zeros_like(dgate_c)

    @pl.when(f == 0)
    def _():
        for s, (n_ref, g_ref) in enumerate(sources):
            logits = lax.dot_general(router_t[...], n_ref[...], (((1,), (1,)), ((), ())), preferred_element_type=f32)
            ids = lax.broadcasted_iota(jnp.int32, logits.shape, 0)
            power = jnp.exp(logits - jnp.max(logits, axis=0, keepdims=True))
            prob = power / jnp.sum(power, axis=0, keepdims=True)
            chosen = (ids == info[4 * s + 2:4 * s + 3, :]) | (ids == info[4 * s + 3:4 * s + 4, :])
            both = jnp.sum(jnp.where(chosen, prob, 0.0), axis=0, keepdims=True)
            gate_row = jnp.sum(jnp.where(ids == expert, prob, 0.0), axis=0, keepdims=True) / both
            slot_row = jnp.where(e == 0, info[4 * s:4 * s + 1, :], info[4 * s + 1:4 * s + 2, :])
            match = slot_row == lax.broadcasted_iota(jnp.int32, (cap, rows), 0)
            one_hot = jnp.where(match, 1.0, 0.0).astype(bf16)
            part = slice(s * cap, (s + 1) * cap)
            gate_s[part, :] = jnp.sum(jnp.where(match, gate_row, 0.0), axis=1, keepdims=True)
            hot[s, pl.ds(pl.multiple_of(e * cap, cap), cap), :] = one_hot
            x_s[part, :] = jnp.dot(one_hot, n_ref[...], preferred_element_type=f32).astype(bf16)
            g_rows = jnp.dot(one_hot, g_ref[...], preferred_element_type=f32)
            g_s[part, :] = g_rows.astype(bf16)
            dy_s[part, :] = (gate_s[part, :] * g_rows).astype(bf16)
        x_out[0] = x_s[...]
        dy_out[0] = dy_s[...]

    pre = jnp.dot(x_s[...], w_in[0], preferred_element_type=f32)
    act, slope = gelu_and_slope(pre)
    act = act.astype(bf16)
    act_out[0] = act
    dact = lax.dot_general(dy_s[...], w_out[0], (((1,), (1,)), ((), ())), preferred_element_type=f32)
    dpre = (dact * slope).astype(bf16)
    dpre_out[0] = dpre
    y_part = jnp.dot(act, w_out[0], preferred_element_type=f32)
    d_part = lax.dot_general(dpre, w_in[0], (((1,), (1,)), ((), ())), preferred_element_type=f32)

    @pl.when(f == 0)
    def _():
        y_sum[...] = y_part
        d_sum[...] = d_part

    @pl.when(f != 0)
    def _():
        y_sum[...] += y_part
        d_sum[...] += d_part

    @pl.when(f == pl.num_programs(1) - 1)
    def _():
        y_rows = y_sum[...].astype(bf16).astype(f32)
        dgate = jnp.sum(y_rows * g_s[...].astype(f32), axis=1, keepdims=True)
        y_rows = (gate_s[...] * y_rows).astype(bf16)
        d_rows = d_sum[...].astype(bf16)
        for s in range(2):
            part = slice(s * cap, (s + 1) * cap)
            here = pl.ds(pl.multiple_of(e * cap, cap), cap)
            y_all[s, here, :] = y_rows[part]
            d_all[s, here, :] = d_rows[part]
            slot_row = jnp.where(e == 0, info[4 * s:4 * s + 1, :], info[4 * s + 1:4 * s + 2, :])
            match = slot_row == lax.broadcasted_iota(jnp.int32, (cap, rows), 0)
            row = jnp.sum(jnp.where(match, dgate[part], 0.0), axis=0, keepdims=True)
            for c in range(TOP):
                routed = info[4 * s + 2 + c:4 * s + 3 + c, :] == expert
                dgate_c[TOP * s + c:TOP * s + c + 1, :] += jnp.where(routed, row, 0.0)

    @pl.when((e == pl.num_programs(0) - 1) & (f == pl.num_programs(1) - 1))
    def _():
        turn = (((0,), (0,)), ((), ()))
        for s, (y_ref, r_ref) in enumerate(((y_a, r_a), (y_b, r_b))):
            y_ref[...] = lax.dot_general(hot[s], y_all[s], turn, preferred_element_type=f32).astype(bf16)
            r_ref[0:rows, :] = lax.dot_general(hot[s], d_all[s], turn, preferred_element_type=f32).astype(bf16)
            value = dgate_c[TOP * s:TOP * s + TOP, :]
            high = value.astype(bf16)
            value = value - high.astype(f32)
            middle = value.astype(bf16)
            low = (value - middle.astype(f32)).astype(bf16)
            pieces = jnp.concatenate([high.astype(f32), middle.astype(f32), low.astype(f32), jnp.zeros((2, rows), f32)], axis=0)
            over = jnp.concatenate([pieces[:, width:], jnp.zeros((8, 2 * width - rows), f32)], axis=1)
            r_ref[rows:rows + 16, :] = jnp.concatenate([pieces[:, 0:width], over], axis=0).astype(bf16)


def unpack_dgate(tail, rows):
    tail = tail.astype(f32)
    pieces = jnp.concatenate([tail[0:8], tail[8:16]], axis=1)[:, 0:rows]
    return pieces[0:2] + pieces[2:4] + pieces[4:6]


def expert_block(k, blocks, first, n_a, n_b, g_a, g_b, info, router_t, w_in, w_out, cap, kept):
    rows, width = n_a.shape
    local, _, hidden = w_in.shape
    part = 768 if hidden % 768 == 0 else hidden
    once = pl.Buffered(1)
    whole = lambda *shape: pl.BlockSpec(shape, lambda e, f: (0,) * len(shape), pipeline_mode=once)
    wide = pl.BlockSpec((1, 2 * cap, part), lambda e, f: (e, k, f))
    slim = pl.BlockSpec((1, 2 * cap, width), lambda e, f: (e, k, 0))
    slots = blocks * 2 * cap
    shapes = [
        jax.ShapeDtypeStruct((rows, width), bf16), jax.ShapeDtypeStruct((rows, width), bf16),
        jax.ShapeDtypeStruct((rows + 16, width), bf16), jax.ShapeDtypeStruct((rows + 16, width), bf16),
        jax.ShapeDtypeStruct((local, slots, hidden), bf16), jax.ShapeDtypeStruct((local, slots, hidden), bf16),
        jax.ShapeDtypeStruct((local, slots, width), bf16), jax.ShapeDtypeStruct((local, slots, width), bf16),
    ]
    in_specs = [
        pl.BlockSpec(memory_space=pltpu.SMEM), whole(rows, width), whole(rows, width), whole(rows, width), whole(rows, width),
        whole(8, rows), whole(*router_t.shape),
        pl.BlockSpec((1, width, part), lambda e, f: (e, 0, f)), pl.BlockSpec((1, part, width), lambda e, f: (e, f, 0)),
    ]
    args = [first, n_a, n_b, g_a, g_b, info, router_t, w_in, w_out]
    alias = {}
    if kept is not None:
        alias = {len(args) + i: 4 + i for i in range(4)}
        in_specs += [pl.BlockSpec(memory_space=pl.ANY)] * 4
        args += list(kept)
    out = pl.pallas_call(
        expert_kernel,
        grid=(local, hidden // part),
        in_specs=in_specs,
        out_specs=[whole(rows, width), whole(rows, width), whole(rows + 16, width), whole(rows + 16, width), wide, wide, slim, slim],
        out_shape=shapes,
        scratch_shapes=[
            pltpu.VMEM((2, local * cap, rows), bf16),
            pltpu.VMEM((2 * cap, width), bf16), pltpu.VMEM((2 * cap, width), bf16), pltpu.VMEM((2 * cap, width), bf16),
            pltpu.VMEM((2 * cap, 1), f32),
            pltpu.VMEM((2 * cap, width), f32), pltpu.VMEM((2 * cap, width), f32),
            pltpu.VMEM((2, local * cap, width), bf16), pltpu.VMEM((2, local * cap, width), bf16),
            pltpu.VMEM((8, rows), f32),
        ],
        input_output_aliases=alias,
        compiler_params=pltpu.CompilerParams(vmem_limit_bytes=48 * 1024 * 1024),
        cost_estimate=pl.CostEstimate(flops=2 * local * cap * (8 * width * hidden + 8 * width * rows), bytes_accessed=60 * 1024 * 1024, transcendentals=2 * local * cap * hidden),
        name="expert_block",
    )(*args)
    return out[:4], out[4:]


def chip_ring(chips):
    return [0] + list(range(1, chips, 2)) + [z for z in range(chips - 1, 0, -1) if z % 2 == 0]


class Group:
    def __init__(self):
        self.size = lax.axis_size("grp")
        self.chips = self.size // 2
        self.order = chip_ring(self.chips)
        me = lax.axis_index("grp")
        self.me, self.chip, self.core = me, me // 2, me % 2

    def onward(self, x):
        pairs = []
        for i, z in enumerate(self.order):
            after = self.order[(i + 1) % self.chips]
            pairs += [(2 * z, 2 * after), (2 * z + 1, 2 * after + 1)]
        return lax.ppermute(x, "grp", pairs)

    def swap(self, x):
        return lax.ppermute(x, "grp", [(i, i ^ 1) for i in range(self.size)])

    def source_chip(self, k):
        table = [0] * self.chips
        for i, z in enumerate(self.order):
            table[z] = self.order[(i - k) % self.chips]
        return jnp.asarray(table, jnp.int32)[self.chip]


def pick_constant(table, index):
    value = jnp.int32(table[0])
    for i in range(1, len(table)):
        value = jnp.where(index == i, jnp.int32(table[i]), value)
    return value


def gather_kernel(chips, reps, *refs):
    count = 5
    shard, tally = refs[:count], refs[count]
    full, tally_all = refs[count + 1:2 * count + 1], refs[2 * count + 1]
    own_sem, ring_send, ring_recv, core_send, core_recv, rep_send, rep_recv, tally_in, tally_sum, tally_vmem = refs[2 * count + 2:]
    order = chip_ring(chips)
    rep, me = lax.axis_index("rep"), lax.axis_index("grp")
    chip, core = me // 2, me % 2
    after, before = [0] * chips, [0] * chips
    for i, z in enumerate(order):
        after[z], before[z] = order[(i + 1) % chips], order[(i - 1) % chips]
    after = 2 * pick_constant(after, chip) + core
    before = 2 * pick_constant(before, chip) + core
    sibling = 2 * chip + 1 - core
    mesh_id = pl.DeviceIdType.MESH

    barrier = pltpu.get_barrier_semaphore()
    peers = [(rep, after), (rep, before), (rep, sibling)]
    peers += [(lax.rem(rep + k, reps), me) for k in range(1, reps)]
    for peer in peers:
        pl.semaphore_signal(barrier, inc=1, device_id=peer, device_id_type=mesh_id)
    pl.semaphore_wait(barrier, len(peers))

    def place(a, owner):
        if a == count:
            return tally_all.at[owner]
        rows = shard[a].shape[0]
        return full[a].at[pl.ds(pl.multiple_of(owner * rows, rows), rows), :]

    def remote(src, dst, send, recv, target):
        return pltpu.make_async_remote_copy(
            src_ref=src, dst_ref=dst, send_sem=send, recv_sem=recv, device_id=target, device_id_type=mesh_id
        )

    tallies = [
        remote(tally, tally_in.at[k - 1], rep_send.at[k - 1], rep_recv.at[k - 1], (lax.rem(rep + k, reps), me))
        for k in range(1, reps)
    ]
    for copy in tallies:
        copy.start()
    own_tally = pltpu.make_async_copy(tally, tally_vmem, own_sem.at[count])
    own_tally.start()

    pending = []
    moved = [None] * (count + 1)
    own = []
    for a in range(count):
        keep = pltpu.make_async_copy(shard[a], place(a, me), own_sem.at[a])
        keep.start()
        own.append(keep)
        ring = remote(shard[a], place(a, me), ring_send.at[0, a], ring_recv.at[0, a], (rep, after))
        ring.start()
        across = remote(shard[a], place(a, me), core_send.at[0, a], core_recv.at[0, a], (rep, sibling))
        across.start()
        moved[a] = ring
        pending += [ring, across]

    own_tally.wait()
    total = tally_vmem[...]
    for k, copy in enumerate(tallies):
        copy.wait_recv()
        total = total + tally_in[k]
    tally_sum[...] = total
    keep = pltpu.make_async_copy(tally_sum, place(count, me), own_sem.at[count + 1])
    keep.start()
    own.append(keep)
    ring = remote(tally_sum, place(count, me), ring_send.at[0, count], ring_recv.at[0, count], (rep, after))
    ring.start()
    across = remote(tally_sum, place(count, me), core_send.at[0, count], core_recv.at[0, count], (rep, sibling))
    across.start()
    moved[count] = ring
    pending += [ring, across]

    for k in range(1, chips):
        source = [0] * chips
        for i, z in enumerate(order):
            source[z] = order[(i - k) % chips]
        owner = 2 * pick_constant(source, chip) + core
        for a in range(count + 1):
            moved[a].wait_recv()
            block = place(a, owner)
            if k < chips - 1:
                ring = remote(block, block, ring_send.at[k, a], ring_recv.at[k, a], (rep, after))
                ring.start()
                moved[a] = ring
                pending.append(ring)
            across = remote(block, block, core_send.at[k, a], core_recv.at[k, a], (rep, sibling))
            across.start()
            pending.append(across)
    for copy in pending:
        copy.wait_send()
    for copy in tallies:
        copy.wait_send()
    for keep in own:
        keep.wait()
    for k in range(chips):
        source = [0] * chips
        for i, z in enumerate(order):
            source[z] = order[(i - k) % chips]
        owner = 2 * pick_constant(source, chip) + 1 - core
        for a in range(count + 1):
            block = place(a, owner)
            remote(block, block, core_send.at[k, a], core_recv.at[k, a], (rep, sibling)).wait_recv()


def gather_group(arrays, tally):
    size, reps = lax.axis_size("grp"), lax.axis_size("rep")
    chips = size // 2
    count = len(arrays)
    hbm = pl.BlockSpec(memory_space=pl.ANY)
    dma = pltpu.SemaphoreType.DMA
    return pl.pallas_call(
        partial(gather_kernel, chips, reps),
        in_specs=[hbm] * (count + 1),
        out_specs=[hbm] * (count + 1),
        out_shape=[jax.ShapeDtypeStruct((size * x.shape[0], x.shape[1]), x.dtype) for x in arrays]
        + [jax.ShapeDtypeStruct((size,) + tally.shape, f32)],
        scratch_shapes=[
            dma((count + 2,)), dma((chips, count + 1)), dma((chips, count + 1)), dma((chips, count + 1)), dma((chips, count + 1)),
            dma((reps,)), dma((reps,)),
            pltpu.VMEM((reps - 1,) + tally.shape, f32), pltpu.VMEM(tally.shape, f32), pltpu.VMEM(tally.shape, f32),
        ],
        compiler_params=pltpu.CompilerParams(collective_id=0, has_side_effects=True),
        cost_estimate=pl.CostEstimate(flops=0, bytes_accessed=16 * 1024 * 1024, transcendentals=0),
        name="gather_group",
    )(*arrays, tally)


def pack_small(gain_attn, gain_ffn, router, rel_bias, routes):
    def lanes(x):
        return jnp.pad(x, ((0, 0), (0, 128 - x.shape[1])))

    rows = jnp.concatenate([
        lanes(gain_attn[None]), lanes(gain_ffn[None]), lanes(rel_bias), lanes(router.T),
        routes.T.astype(bf16).reshape(-1, 128),
    ], axis=0)
    return jnp.pad(rows, ((0, -rows.shape[0] % 16), (0, 0)))


def unpack_small(packed, size, shard, bias_rows, heads, experts, tokens):
    blocks = packed.reshape(size, -1, 128)
    gain_one = blocks[:, 0, 0:shard].reshape(-1)
    gain_two = blocks[:, 1, 0:shard].reshape(-1)
    at = 2 + bias_rows
    table = blocks[:, 2:at, 0:heads].reshape(-1, heads)
    router_t = jnp.transpose(blocks[:, at:at + experts, 0:shard], (1, 0, 2)).reshape(experts, -1)
    at += experts
    routes = blocks[:, at:at + TOP * tokens // 128].reshape(size, TOP, tokens).astype(jnp.int32)
    return gain_one, gain_two, table, router_t, routes


def outer_sum(left_rows, right_rows):
    return lax.dot_general(
        left_rows, right_rows, (((0,), (0,)), ((), ())), preferred_element_type=jnp.float32
    )


def back_proj(grad_rows, weight):
    return lax.dot_general(
        grad_rows, weight, (((1,), (1,)), ((), ())), preferred_element_type=jnp.float32
    )


def reduce_steps(group, own, sibling, sent_as=bf16):
    moving, total = None, None
    for k in list(range(1, group.chips)) + [0]:
        pins = yield moving, total
        other = group.swap(sibling[k].astype(sent_as))
        if pins is not None:
            other, moving = after((other, moving), pins)
        total = own[k].astype(f32) + other.astype(f32)
        if moving is not None:
            total = total + moving.astype(f32)
        if k != 0:
            total = total.astype(sent_as)
            moving = group.onward(total)
    yield moving, total


def local_slots(routes_all, first, local):
    ids = first + lax.iota(jnp.int32, local)
    hot = jnp.any(routes_all[:, None, :, :] == ids[None, :, None, None], axis=2).astype(jnp.int32)
    return jnp.where(hot != 0, jnp.cumsum(hot, axis=2) - hot, -1)


def shards(
    tokens,
    segments,
    routes,
    gain_attn,
    w_query,
    w_key,
    w_value,
    w_output,
    rel_bias,
    gain_ffn,
    router,
    w_in,
    w_out,
    cotangent,
):
    group = Group()
    tok_rows, width = tokens.shape
    exp_local = w_in.shape[0]
    groups = group.size
    experts = exp_local * groups
    capacity = 2 * tok_rows * TOP // experts
    choose = routes[:, :, None] == lax.iota(jnp.int32, experts)[None, None, :]
    tally = jnp.pad(jnp.sum(choose.astype(f32), axis=(0, 1))[None], ((0, 7), (0, 128 - experts)))
    small = pack_small(gain_attn, gain_ffn, router, rel_bias, routes)
    query_full, key_full, value_full, output_full, small_all, tally_all = gather_group(
        (w_query, w_key, w_value, w_output, small), tally
    )
    gain_one, gain_two, table_full, router_t, routes_all = unpack_small(
        small_all, groups, gain_attn.shape[0], rel_bias.shape[0], rel_bias.shape[1], experts, tok_rows
    )
    router_full = router_t.T
    counts = jnp.sum(tally_all[:, 0, 0:experts], axis=0)
    first = (group.me * exp_local).astype(jnp.int32)
    slots_all = local_slots(routes_all, first, exp_local)

    kept_grad = jnp.where((segments != 0)[:, None], cotangent, jnp.zeros_like(cotangent))
    grad_ring = [kept_grad]
    for k in range(1, group.chips):
        grad_ring.append(group.onward(grad_ring[-1]))

    inputs = tokens.astype(f32)
    scale_one = rms_scale(inputs)
    normed_one = (inputs * scale_one * gain_one.astype(f32)).astype(bf16)
    normed_one = after(normed_one, grad_ring[1])
    query_rows = jnp.dot(normed_one, query_full, preferred_element_type=f32).astype(bf16)
    key_rows = jnp.dot(normed_one, key_full, preferred_element_type=f32).astype(bf16)
    value_rows = jnp.dot(normed_one, value_full, preferred_element_type=f32).astype(bf16)
    base = bias_base(table_full)
    context, lse = attend(query_rows, key_rows, value_rows, segments, base)
    context = after(context, grad_ring[2])
    hidden_one = inputs + jnp.dot(context, output_full, preferred_element_type=f32)
    scale_two = rms_scale(hidden_one)
    normed_two = (hidden_one * scale_two * gain_two.astype(f32)).astype(bf16)

    kept = None
    results = []
    sibs = [group.swap(block) for block in grad_ring[:3]]
    ring = list(grad_ring)
    norm_ring = [normed_two]
    for k in range(group.chips):
        if k >= 3:
            ring[k] = after(ring[k], results[k - 3][2])
            sibs.append(group.swap(ring[k]))
        norm_now = norm_ring[k]
        norm_sib = group.swap(norm_now)
        if k < group.chips - 1:
            moved = group.onward(norm_now)
        chip = group.source_chip(k)
        info = jnp.concatenate(
            [
                lax.dynamic_index_in_dim(rows, 2 * chip + core, 0, keepdims=False)
                for core in (group.core, 1 - group.core)
                for rows in (slots_all, routes_all)
            ],
            axis=0,
        )
        if k == group.chips - 1:
            back_own, back_sib = [r[2] for r in results], [r[3] for r in results]
            back_steps = reduce_steps(group, back_own, back_sib)
            next(back_steps)
            sent = back_steps.send(None)[1]
            info = after(info, sent)
        outs, kept = expert_block(
            k, group.chips, first.reshape(1), norm_now, norm_sib, ring[k], sibs[k],
            info, router_t, w_in, w_out, capacity, kept,
        )
        results.append(outs)
        if k == group.chips - 1:
            back_own.append(outs[2])
            back_sib.append(outs[3])
        if k < group.chips - 1:
            norm_ring.append(after(moved, outs[2]))

    act_all, dpre_all, x_all, dy_all = kept
    chips = group.chips
    for k in range(2, chips - 1):
        sent = back_steps.send(outs[2])[1]
    up_grad = jnp.einsum("ekd,ekf->edf", after(x_all, sent), dpre_all, preferred_element_type=f32).astype(bf16)
    sent = back_steps.send(up_grad)[1]
    up_share = lax.psum_scatter(after(up_grad, sent), "rep", scatter_dimension=1, tiled=True)
    down_grad = jnp.einsum("ekf,ekd->efd", act_all, after(dy_all, sent), preferred_element_type=f32).astype(bf16)
    back = back_steps.send(down_grad)[1]
    down_share = lax.psum_scatter(after(down_grad, back), "rep", scatter_dimension=1, tiled=True)

    y_own, y_sib = after(([r[0] for r in results], [r[1] for r in results]), back)
    y_steps = reduce_steps(group, y_own, y_sib)
    next(y_steps)
    y_moving = y_steps.send(None)[0]

    logits = jnp.dot(normed_two, router_full, preferred_element_type=f32)
    router_prob = jax.nn.softmax(logits, axis=-1)
    picked_prob = jnp.sum(jnp.where(choose, router_prob[:, None, :], 0.0), axis=-1)
    prob_sum = jnp.sum(picked_prob, axis=-1, keepdims=True)
    all_tokens = tok_rows * lax.axis_size("rep") * groups
    fraction = counts / (TOP * all_tokens)

    grad_out = kept_grad.astype(f32)
    grad_gate = unpack_dgate(back[tok_rows:], tok_rows).T
    grad_norm_two = back[0:tok_rows]
    grad_picked = grad_gate / prob_sum - jnp.sum(
        grad_gate * picked_prob, axis=-1, keepdims=True
    ) / (prob_sum * prob_sum)
    grad_router_prob = (
        jnp.sum(jnp.where(choose, grad_picked[:, :, None], 0.0), axis=1)
        + aux_weight * experts * fraction / all_tokens
    )
    grad_logits = (
        router_prob
        * (grad_router_prob - jnp.sum(router_prob * grad_router_prob, axis=-1, keepdims=True))
    ).astype(jnp.bfloat16)
    router_grad = outer_sum(normed_two, grad_logits)
    grad_norm_two = grad_norm_two + back_proj(grad_logits, router_full)
    gain_two_grad = jnp.sum(grad_norm_two * (hidden_one * scale_two), axis=0)
    scaled_two = grad_norm_two * gain_two.astype(jnp.float32)
    grad_hidden_one = (
        grad_out
        + scale_two * scaled_two
        - hidden_one * scale_two**3 * jnp.mean(scaled_two * hidden_one, axis=-1, keepdims=True)
    )
    grad_attn = grad_hidden_one.astype(jnp.bfloat16)
    output_grad = outer_sum(context, grad_attn)
    grad_context = back_proj(grad_attn, output_full).astype(jnp.bfloat16)
    grad_query_rows, grad_key_rows, grad_value_rows, near_grad, far_grad = attend_back(
        query_rows, key_rows, value_rows, segments, base, context, grad_context, lse
    )
    grad_query_rows = after(grad_query_rows, y_moving)
    query_grad = outer_sum(normed_one, grad_query_rows)
    key_grad = outer_sum(normed_one, grad_key_rows)
    value_grad = outer_sum(normed_one, grad_value_rows)
    grad_norm_one = (
        back_proj(grad_query_rows, query_full)
        + back_proj(grad_key_rows, key_full)
        + back_proj(grad_value_rows, value_full)
    )
    gain_one_grad = jnp.sum(grad_norm_one * (inputs * scale_one), axis=0)
    scaled_one = grad_norm_one * gain_one.astype(jnp.float32)
    grad_input = (
        grad_hidden_one
        + scale_one * scaled_one
        - inputs * scale_one**3 * jnp.mean(scaled_one * inputs, axis=-1, keepdims=True)
    )
    table_grad = table_back(near_grad, far_grad, table_full.shape[0])
    def shares(x, rows):
        x = x.reshape(x.shape[:-2] + (groups, rows, x.shape[-1]))
        def one(k, core):
            return lax.dynamic_index_in_dim(x, 2 * group.source_chip(k) + core, x.ndim - 3, keepdims=False)
        return [one(k, group.core) for k in range(chips)], [one(k, 1 - group.core) for k in range(chips)]

    for k in range(2, chips):
        y_steps.send(grad_query_rows)
    rows = width // groups
    dense = after(jnp.stack([query_grad, key_grad, value_grad, output_grad]).astype(bf16), grad_input)
    dense_steps = reduce_steps(group, *shares(dense, rows))

    def lanes(x):
        return jnp.pad(x, ((0, 0), (0, 0), (0, 128 - x.shape[2])))

    heads = table_grad.shape[1]
    bias_rows = table_grad.shape[0] // groups
    prob_row = jnp.broadcast_to(jnp.sum(router_prob, axis=0), (groups, 1, experts))
    small = jnp.concatenate([
        lanes(gain_one_grad.reshape(groups, 1, rows)), lanes(gain_two_grad.reshape(groups, 1, rows)),
        lanes(prob_row), lanes(table_grad.reshape(groups, bias_rows, heads)),
        lanes(jnp.transpose(router_grad.T.reshape(experts, groups, rows), (1, 0, 2))),
    ], axis=1)
    small = jnp.pad(small, ((0, 0), (0, -small.shape[1] % 8), (0, 0)))
    small_steps = reduce_steps(group, *shares(small.reshape(-1, 128), small.shape[1]), f32)
    next(dense_steps)
    next(small_steps)
    for k in range(chips):
        dense_sum, small_sum = dense_steps.send(None)[1], small_steps.send(None)[1]
    mixed = y_steps.send(grad_input)[1]
    output = (hidden_one + mixed).astype(bf16)

    def over_rep(x):
        total = x.astype(f32)
        for k in range(1, lax.axis_size("rep")):
            total = total + lax.ppermute(x, "rep", [(i, i ^ k) for i in range(lax.axis_size("rep"))]).astype(f32)
        return total

    dense, small = over_rep(dense_sum.astype(bf16)), over_rep(small_sum)
    at = 3 + bias_rows
    balance_terms = experts * experts * fraction * (small[2, 0:experts] / all_tokens)
    loss = aux_weight / experts * jnp.sum(balance_terms)
    return (
        output,
        loss,
        balance_terms,
        grad_input,
        small[0, 0:rows],
        dense[0],
        dense[1],
        dense[2],
        dense[3],
        small[3:at, 0:heads],
        small[1, 0:rows],
        small[at:at + experts, 0:rows].T,
        up_share.astype(f32),
        down_share.astype(f32),
    )


def solution(mesh):
    return jax.shard_map(
        shards,
        mesh=mesh,
        in_specs=(
            P(("rep", "grp"), None),
            P(("rep", "grp")),
            P(("rep", "grp"), None),
            P("grp"),
            P("grp", None),
            P("grp", None),
            P("grp", None),
            P("grp", None),
            P("grp", None),
            P("grp"),
            P("grp", None),
            P("grp", None, None),
            P("grp", None, None),
            P(("rep", "grp"), None),
        ),
        out_specs=(
            P(("rep", "grp"), None),
            P(),
            P(),
            P(("rep", "grp"), None),
            P("grp"),
            P("grp", None),
            P("grp", None),
            P("grp", None),
            P("grp", None),
            P("grp", None),
            P("grp"),
            P("grp", None),
            P("grp", "rep", None),
            P("grp", "rep", None),
        ),
        check_vma=False,
    )
```

```python
from functools import partial

import jax
import jax.numpy as jnp
from jax import lax
from jax.experimental import pallas as pl
from jax.experimental.pallas import tpu as pltpu
from jax.sharding import PartitionSpec as P

TOP = 2
QB = 128
PAIR = 128
NEAR = 2 * QB
SPAN = 3 * QB
OUT_OF_DOC = -1e30
FAR_MARKS = (18, 20, 23, 26, 30, 34, 39, 45, 51, 58, 66, 76, 86, 98, 112)
norm_eps = 1e-06
aux_weight = 0.01
f32, bf16 = jnp.float32, jnp.bfloat16


def after(x, *earlier):
    return lax.optimization_barrier((x, earlier))[0]


def rms_scale(values):
    return lax.rsqrt(jnp.mean(values * values, axis=-1, keepdims=True) + norm_eps)


def bucket_of(distance):
    far_part = jnp.zeros_like(distance)
    for far_mark in FAR_MARKS:
        far_part = far_part + (distance >= far_mark).astype(jnp.int32)
    return jnp.minimum(distance, 16) + far_part


def band_hot(buckets):
    lane = lax.broadcasted_iota(jnp.int32, (8, SPAN), 1)
    row = lax.broadcasted_iota(jnp.int32, (8, SPAN), 0)
    turn = (lane - row + SPAN) % SPAN
    diff = jnp.where(turn < QB, turn, turn - SPAN) + QB
    bucket = bucket_of(jnp.maximum(diff, 0)).reshape(1, 8 * SPAN)
    return bucket == lax.iota(jnp.int32, buckets)[:, None]


def split_pair(rows, low_lanes):
    zero = jnp.zeros_like(rows)
    return jnp.concatenate(
        [jnp.where(low_lanes, rows, zero), jnp.where(low_lanes, zero, rows)], axis=0
    )


def fill_mask(seg_col, seg_row, mask):
    seq = mask.shape[0]
    for i in range(seq // QB):
        length = (i + 1) * QB
        sk = seg_col[0:length, :]
        sq = seg_row[:, i * QB:(i + 1) * QB]
        kp = lax.broadcasted_iota(jnp.int32, (length, QB), 0)
        qp = lax.broadcasted_iota(jnp.int32, (length, QB), 1) + i * QB
        ok = (sk == sq) & (kp <= qp) & ((sq != 0) | (kp == qp))
        mask[0:length, i * QB:(i + 1) * QB] = jnp.where(ok, 0.0, OUT_OF_DOC).astype(f32)


def fill_near(base, near):
    for head in range(2):
        rows = base[head]
        for a in range(NEAR // 8):
            turned = rows if a == 0 else pltpu.roll(rows, 8 * a, 1)
            near[8 * a:8 * a + 8, head * QB:(head + 1) * QB] = turned[:, 0:QB]


def scores_chunk(k, lo, hi, qcat, mask, near, i):
    s = lax.dot_general(k[lo:hi, :], qcat, (((1,), (1,)), ((), ())), preferred_element_type=f32)
    m = mask[lo:hi, i * QB:(i + 1) * QB]
    s = s + jnp.concatenate([m, m], axis=1)
    start = (i - 1) * QB
    if lo >= start:
        s = s + near[lo - start:hi - start, :]
    return s


def fwd_kernel(base, seg_col, seg_row, q, k, v, ctx, lse, mask, near, scores, probs, v_t):
    seq = q.shape[0]

    @pl.when(pl.program_id(0) == 0)
    def _():
        fill_mask(seg_col, seg_row, mask)

    fill_near(base, near)
    v_t[...] = v[...].T
    low_lanes = lax.broadcasted_iota(jnp.int32, (QB, PAIR), 1) < PAIR // 2
    scale = (PAIR // 2) ** -0.5
    for i in range(seq // QB):
        qs = slice(i * QB, (i + 1) * QB)
        qcat = split_pair(q[qs, :] * jnp.asarray(scale, bf16), low_lanes)
        top = None
        for c in range(i + 1):
            s = scores_chunk(k, c * QB, (c + 1) * QB, qcat, mask, near, i)
            scores[c * QB:(c + 1) * QB, :] = s
            here = jnp.max(s.reshape(QB // 8, 8, NEAR), axis=0)
            top = here if top is None else jnp.maximum(top, here)
        top = jnp.max(top, axis=0, keepdims=True)
        total = jnp.zeros((8, NEAR), f32)
        for c in range(i + 1):
            p = jnp.exp(scores[c * QB:(c + 1) * QB, :] - top)
            total = total + jnp.sum(p.reshape(QB // 8, 8, NEAR), axis=0)
            probs[c * QB:(c + 1) * QB, :] = p.astype(bf16)
        total = jnp.sum(total, axis=0, keepdims=True)
        length = (i + 1) * QB
        out = jnp.dot(v_t[:, 0:length], probs[0:length, :], preferred_element_type=f32) / total
        half = PAIR // 2
        both = jnp.concatenate([out[0:half, 0:QB], out[half:PAIR, QB:NEAR]], axis=0)
        ctx[qs, :] = both.T.astype(bf16)
        lse[0, i:i + 1, :] = top + jnp.log(total)


def attend(q, k, v, seg, base):
    seq, width = q.shape
    pairs = width // PAIR
    col = pl.BlockSpec((seq, PAIR), lambda h: (0, h))
    whole = lambda *shape: pl.BlockSpec(shape, lambda h: (0,) * len(shape))
    return pl.pallas_call(
        fwd_kernel,
        grid=(pairs,),
        in_specs=[pl.BlockSpec((2, 8, SPAN), lambda h: (h, 0, 0)), whole(seq, 1), whole(1, seq), col, col, col],
        out_specs=[col, pl.BlockSpec((1, seq // QB, NEAR), lambda h: (h, 0, 0))],
        out_shape=[
            jax.ShapeDtypeStruct((seq, width), bf16),
            jax.ShapeDtypeStruct((pairs, seq // QB, NEAR), f32),
        ],
        scratch_shapes=[
            pltpu.VMEM((seq, seq), f32),
            pltpu.VMEM((NEAR, NEAR), f32),
            pltpu.VMEM((seq, NEAR), f32),
            pltpu.VMEM((seq, NEAR), bf16),
            pltpu.VMEM((PAIR, seq), bf16),
        ],
        compiler_params=pltpu.CompilerParams(vmem_limit_bytes=32 * 1024 * 1024),
        cost_estimate=pl.CostEstimate(flops=1, bytes_accessed=1024, transcendentals=0),
        name="attend",
    )(base, seg.reshape(seq, 1), seg.reshape(1, seq), q, k, v)


def bwd_kernel(base, seg_col, seg_row, q, k, v, ctx, dctx, lse, dq, dk, dv, dnear, dfar,
               mask, near, ds_all, p_all, k_t, dk_sum, dv_sum, dnear_sum, dfar_sum):
    seq = q.shape[0]

    @pl.when(pl.program_id(0) == 0)
    def _():
        fill_mask(seg_col, seg_row, mask)

    fill_near(base, near)
    k_t[...] = k[...].T
    low_lanes = lax.broadcasted_iota(jnp.int32, (QB, PAIR), 1) < PAIR // 2
    half = PAIR // 2
    scale = half ** -0.5
    dnear_sum[...] = jnp.zeros_like(dnear_sum)
    dfar_sum[...] = jnp.zeros_like(dfar_sum)
    for i in reversed(range(seq // QB)):
        qs = slice(i * QB, (i + 1) * QB)
        length = (i + 1) * QB
        qcat = split_pair(q[qs, :] * jnp.asarray(scale, bf16), low_lanes)
        dcat = split_pair(dctx[qs, :], low_lanes)
        dots = (ctx[qs, :].astype(f32) * dctx[qs, :].astype(f32)).T
        centre = jnp.concatenate(
            [jnp.sum(dots[0:half], axis=0, keepdims=True), jnp.sum(dots[half:], axis=0, keepdims=True)], axis=1
        )
        norm = lse[0, i:i + 1, :]
        for c in range(i + 1):
            lo, hi = c * QB, (c + 1) * QB
            s = scores_chunk(k, lo, hi, qcat, mask, near, i)
            p = jnp.exp(s - norm)
            p_all[lo:hi, :] = p.astype(bf16)
            dp = lax.dot_general(v[lo:hi, :], dcat, (((1,), (1,)), ((), ())), preferred_element_type=f32)
            ds = p * (dp - centre)
            ds_all[lo:hi, :] = ds.astype(bf16)
            start = (i - 1) * QB
            if lo >= start:
                dnear_sum[lo - start:hi - start, :] += ds
            else:
                dfar_sum[...] += jnp.sum(ds.reshape(QB // 8, 8, NEAR), axis=0)
        out = jnp.dot(k_t[:, 0:length], ds_all[0:length, :], preferred_element_type=f32)
        both = jnp.concatenate([out[0:half, 0:QB], out[half:PAIR, QB:NEAR]], axis=0)
        dq[qs, :] = (both.T * scale).astype(bf16)
        dk_part = jnp.dot(ds_all[0:length, :], qcat, preferred_element_type=f32)
        dv_part = jnp.dot(p_all[0:length, :], dcat, preferred_element_type=f32)
        if i == seq // QB - 1:
            dk_sum[0:length, :] = dk_part
            dv_sum[0:length, :] = dv_part
        else:
            dk_sum[0:length, :] += dk_part
            dv_sum[0:length, :] += dv_part
    dk[...] = dk_sum[...].astype(bf16)
    dv[...] = dv_sum[...].astype(bf16)
    for head in range(2):
        total = jnp.zeros((8, SPAN), f32)
        for a in range(NEAR // 8):
            rows = dnear_sum[8 * a:8 * a + 8, head * QB:(head + 1) * QB]
            rows = jnp.concatenate([rows, jnp.zeros((8, SPAN - QB), f32)], axis=1)
            total = total + (rows if a == 0 else pltpu.roll(rows, SPAN - 8 * a, 1))
        dnear[head] = total
    dfar[0] = dfar_sum[...]


def attend_back(q, k, v, seg, base, ctx, dctx, lse):
    seq, width = q.shape
    pairs = width // PAIR
    col = pl.BlockSpec((seq, PAIR), lambda h: (0, h))
    band = pl.BlockSpec((2, 8, SPAN), lambda h: (h, 0, 0))
    whole = lambda *shape: pl.BlockSpec(shape, lambda h: (0,) * len(shape))
    rows = jax.ShapeDtypeStruct((seq, width), bf16)
    return pl.pallas_call(
        bwd_kernel,
        grid=(pairs,),
        in_specs=[band, whole(seq, 1), whole(1, seq), col, col, col, col, col,
                  pl.BlockSpec((1, seq // QB, NEAR), lambda h: (h, 0, 0))],
        out_specs=[col, col, col, band, pl.BlockSpec((1, 8, NEAR), lambda h: (h, 0, 0))],
        out_shape=[rows, rows, rows, jax.ShapeDtypeStruct((2 * pairs, 8, SPAN), f32),
                   jax.ShapeDtypeStruct((pairs, 8, NEAR), f32)],
        scratch_shapes=[
            pltpu.VMEM((seq, seq), f32),
            pltpu.VMEM((NEAR, NEAR), f32),
            pltpu.VMEM((seq, NEAR), bf16),
            pltpu.VMEM((seq, NEAR), bf16),
            pltpu.VMEM((PAIR, seq), bf16),
            pltpu.VMEM((seq, PAIR), f32),
            pltpu.VMEM((seq, PAIR), f32),
            pltpu.VMEM((NEAR, NEAR), f32),
            pltpu.VMEM((8, NEAR), f32),
        ],
        compiler_params=pltpu.CompilerParams(vmem_limit_bytes=40 * 1024 * 1024),
        cost_estimate=pl.CostEstimate(flops=1, bytes_accessed=1024, transcendentals=0),
        name="attend_back",
    )(base, seg.reshape(seq, 1), seg.reshape(1, seq), q, k, v, ctx, dctx, lse)


def bias_base(table):
    buckets, heads = table.shape
    hot = band_hot(buckets).astype(bf16)
    base = lax.dot_general(table, hot, (((0,), (0,)), ((), ())), preferred_element_type=f32)
    last = table[buckets - 1].astype(f32)
    return base.reshape(heads, 8, SPAN) - last[:, None, None]


def table_back(dnear, dfar, buckets):
    heads = dnear.shape[0]
    hot = band_hot(buckets).astype(f32)
    grad = lax.dot_general(hot, dnear.reshape(heads, 8 * SPAN), (((1,), (1,)), ((), ())),
                           preferred_element_type=f32, precision=lax.Precision.HIGHEST)
    far = jnp.sum(dfar.reshape(heads // 2, 8, 2, QB), axis=(1, 3)).reshape(1, heads)
    last = (lax.iota(jnp.int32, buckets) == buckets - 1)[:, None]
    return grad + jnp.where(last, far, 0.0)


def gelu_and_slope(u):
    root = (2.0 / jnp.pi) ** 0.5
    square = u * u
    bent = jnp.tanh(u * (root + (root * 0.044715) * square))
    rise = 0.5 + 0.5 * bent
    slope = rise + (0.5 * u) * (1.0 - bent * bent) * (root + (root * 3 * 0.044715) * square)
    return u * rise, slope


def expert_kernel(first, n_a, n_b, g_a, g_b, info, router_t, w_in, w_out, *rest):
    (y_a, y_b, r_a, r_b, act_out, dpre_out, x_out, dy_out,
     hot, x_s, g_s, dy_s, gate_s, y_sum, d_sum, y_all, d_all, dgate_c) = rest[-18:]
    e, f = pl.program_id(0), pl.program_id(1)
    rows, width = n_a.shape
    cap = x_s.shape[0] // 2
    expert = first[0] + e
    sources = ((n_a, g_a), (n_b, g_b))

    @pl.when((e == 0) & (f == 0))
    def _():
        dgate_c[...] = jnp.zeros_like(dgate_c)

    @pl.when(f == 0)
    def _():
        for s, (n_ref, g_ref) in enumerate(sources):
            logits = lax.dot_general(router_t[...], n_ref[...], (((1,), (1,)), ((), ())), preferred_element_type=f32)
            ids = lax.broadcasted_iota(jnp.int32, logits.shape, 0)
            power = jnp.exp(logits - jnp.max(logits, axis=0, keepdims=True))
            prob = power / jnp.sum(power, axis=0, keepdims=True)
            chosen = (ids == info[4 * s + 2:4 * s + 3, :]) | (ids == info[4 * s + 3:4 * s + 4, :])
            both = jnp.sum(jnp.where(chosen, prob, 0.0), axis=0, keepdims=True)
            gate_row = jnp.sum(jnp.where(ids == expert, prob, 0.0), axis=0, keepdims=True) / both
            slot_row = jnp.where(e == 0, info[4 * s:4 * s + 1, :], info[4 * s + 1:4 * s + 2, :])
            match = slot_row == lax.broadcasted_iota(jnp.int32, (cap, rows), 0)
            one_hot = jnp.where(match, 1.0, 0.0).astype(bf16)
            part = slice(s * cap, (s + 1) * cap)
            gate_s[part, :] = jnp.sum(jnp.where(match, gate_row, 0.0), axis=1, keepdims=True)
            hot[s, pl.ds(pl.multiple_of(e * cap, cap), cap), :] = one_hot
            x_s[part, :] = jnp.dot(one_hot, n_ref[...], preferred_element_type=f32).astype(bf16)
            g_rows = jnp.dot(one_hot, g_ref[...], preferred_element_type=f32)
            g_s[part, :] = g_rows.astype(bf16)
            dy_s[part, :] = (gate_s[part, :] * g_rows).astype(bf16)
        y_sum[...] = jnp.zeros_like(y_sum)
        d_sum[...] = jnp.zeros_like(d_sum)
        x_out[0] = x_s[...]
        dy_out[0] = dy_s[...]

    pre = jnp.dot(x_s[...], w_in[0], preferred_element_type=f32)
    dact = lax.dot_general(dy_s[...], w_out[0], (((1,), (1,)), ((), ())), preferred_element_type=f32)
    act, slope = gelu_and_slope(pre)
    act_out[0] = act.astype(bf16)
    dpre_out[0] = (dact * slope).astype(bf16)
    y_sum[...] += jnp.dot(act_out[0], w_out[0], preferred_element_type=f32)
    d_sum[...] += lax.dot_general(dpre_out[0], w_in[0], (((1,), (1,)), ((), ())), preferred_element_type=f32)

    @pl.when(f == pl.num_programs(1) - 1)
    def _():
        y_rows = y_sum[...].astype(bf16).astype(f32)
        dgate = jnp.sum(y_rows * g_s[...].astype(f32), axis=1, keepdims=True)
        y_rows = (gate_s[...] * y_rows).astype(bf16)
        d_rows = d_sum[...].astype(bf16)
        for s in range(2):
            part = slice(s * cap, (s + 1) * cap)
            here = pl.ds(pl.multiple_of(e * cap, cap), cap)
            y_all[s, here, :] = y_rows[part]
            d_all[s, here, :] = d_rows[part]
            slot_row = jnp.where(e == 0, info[4 * s:4 * s + 1, :], info[4 * s + 1:4 * s + 2, :])
            match = slot_row == lax.broadcasted_iota(jnp.int32, (cap, rows), 0)
            row = jnp.sum(jnp.where(match, dgate[part], 0.0), axis=0, keepdims=True)
            for c in range(TOP):
                routed = info[4 * s + 2 + c:4 * s + 3 + c, :] == expert
                dgate_c[TOP * s + c:TOP * s + c + 1, :] += jnp.where(routed, row, 0.0)

    @pl.when((e == pl.num_programs(0) - 1) & (f == pl.num_programs(1) - 1))
    def _():
        turn = (((0,), (0,)), ((), ()))
        for s, (y_ref, r_ref) in enumerate(((y_a, r_a), (y_b, r_b))):
            y_ref[...] = lax.dot_general(hot[s], y_all[s], turn, preferred_element_type=f32).astype(bf16)
            r_ref[0:rows, :] = lax.dot_general(hot[s], d_all[s], turn, preferred_element_type=f32).astype(bf16)
            value = dgate_c[TOP * s:TOP * s + TOP, :]
            high = value.astype(bf16)
            value = value - high.astype(f32)
            middle = value.astype(bf16)
            low = (value - middle.astype(f32)).astype(bf16)
            pieces = jnp.concatenate([high.astype(f32), middle.astype(f32), low.astype(f32), jnp.zeros((2, rows), f32)], axis=0)
            over = jnp.concatenate([pieces[:, width:], jnp.zeros((8, 2 * width - rows), f32)], axis=1)
            r_ref[rows:rows + 16, :] = jnp.concatenate([pieces[:, 0:width], over], axis=0).astype(bf16)


def unpack_dgate(tail, rows):
    tail = tail.astype(f32)
    pieces = jnp.concatenate([tail[0:8], tail[8:16]], axis=1)[:, 0:rows]
    return pieces[0:2] + pieces[2:4] + pieces[4:6]


def expert_block(k, blocks, first, n_a, n_b, g_a, g_b, info, router_t, w_in, w_out, cap, kept):
    rows, width = n_a.shape
    local, _, hidden = w_in.shape
    part = 768 if hidden % 768 == 0 else hidden
    once = pl.Buffered(1)
    whole = lambda *shape: pl.BlockSpec(shape, lambda e, f: (0,) * len(shape), pipeline_mode=once)
    wide = pl.BlockSpec((1, 2 * cap, part), lambda e, f: (e, k, f))
    slim = pl.BlockSpec((1, 2 * cap, width), lambda e, f: (e, k, 0))
    slots = blocks * 2 * cap
    shapes = [
        jax.ShapeDtypeStruct((rows, width), bf16), jax.ShapeDtypeStruct((rows, width), bf16),
        jax.ShapeDtypeStruct((rows + 16, width), bf16), jax.ShapeDtypeStruct((rows + 16, width), bf16),
        jax.ShapeDtypeStruct((local, slots, hidden), bf16), jax.ShapeDtypeStruct((local, slots, hidden), bf16),
        jax.ShapeDtypeStruct((local, slots, width), bf16), jax.ShapeDtypeStruct((local, slots, width), bf16),
    ]
    in_specs = [
        pl.BlockSpec(memory_space=pltpu.SMEM), whole(rows, width), whole(rows, width), whole(rows, width), whole(rows, width),
        whole(8, rows), whole(*router_t.shape),
        pl.BlockSpec((1, width, part), lambda e, f: (e, 0, f)), pl.BlockSpec((1, part, width), lambda e, f: (e, f, 0)),
    ]
    args = [first, n_a, n_b, g_a, g_b, info, router_t, w_in, w_out]
    alias = {}
    if kept is not None:
        alias = {len(args) + i: 4 + i for i in range(4)}
        in_specs += [pl.BlockSpec(memory_space=pl.ANY)] * 4
        args += list(kept)
    out = pl.pallas_call(
        expert_kernel,
        grid=(local, hidden // part),
        in_specs=in_specs,
        out_specs=[whole(rows, width), whole(rows, width), whole(rows + 16, width), whole(rows + 16, width), wide, wide, slim, slim],
        out_shape=shapes,
        scratch_shapes=[
            pltpu.VMEM((2, local * cap, rows), bf16),
            pltpu.VMEM((2 * cap, width), bf16), pltpu.VMEM((2 * cap, width), bf16), pltpu.VMEM((2 * cap, width), bf16),
            pltpu.VMEM((2 * cap, 1), f32),
            pltpu.VMEM((2 * cap, width), f32), pltpu.VMEM((2 * cap, width), f32),
            pltpu.VMEM((2, local * cap, width), bf16), pltpu.VMEM((2, local * cap, width), bf16),
            pltpu.VMEM((8, rows), f32),
        ],
        input_output_aliases=alias,
        compiler_params=pltpu.CompilerParams(vmem_limit_bytes=48 * 1024 * 1024),
        cost_estimate=pl.CostEstimate(flops=2 * local * cap * (8 * width * hidden + 8 * width * rows), bytes_accessed=60 * 1024 * 1024, transcendentals=2 * local * cap * hidden),
        name="expert_block",
    )(*args)
    return out[:4], out[4:]


def chip_ring(chips):
    return [0] + list(range(1, chips, 2)) + [z for z in range(chips - 1, 0, -1) if z % 2 == 0]


class Group:
    def __init__(self):
        self.size = lax.axis_size("grp")
        self.chips = self.size // 2
        self.order = chip_ring(self.chips)
        me = lax.axis_index("grp")
        self.me, self.chip, self.core = me, me // 2, me % 2

    def onward(self, x):
        pairs = []
        for i, z in enumerate(self.order):
            after = self.order[(i + 1) % self.chips]
            pairs += [(2 * z, 2 * after), (2 * z + 1, 2 * after + 1)]
        return lax.ppermute(x, "grp", pairs)

    def swap(self, x):
        return lax.ppermute(x, "grp", [(i, i ^ 1) for i in range(self.size)])

    def source_chip(self, k):
        table = [0] * self.chips
        for i, z in enumerate(self.order):
            table[z] = self.order[(i - k) % self.chips]
        return jnp.asarray(table, jnp.int32)[self.chip]


def pick_constant(table, index):
    value = jnp.int32(table[0])
    for i in range(1, len(table)):
        value = jnp.where(index == i, jnp.int32(table[i]), value)
    return value


def gather_kernel(chips, reps, stack, small, tally, stack_all, small_all, tally_all,
                  own_sem, ring_send, ring_recv, core_send, core_recv, own_send, own_recv,
                  plane_send, plane_recv, cross_send, cross_recv, rep_send, rep_recv, tally_in, tally_sum, tally_vmem):
    order = chip_ring(chips)
    mats, rows = stack.shape[0], stack.shape[1]
    rep, me = lax.axis_index("rep"), lax.axis_index("grp")
    chip, core = me // 2, me % 2
    mine = lax.rem(rep, mats)
    after_z, before_z = [0] * chips, [0] * chips
    for i, z in enumerate(order):
        after_z[z], before_z[z] = order[(i + 1) % chips], order[(i - 1) % chips]
    onward = 2 * pick_constant(after_z, chip) + core
    before = 2 * pick_constant(before_z, chip) + core
    sibling = 2 * chip + 1 - core
    mesh_id = pl.DeviceIdType.MESH
    plane = [(rep - mine) + lax.rem(mine + j, mats) for j in range(1, mats)]

    barrier = pltpu.get_barrier_semaphore()
    peers = [(rep, onward), (rep, before), (rep, sibling)] + [(lax.rem(rep + k, reps), me) for k in range(1, reps)]
    for peer in peers:
        pl.semaphore_signal(barrier, inc=1, device_id=peer, device_id_type=mesh_id)
    pl.semaphore_wait(barrier, len(peers))

    def remote(src, dst, send, recv, target):
        return pltpu.make_async_remote_copy(
            src_ref=src, dst_ref=dst, send_sem=send, recv_sem=recv, device_id=target, device_id_type=mesh_id
        )

    def owner_of(k, which_core):
        source = [0] * chips
        for i, z in enumerate(order):
            source[z] = order[(i - k) % chips]
        return 2 * pick_constant(source, chip) + which_core

    def shard(mat, owner):
        return stack_all.at[mat, pl.ds(pl.multiple_of(owner * rows, rows), rows), :]

    def places(k, which_core):
        owner = owner_of(k, which_core)
        return [shard(mine, owner), small_all.at[owner], tally_all.at[owner]]

    def matrix(j):
        return lax.rem(mine + j, mats)

    sent = []

    def start(copy):
        copy.start()
        sent.append(copy)
        return copy

    tallies = [
        start(remote(tally, tally_in.at[k - 1], rep_send.at[k - 1], rep_recv.at[k - 1], (lax.rem(rep + k, reps), me)))
        for k in range(1, reps)
    ]
    own = [
        pltpu.make_async_copy(stack, stack_all.at[:, pl.ds(pl.multiple_of(me * rows, rows), rows), :], own_sem.at[0]),
        pltpu.make_async_copy(small, small_all.at[me], own_sem.at[1]),
        pltpu.make_async_copy(tally, tally_vmem, own_sem.at[2]),
    ]
    for copy in own:
        copy.start()
    here = places(0, core)
    moved = [
        start(remote(stack.at[mine], here[0], ring_send.at[0, 0], ring_recv.at[0, 0], (rep, onward))),
        start(remote(small, here[1], ring_send.at[0, 1], ring_recv.at[0, 1], (rep, onward))),
    ]
    everywhere = stack_all.at[:, pl.ds(pl.multiple_of(me * rows, rows), rows), :]
    start(remote(small, here[1], core_send.at[0, 1], core_recv.at[0, 1], (rep, sibling)))
    start(remote(stack, everywhere, own_send, own_recv, (rep, sibling)))
    own[2].wait()
    total = tally_vmem[...]
    for k, copy in enumerate(tallies):
        copy.wait_recv()
        total = total + tally_in[k]
    tally_sum[...] = total
    keep = pltpu.make_async_copy(tally_sum, here[2], own_sem.at[3])
    keep.start()
    own = [own[0], own[1], keep]
    moved.append(start(remote(tally_sum, here[2], ring_send.at[0, 2], ring_recv.at[0, 2], (rep, onward))))
    start(remote(tally_sum, here[2], core_send.at[0, 2], core_recv.at[0, 2], (rep, sibling)))

    def pass_across(k):
        for j in range(1, mats):
            block = shard(matrix(j), owner_of(k, core))
            remote(block, block, plane_send.at[k, j - 1], plane_recv.at[k, mats - 1 - j], (plane[j - 1], me)).wait_recv()
            start(remote(block, block, cross_send.at[k, mats - 1 - j], cross_recv.at[k, j - 1], (rep, sibling)))

    for k in range(1, chips):
        here = places(k, core)
        for a in range(3):
            moved[a].wait_recv()
            if k < chips - 1:
                moved[a] = start(remote(here[a], here[a], ring_send.at[k, a], ring_recv.at[k, a], (rep, onward)))
            if a == 0:
                for j in range(1, mats):
                    start(remote(here[0], here[0], plane_send.at[k, j - 1], plane_recv.at[k, j - 1], (plane[j - 1], me)))
            start(remote(here[a], here[a], core_send.at[k, a], core_recv.at[k, a], (rep, sibling)))
        if k > 1:
            pass_across(k - 1)
    pass_across(chips - 1)
    for copy in sent:
        copy.wait_send()
    for copy in own:
        copy.wait()
    other = stack_all.at[:, pl.ds(pl.multiple_of(sibling * rows, rows), rows), :]
    remote(stack, other, own_send, own_recv, (rep, sibling)).wait_recv()
    for k in range(chips):
        there = places(k, 1 - core)
        for a in range(3):
            if a > 0 or k > 0:
                remote(there[a], there[a], core_send.at[k, a], core_recv.at[k, a], (rep, sibling)).wait_recv()
        if k > 0:
            for j in range(1, mats):
                block = shard(matrix(j), owner_of(k, 1 - core))
                remote(block, block, cross_send.at[k, j - 1], cross_recv.at[k, j - 1], (rep, sibling)).wait_recv()


def gather_group(stack, small, tally):
    size, reps = lax.axis_size("grp"), lax.axis_size("rep")
    chips = size // 2
    mats, rows, width = stack.shape
    hbm = pl.BlockSpec(memory_space=pl.ANY)
    dma = pltpu.SemaphoreType.DMA
    return pl.pallas_call(
        partial(gather_kernel, chips, reps),
        in_specs=[hbm] * 3,
        out_specs=[hbm] * 3,
        out_shape=[
            jax.ShapeDtypeStruct((mats, size * rows, width), stack.dtype),
            jax.ShapeDtypeStruct((size,) + small.shape, small.dtype),
            jax.ShapeDtypeStruct((size,) + tally.shape, f32),
        ],
        scratch_shapes=[
            dma((4,)), dma((chips, 3)), dma((chips, 3)), dma((chips, 3)), dma((chips, 3)), dma, dma,
            dma((chips, mats - 1)), dma((chips, mats - 1)), dma((chips, mats - 1)), dma((chips, mats - 1)),
            dma((reps,)), dma((reps,)),
            pltpu.VMEM((reps - 1,) + tally.shape, f32), pltpu.VMEM(tally.shape, f32), pltpu.VMEM(tally.shape, f32),
        ],
        compiler_params=pltpu.CompilerParams(collective_id=0, has_side_effects=True),
        cost_estimate=pl.CostEstimate(flops=0, bytes_accessed=16 * 1024 * 1024, transcendentals=0),
        name="gather_group",
    )(stack, small, tally)


def pack_small(gain_attn, gain_ffn, router, rel_bias, routes):
    def lanes(x):
        return jnp.pad(x, ((0, 0), (0, 128 - x.shape[1])))

    rows = jnp.concatenate([
        lanes(gain_attn[None]), lanes(gain_ffn[None]), lanes(rel_bias), lanes(router.T),
        routes.T.astype(bf16).reshape(-1, 128),
    ], axis=0)
    return jnp.pad(rows, ((0, -rows.shape[0] % 16), (0, 0)))


def unpack_small(packed, size, shard, bias_rows, heads, experts, tokens):
    blocks = packed.reshape(size, -1, 128)
    gain_one = blocks[:, 0, 0:shard].reshape(-1)
    gain_two = blocks[:, 1, 0:shard].reshape(-1)
    at = 2 + bias_rows
    table = blocks[:, 2:at, 0:heads].reshape(-1, heads)
    router_t = jnp.transpose(blocks[:, at:at + experts, 0:shard], (1, 0, 2)).reshape(experts, -1)
    at += experts
    routes = blocks[:, at:at + TOP * tokens // 128].reshape(size, TOP, tokens).astype(jnp.int32)
    return gain_one, gain_two, table, router_t, routes


def outer_sum(left_rows, right_rows):
    return lax.dot_general(
        left_rows, right_rows, (((0,), (0,)), ((), ())), preferred_element_type=jnp.float32
    )


def back_proj(grad_rows, weight):
    return lax.dot_general(
        grad_rows, weight, (((1,), (1,)), ((), ())), preferred_element_type=jnp.float32
    )


def reduce_steps(group, own, sibling, sent_as=bf16):
    moving, total = None, None
    for k in list(range(1, group.chips)) + [0]:
        pins = yield moving, total
        other = group.swap(sibling[k].astype(sent_as))
        if pins is not None:
            other, moving = after((other, moving), pins)
        total = own[k].astype(f32) + other.astype(f32)
        if moving is not None:
            total = total + moving.astype(f32)
        if k != 0:
            total = total.astype(sent_as)
            moving = group.onward(total)
    yield moving, total


def local_slots(routes_all, first, local):
    ids = first + lax.iota(jnp.int32, local)
    hot = jnp.any(routes_all[:, None, :, :] == ids[None, :, None, None], axis=2).astype(jnp.int32)
    return jnp.where(hot != 0, jnp.cumsum(hot, axis=2) - hot, -1)


def shards(
    tokens,
    segments,
    routes,
    gain_attn,
    w_query,
    w_key,
    w_value,
    w_output,
    rel_bias,
    gain_ffn,
    router,
    w_in,
    w_out,
    cotangent,
):
    group = Group()
    tok_rows, width = tokens.shape
    exp_local = w_in.shape[0]
    groups = group.size
    experts = exp_local * groups
    capacity = 2 * tok_rows * TOP // experts
    choose = routes[:, :, None] == lax.iota(jnp.int32, experts)[None, None, :]
    tally = jnp.pad(jnp.sum(choose.astype(f32), axis=(0, 1))[None], ((0, 7), (0, 128 - experts)))
    small = pack_small(gain_attn, gain_ffn, router, rel_bias, routes)
    stack_all, small_all, tally_all = gather_group(jnp.stack([w_query, w_key, w_value, w_output]), small, tally)
    query_full, key_full, value_full, output_full = [stack_all[m] for m in range(4)]
    gain_one, gain_two, table_full, router_t, routes_all = unpack_small(
        small_all, groups, gain_attn.shape[0], rel_bias.shape[0], rel_bias.shape[1], experts, tok_rows
    )
    router_full = router_t.T
    counts = jnp.sum(tally_all[:, 0, 0:experts], axis=0)
    first = (group.me * exp_local).astype(jnp.int32)
    slots_all = local_slots(routes_all, first, exp_local)

    kept_grad = jnp.where((segments != 0)[:, None], cotangent, jnp.zeros_like(cotangent))
    grad_ring = [kept_grad]
    for k in range(1, group.chips):
        grad_ring.append(group.onward(grad_ring[-1]))

    inputs = tokens.astype(f32)
    scale_one = rms_scale(inputs)
    normed_one = (inputs * scale_one * gain_one.astype(f32)).astype(bf16)
    normed_one = after(normed_one, grad_ring[1])
    query_rows = jnp.dot(normed_one, query_full, preferred_element_type=f32).astype(bf16)
    key_rows = jnp.dot(normed_one, key_full, preferred_element_type=f32).astype(bf16)
    value_rows = jnp.dot(normed_one, value_full, preferred_element_type=f32).astype(bf16)
    base = bias_base(table_full)
    context, lse = attend(query_rows, key_rows, value_rows, after(segments, slots_all), base)
    context = after(context, grad_ring[2])
    hidden_one = inputs + jnp.dot(context, output_full, preferred_element_type=f32)
    scale_two = rms_scale(hidden_one)
    normed_two = (hidden_one * scale_two * gain_two.astype(f32)).astype(bf16)

    kept = None
    results = []
    sibs = [group.swap(block) for block in grad_ring[:3]]
    ring = list(grad_ring)
    norm_ring = [normed_two]
    for k in range(group.chips):
        if k >= 3:
            sibs.append(group.swap(after(ring[k], results[k - 3][2])))
        norm_now = norm_ring[k]
        norm_sib = group.swap(norm_now)
        if k < group.chips - 1:
            moved = group.onward(norm_now)
        chip = group.source_chip(k)
        info = jnp.concatenate(
            [
                lax.dynamic_index_in_dim(rows, 2 * chip + core, 0, keepdims=False)
                for core in (group.core, 1 - group.core)
                for rows in (slots_all, routes_all)
            ],
            axis=0,
        )
        if k == 1:
            info = after(info, ring[3:])
        if k == group.chips - 1:
            back_own, back_sib = [r[2] for r in results], [r[3] for r in results]
            back_steps = reduce_steps(group, back_own, back_sib)
            next(back_steps)
            sent = back_steps.send(None)[1]
            info = after(info, sent)
        outs, kept = expert_block(
            k, group.chips, first.reshape(1), norm_now, norm_sib, ring[k], sibs[k],
            info, router_t, w_in, w_out, capacity, kept,
        )
        results.append(outs)
        if k == group.chips - 1:
            back_own.append(outs[2])
            back_sib.append(outs[3])
        if k < group.chips - 1:
            norm_ring.append(after(moved, outs[2]))

    act_all, dpre_all, x_all, dy_all = kept
    chips = group.chips
    for k in range(2, chips - 1):
        sent = back_steps.send(outs[2])[1]
    up_grad = jnp.einsum("ekd,ekf->edf", after(x_all, sent), dpre_all, preferred_element_type=f32).astype(bf16)
    sent = back_steps.send(up_grad)[1]
    up_share = lax.psum_scatter(after(up_grad, sent), "rep", scatter_dimension=1, tiled=True)
    down_grad = jnp.einsum("ekf,ekd->efd", act_all, after(dy_all, sent), preferred_element_type=f32).astype(bf16)
    back = back_steps.send(down_grad)[1]
    down_share = lax.psum_scatter(after(down_grad, back), "rep", scatter_dimension=1, tiled=True)

    y_steps = reduce_steps(group, [r[0] for r in results], [r[1] for r in results])
    next(y_steps)
    y_moving, sent = y_steps.send(back)
    back = after(back, sent)

    logits = jnp.dot(normed_two, router_full, preferred_element_type=f32)
    router_prob = jax.nn.softmax(logits, axis=-1)
    picked_prob = jnp.sum(jnp.where(choose, router_prob[:, None, :], 0.0), axis=-1)
    prob_sum = jnp.sum(picked_prob, axis=-1, keepdims=True)
    all_tokens = tok_rows * lax.axis_size("rep") * groups
    fraction = counts / (TOP * all_tokens)

    grad_out = kept_grad.astype(f32)
    grad_gate = unpack_dgate(back[tok_rows:], tok_rows).T
    grad_norm_two = back[0:tok_rows]
    grad_picked = grad_gate / prob_sum - jnp.sum(
        grad_gate * picked_prob, axis=-1, keepdims=True
    ) / (prob_sum * prob_sum)
    grad_router_prob = (
        jnp.sum(jnp.where(choose, grad_picked[:, :, None], 0.0), axis=1)
        + aux_weight * experts * fraction / all_tokens
    )
    grad_logits = (
        router_prob
        * (grad_router_prob - jnp.sum(router_prob * grad_router_prob, axis=-1, keepdims=True))
    ).astype(jnp.bfloat16)
    router_grad = outer_sum(normed_two, grad_logits)
    grad_norm_two = grad_norm_two + back_proj(grad_logits, router_full)
    gain_two_grad = jnp.sum(grad_norm_two * (hidden_one * scale_two), axis=0)
    scaled_two = grad_norm_two * gain_two.astype(jnp.float32)
    grad_hidden_one = (
        grad_out
        + scale_two * scaled_two
        - hidden_one * scale_two**3 * jnp.mean(scaled_two * hidden_one, axis=-1, keepdims=True)
    )
    grad_attn = grad_hidden_one.astype(jnp.bfloat16)
    output_grad = outer_sum(context, grad_attn)
    grad_context = back_proj(grad_attn, output_full).astype(jnp.bfloat16)
    grad_query_rows, grad_key_rows, grad_value_rows, near_grad, far_grad = attend_back(
        query_rows, key_rows, value_rows, segments, base, context, grad_context, lse
    )
    sent = None
    for k in range(2, chips - 1):
        y_moving, sent = y_steps.send(grad_query_rows)
    grad_query_rows, grad_key_rows, grad_value_rows = after((grad_query_rows, grad_key_rows, grad_value_rows), sent)
    query_grad = outer_sum(normed_one, grad_query_rows)
    key_grad = outer_sum(normed_one, grad_key_rows)
    value_grad = outer_sum(normed_one, grad_value_rows)
    grad_norm_one = (
        back_proj(grad_query_rows, query_full)
        + back_proj(grad_key_rows, key_full)
        + back_proj(grad_value_rows, value_full)
    )
    gain_one_grad = jnp.sum(grad_norm_one * (inputs * scale_one), axis=0)
    scaled_one = grad_norm_one * gain_one.astype(jnp.float32)
    grad_input = (
        grad_hidden_one
        + scale_one * scaled_one
        - inputs * scale_one**3 * jnp.mean(scaled_one * inputs, axis=-1, keepdims=True)
    )
    table_grad = table_back(near_grad, far_grad, table_full.shape[0])
    def shares(x, rows):
        x = x.reshape(x.shape[:-2] + (groups, rows, x.shape[-1]))
        def one(k, core):
            return lax.dynamic_index_in_dim(x, 2 * group.source_chip(k) + core, x.ndim - 3, keepdims=False)
        return [one(k, group.core) for k in range(chips)], [one(k, 1 - group.core) for k in range(chips)]

    rows = width // groups
    dense = jnp.stack([query_grad, key_grad, value_grad, output_grad]).astype(bf16)
    dense_steps = reduce_steps(group, *shares(dense, rows))

    def lanes(x):
        return jnp.pad(x, ((0, 0), (0, 0), (0, 128 - x.shape[2])))

    heads = table_grad.shape[1]
    bias_rows = table_grad.shape[0] // groups
    prob_row = jnp.broadcast_to(jnp.sum(router_prob, axis=0), (groups, 1, experts))
    small = jnp.concatenate([
        lanes(gain_one_grad.reshape(groups, 1, rows)), lanes(gain_two_grad.reshape(groups, 1, rows)),
        lanes(prob_row), lanes(table_grad.reshape(groups, bias_rows, heads)),
        lanes(jnp.transpose(router_grad.T.reshape(experts, groups, rows), (1, 0, 2))),
    ], axis=1)
    small = jnp.pad(small, ((0, 0), (0, -small.shape[1] % 8), (0, 0)))
    small_steps = reduce_steps(group, *shares(small.reshape(-1, 128), small.shape[1]), f32)
    next(dense_steps)
    next(small_steps)
    up_share, down_share = up_share.astype(f32), down_share.astype(f32)
    pins = y_moving
    for k in range(1, chips):
        dense_sum, small_sum = dense_steps.send(pins)[1], small_steps.send(pins)[1]
        pins = (up_share, grad_input) if k == 1 else None
    y_steps.send((dense_sum, small_sum))
    dense_sum, small_sum = dense_steps.send(None)[1], small_steps.send(None)[1]
    mixed = y_steps.send(dense_sum)[1]
    output = (hidden_one + mixed).astype(bf16)

    def over_rep(x):
        count = lax.axis_size("rep")
        return x.astype(f32), [lax.ppermute(x, "rep", [(i, i ^ k) for i in range(count)]) for k in range(1, count)]

    (dense, dense_moved), (small, small_moved) = over_rep(dense_sum.astype(bf16)), over_rep(small_sum)
    for got, also in zip(after(dense_moved, down_share), small_moved):
        dense, small = dense + got.astype(f32), small + also
    at = 3 + bias_rows
    balance_terms = experts * experts * fraction * (small[2, 0:experts] / all_tokens)
    loss = aux_weight / experts * jnp.sum(balance_terms)
    return (
        output,
        loss,
        balance_terms,
        grad_input,
        small[0, 0:rows],
        dense[0],
        dense[1],
        dense[2],
        dense[3],
        small[3:at, 0:heads],
        small[1, 0:rows],
        small[at:at + experts, 0:rows].T,
        up_share,
        down_share,
    )


def solution(mesh):
    return jax.shard_map(
        shards,
        mesh=mesh,
        in_specs=(
            P(("rep", "grp"), None),
            P(("rep", "grp")),
            P(("rep", "grp"), None),
            P("grp"),
            P("grp", None),
            P("grp", None),
            P("grp", None),
            P("grp", None),
            P("grp", None),
            P("grp"),
            P("grp", None),
            P("grp", None, None),
            P("grp", None, None),
            P(("rep", "grp"), None),
        ),
        out_specs=(
            P(("rep", "grp"), None),
            P(),
            P(),
            P(("rep", "grp"), None),
            P("grp"),
            P("grp", None),
            P("grp", None),
            P("grp", None),
            P("grp", None),
            P("grp", None),
            P("grp"),
            P("grp", None),
            P("grp", "rep", None),
            P("grp", "rep", None),
        ),
        check_vma=False,
    )
```

```python
from functools import partial

import jax
import jax.numpy as jnp
from jax import lax
from jax.experimental import pallas as pl
from jax.experimental.pallas import tpu as pltpu
from jax.sharding import PartitionSpec as P

TOP = 2
QB = 128
PAIR = 128
NEAR = 2 * QB
SPAN = 3 * QB
OUT_OF_DOC = -1e30
FAR_MARKS = (18, 20, 23, 26, 30, 34, 39, 45, 51, 58, 66, 76, 86, 98, 112)
norm_eps = 1e-06
aux_weight = 0.01
f32, bf16 = jnp.float32, jnp.bfloat16


def after(x, *earlier):
    return lax.optimization_barrier((x, earlier))[0]


def rms_scale(values):
    return lax.rsqrt(jnp.mean(values * values, axis=-1, keepdims=True) + norm_eps)


def bucket_of(distance):
    far_part = jnp.zeros_like(distance)
    for far_mark in FAR_MARKS:
        far_part = far_part + (distance >= far_mark).astype(jnp.int32)
    return jnp.minimum(distance, 16) + far_part


def band_hot(buckets):
    lane = lax.broadcasted_iota(jnp.int32, (8, SPAN), 1)
    row = lax.broadcasted_iota(jnp.int32, (8, SPAN), 0)
    turn = (lane - row + SPAN) % SPAN
    diff = jnp.where(turn < QB, turn, turn - SPAN) + QB
    bucket = bucket_of(jnp.maximum(diff, 0)).reshape(1, 8 * SPAN)
    return bucket == lax.iota(jnp.int32, buckets)[:, None]


def split_pair(rows, low_lanes):
    zero = jnp.zeros_like(rows)
    return jnp.concatenate(
        [jnp.where(low_lanes, rows, zero), jnp.where(low_lanes, zero, rows)], axis=0
    )


def fill_mask(seg_col, seg_row, mask):
    seq = mask.shape[0]
    for i in range(seq // QB):
        length = (i + 1) * QB
        sk = seg_col[0:length, :]
        sq = seg_row[:, i * QB:(i + 1) * QB]
        kp = lax.broadcasted_iota(jnp.int32, (length, QB), 0)
        qp = lax.broadcasted_iota(jnp.int32, (length, QB), 1) + i * QB
        ok = (sk == sq) & (kp <= qp) & ((sq != 0) | (kp == qp))
        mask[0:length, i * QB:(i + 1) * QB] = jnp.where(ok, 0.0, OUT_OF_DOC).astype(f32)


def fill_near(base, near):
    for head in range(2):
        rows = base[head]
        for a in range(NEAR // 8):
            turned = rows if a == 0 else pltpu.roll(rows, 8 * a, 1)
            near[8 * a:8 * a + 8, head * QB:(head + 1) * QB] = turned[:, 0:QB]


def scores_chunk(k, lo, hi, qcat, mask, near, i):
    s = lax.dot_general(k[lo:hi, :], qcat, (((1,), (1,)), ((), ())), preferred_element_type=f32)
    m = mask[lo:hi, i * QB:(i + 1) * QB]
    s = s + jnp.concatenate([m, m], axis=1)
    start = (i - 1) * QB
    if lo >= start:
        s = s + near[lo - start:hi - start, :]
    return s


def fwd_kernel(base, seg_col, seg_row, q, k, v, ctx, lse, mask, near, scores, probs, v_t):
    seq = q.shape[0]

    @pl.when(pl.program_id(0) == 0)
    def _():
        fill_mask(seg_col, seg_row, mask)

    fill_near(base, near)
    v_t[...] = v[...].T
    low_lanes = lax.broadcasted_iota(jnp.int32, (QB, PAIR), 1) < PAIR // 2
    scale = (PAIR // 2) ** -0.5
    for i in range(seq // QB):
        qs = slice(i * QB, (i + 1) * QB)
        qcat = split_pair(q[qs, :] * jnp.asarray(scale, bf16), low_lanes)
        top = None
        for c in range(i + 1):
            s = scores_chunk(k, c * QB, (c + 1) * QB, qcat, mask, near, i)
            scores[c * QB:(c + 1) * QB, :] = s
            here = jnp.max(s.reshape(QB // 8, 8, NEAR), axis=0)
            top = here if top is None else jnp.maximum(top, here)
        top = jnp.max(top, axis=0, keepdims=True)
        total = jnp.zeros((8, NEAR), f32)
        for c in range(i + 1):
            p = jnp.exp(scores[c * QB:(c + 1) * QB, :] - top)
            total = total + jnp.sum(p.reshape(QB // 8, 8, NEAR), axis=0)
            probs[c * QB:(c + 1) * QB, :] = p.astype(bf16)
        total = jnp.sum(total, axis=0, keepdims=True)
        length = (i + 1) * QB
        out = jnp.dot(v_t[:, 0:length], probs[0:length, :], preferred_element_type=f32) / total
        half = PAIR // 2
        both = jnp.concatenate([out[0:half, 0:QB], out[half:PAIR, QB:NEAR]], axis=0)
        ctx[qs, :] = both.T.astype(bf16)
        lse[0, i:i + 1, :] = top + jnp.log(total)


def attend(q, k, v, seg, base):
    seq, width = q.shape
    pairs = width // PAIR
    col = pl.BlockSpec((seq, PAIR), lambda h: (0, h))
    whole = lambda *shape: pl.BlockSpec(shape, lambda h: (0,) * len(shape))
    return pl.pallas_call(
        fwd_kernel,
        grid=(pairs,),
        in_specs=[pl.BlockSpec((2, 8, SPAN), lambda h: (h, 0, 0)), whole(seq, 1), whole(1, seq), col, col, col],
        out_specs=[col, pl.BlockSpec((1, seq // QB, NEAR), lambda h: (h, 0, 0))],
        out_shape=[
            jax.ShapeDtypeStruct((seq, width), bf16),
            jax.ShapeDtypeStruct((pairs, seq // QB, NEAR), f32),
        ],
        scratch_shapes=[
            pltpu.VMEM((seq, seq), f32),
            pltpu.VMEM((NEAR, NEAR), f32),
            pltpu.VMEM((seq, NEAR), f32),
            pltpu.VMEM((seq, NEAR), bf16),
            pltpu.VMEM((PAIR, seq), bf16),
        ],
        compiler_params=pltpu.CompilerParams(vmem_limit_bytes=32 * 1024 * 1024),
        cost_estimate=pl.CostEstimate(flops=1, bytes_accessed=1024, transcendentals=0),
        name="attend",
    )(base, seg.reshape(seq, 1), seg.reshape(1, seq), q, k, v)


def bwd_kernel(base, seg_col, seg_row, q, k, v, ctx, dctx, lse, dq, dk, dv, dnear, dfar,
               mask, near, ds_all, p_all, k_t, dk_sum, dv_sum, dnear_sum, dfar_sum):
    seq = q.shape[0]

    @pl.when(pl.program_id(0) == 0)
    def _():
        fill_mask(seg_col, seg_row, mask)

    fill_near(base, near)
    k_t[...] = k[...].T
    low_lanes = lax.broadcasted_iota(jnp.int32, (QB, PAIR), 1) < PAIR // 2
    half = PAIR // 2
    scale = half ** -0.5
    dnear_sum[...] = jnp.zeros_like(dnear_sum)
    dfar_sum[...] = jnp.zeros_like(dfar_sum)
    for i in reversed(range(seq // QB)):
        qs = slice(i * QB, (i + 1) * QB)
        length = (i + 1) * QB
        qcat = split_pair(q[qs, :] * jnp.asarray(scale, bf16), low_lanes)
        dcat = split_pair(dctx[qs, :], low_lanes)
        dots = (ctx[qs, :].astype(f32) * dctx[qs, :].astype(f32)).T
        centre = jnp.concatenate(
            [jnp.sum(dots[0:half], axis=0, keepdims=True), jnp.sum(dots[half:], axis=0, keepdims=True)], axis=1
        )
        norm = lse[0, i:i + 1, :]
        for c in range(i + 1):
            lo, hi = c * QB, (c + 1) * QB
            s = scores_chunk(k, lo, hi, qcat, mask, near, i)
            p = jnp.exp(s - norm)
            p_all[lo:hi, :] = p.astype(bf16)
            dp = lax.dot_general(v[lo:hi, :], dcat, (((1,), (1,)), ((), ())), preferred_element_type=f32)
            ds = p * (dp - centre)
            ds_all[lo:hi, :] = ds.astype(bf16)
            start = (i - 1) * QB
            if lo >= start:
                dnear_sum[lo - start:hi - start, :] += ds
            else:
                dfar_sum[...] += jnp.sum(ds.reshape(QB // 8, 8, NEAR), axis=0)
        out = jnp.dot(k_t[:, 0:length], ds_all[0:length, :], preferred_element_type=f32)
        both = jnp.concatenate([out[0:half, 0:QB], out[half:PAIR, QB:NEAR]], axis=0)
        dq[qs, :] = (both.T * scale).astype(bf16)
        dk_part = jnp.dot(ds_all[0:length, :], qcat, preferred_element_type=f32)
        dv_part = jnp.dot(p_all[0:length, :], dcat, preferred_element_type=f32)
        if i == seq // QB - 1:
            dk_sum[0:length, :] = dk_part
            dv_sum[0:length, :] = dv_part
        else:
            dk_sum[0:length, :] += dk_part
            dv_sum[0:length, :] += dv_part
    dk[...] = dk_sum[...].astype(bf16)
    dv[...] = dv_sum[...].astype(bf16)
    for head in range(2):
        total = jnp.zeros((8, SPAN), f32)
        for a in range(NEAR // 8):
            rows = dnear_sum[8 * a:8 * a + 8, head * QB:(head + 1) * QB]
            rows = jnp.concatenate([rows, jnp.zeros((8, SPAN - QB), f32)], axis=1)
            total = total + (rows if a == 0 else pltpu.roll(rows, SPAN - 8 * a, 1))
        dnear[head] = total
    dfar[0] = dfar_sum[...]


def attend_back(q, k, v, seg, base, ctx, dctx, lse):
    seq, width = q.shape
    pairs = width // PAIR
    col = pl.BlockSpec((seq, PAIR), lambda h: (0, h))
    band = pl.BlockSpec((2, 8, SPAN), lambda h: (h, 0, 0))
    whole = lambda *shape: pl.BlockSpec(shape, lambda h: (0,) * len(shape))
    rows = jax.ShapeDtypeStruct((seq, width), bf16)
    return pl.pallas_call(
        bwd_kernel,
        grid=(pairs,),
        in_specs=[band, whole(seq, 1), whole(1, seq), col, col, col, col, col,
                  pl.BlockSpec((1, seq // QB, NEAR), lambda h: (h, 0, 0))],
        out_specs=[col, col, col, band, pl.BlockSpec((1, 8, NEAR), lambda h: (h, 0, 0))],
        out_shape=[rows, rows, rows, jax.ShapeDtypeStruct((2 * pairs, 8, SPAN), f32),
                   jax.ShapeDtypeStruct((pairs, 8, NEAR), f32)],
        scratch_shapes=[
            pltpu.VMEM((seq, seq), f32),
            pltpu.VMEM((NEAR, NEAR), f32),
            pltpu.VMEM((seq, NEAR), bf16),
            pltpu.VMEM((seq, NEAR), bf16),
            pltpu.VMEM((PAIR, seq), bf16),
            pltpu.VMEM((seq, PAIR), f32),
            pltpu.VMEM((seq, PAIR), f32),
            pltpu.VMEM((NEAR, NEAR), f32),
            pltpu.VMEM((8, NEAR), f32),
        ],
        compiler_params=pltpu.CompilerParams(vmem_limit_bytes=40 * 1024 * 1024),
        cost_estimate=pl.CostEstimate(flops=1, bytes_accessed=1024, transcendentals=0),
        name="attend_back",
    )(base, seg.reshape(seq, 1), seg.reshape(1, seq), q, k, v, ctx, dctx, lse)


def bias_base(table):
    buckets, heads = table.shape
    hot = band_hot(buckets).astype(bf16)
    base = lax.dot_general(table, hot, (((0,), (0,)), ((), ())), preferred_element_type=f32)
    last = table[buckets - 1].astype(f32)
    return base.reshape(heads, 8, SPAN) - last[:, None, None]


def table_back(dnear, dfar, buckets):
    heads = dnear.shape[0]
    hot = band_hot(buckets).astype(f32)
    grad = lax.dot_general(hot, dnear.reshape(heads, 8 * SPAN), (((1,), (1,)), ((), ())),
                           preferred_element_type=f32, precision=lax.Precision.HIGHEST)
    far = jnp.sum(dfar.reshape(heads // 2, 8, 2, QB), axis=(1, 3)).reshape(1, heads)
    last = (lax.iota(jnp.int32, buckets) == buckets - 1)[:, None]
    return grad + jnp.where(last, far, 0.0)


def gelu_and_slope(u):
    root = (2.0 / jnp.pi) ** 0.5
    square = u * u
    bent = jnp.tanh(u * (root + (root * 0.044715) * square))
    rise = 0.5 + 0.5 * bent
    slope = rise + (0.5 * u) * (1.0 - bent * bent) * (root + (root * 3 * 0.044715) * square)
    return u * rise, slope


def expert_kernel(first, n_a, n_b, g_a, g_b, info, router_t, w_in, w_out, *rest):
    (y_a, y_b, r_a, r_b, act_out, dpre_out, x_out, dy_out,
     hot, x_s, g_s, dy_s, gate_s, y_sum, d_sum, y_all, d_all, dgate_c) = rest[-18:]
    e, f = pl.program_id(0), pl.program_id(1)
    rows, width = n_a.shape
    cap = x_s.shape[0] // 2
    expert = first[0] + e
    sources = ((n_a, g_a), (n_b, g_b))

    @pl.when((e == 0) & (f == 0))
    def _():
        dgate_c[...] = jnp.zeros_like(dgate_c)

    @pl.when(f == 0)
    def _():
        for s, (n_ref, g_ref) in enumerate(sources):
            logits = lax.dot_general(router_t[...], n_ref[...], (((1,), (1,)), ((), ())), preferred_element_type=f32)
            ids = lax.broadcasted_iota(jnp.int32, logits.shape, 0)
            power = jnp.exp(logits - jnp.max(logits, axis=0, keepdims=True))
            prob = power / jnp.sum(power, axis=0, keepdims=True)
            chosen = (ids == info[4 * s + 2:4 * s + 3, :]) | (ids == info[4 * s + 3:4 * s + 4, :])
            both = jnp.sum(jnp.where(chosen, prob, 0.0), axis=0, keepdims=True)
            gate_row = jnp.sum(jnp.where(ids == expert, prob, 0.0), axis=0, keepdims=True) / both
            slot_row = jnp.where(e == 0, info[4 * s:4 * s + 1, :], info[4 * s + 1:4 * s + 2, :])
            match = slot_row == lax.broadcasted_iota(jnp.int32, (cap, rows), 0)
            one_hot = jnp.where(match, 1.0, 0.0).astype(bf16)
            part = slice(s * cap, (s + 1) * cap)
            gate_s[part, :] = jnp.sum(jnp.where(match, gate_row, 0.0), axis=1, keepdims=True)
            hot[s, pl.ds(pl.multiple_of(e * cap, cap), cap), :] = one_hot
            x_s[part, :] = jnp.dot(one_hot, n_ref[...], preferred_element_type=f32).astype(bf16)
            g_rows = jnp.dot(one_hot, g_ref[...], preferred_element_type=f32)
            g_s[part, :] = g_rows.astype(bf16)
            dy_s[part, :] = (gate_s[part, :] * g_rows).astype(bf16)
        y_sum[...] = jnp.zeros_like(y_sum)
        d_sum[...] = jnp.zeros_like(d_sum)
        x_out[0] = x_s[...]
        dy_out[0] = dy_s[...]

    pre = jnp.dot(x_s[...], w_in[0], preferred_element_type=f32)
    dact = lax.dot_general(dy_s[...], w_out[0], (((1,), (1,)), ((), ())), preferred_element_type=f32)
    act, slope = gelu_and_slope(pre)
    act_out[0] = act.astype(bf16)
    dpre_out[0] = (dact * slope).astype(bf16)
    y_sum[...] += jnp.dot(act_out[0], w_out[0], preferred_element_type=f32)
    d_sum[...] += lax.dot_general(dpre_out[0], w_in[0], (((1,), (1,)), ((), ())), preferred_element_type=f32)

    @pl.when(f == pl.num_programs(1) - 1)
    def _():
        y_rows = y_sum[...].astype(bf16).astype(f32)
        dgate = jnp.sum(y_rows * g_s[...].astype(f32), axis=1, keepdims=True)
        y_rows = (gate_s[...] * y_rows).astype(bf16)
        d_rows = d_sum[...].astype(bf16)
        for s in range(2):
            part = slice(s * cap, (s + 1) * cap)
            here = pl.ds(pl.multiple_of(e * cap, cap), cap)
            y_all[s, here, :] = y_rows[part]
            d_all[s, here, :] = d_rows[part]
            slot_row = jnp.where(e == 0, info[4 * s:4 * s + 1, :], info[4 * s + 1:4 * s + 2, :])
            match = slot_row == lax.broadcasted_iota(jnp.int32, (cap, rows), 0)
            row = jnp.sum(jnp.where(match, dgate[part], 0.0), axis=0, keepdims=True)
            for c in range(TOP):
                routed = info[4 * s + 2 + c:4 * s + 3 + c, :] == expert
                dgate_c[TOP * s + c:TOP * s + c + 1, :] += jnp.where(routed, row, 0.0)

    @pl.when((e == pl.num_programs(0) - 1) & (f == pl.num_programs(1) - 1))
    def _():
        turn = (((0,), (0,)), ((), ()))
        for s, (y_ref, r_ref) in enumerate(((y_a, r_a), (y_b, r_b))):
            y_ref[...] = lax.dot_general(hot[s], y_all[s], turn, preferred_element_type=f32).astype(bf16)
            r_ref[0:rows, :] = lax.dot_general(hot[s], d_all[s], turn, preferred_element_type=f32).astype(bf16)
            value = dgate_c[TOP * s:TOP * s + TOP, :]
            high = value.astype(bf16)
            value = value - high.astype(f32)
            middle = value.astype(bf16)
            low = (value - middle.astype(f32)).astype(bf16)
            pieces = jnp.concatenate([high.astype(f32), middle.astype(f32), low.astype(f32), jnp.zeros((2, rows), f32)], axis=0)
            over = jnp.concatenate([pieces[:, width:], jnp.zeros((8, 2 * width - rows), f32)], axis=1)
            r_ref[rows:rows + 16, :] = jnp.concatenate([pieces[:, 0:width], over], axis=0).astype(bf16)


def unpack_dgate(tail, rows):
    tail = tail.astype(f32)
    pieces = jnp.concatenate([tail[0:8], tail[8:16]], axis=1)[:, 0:rows]
    return pieces[0:2] + pieces[2:4] + pieces[4:6]


def expert_block(k, blocks, first, n_a, n_b, g_a, g_b, info, router_t, w_in, w_out, cap, kept):
    rows, width = n_a.shape
    local, _, hidden = w_in.shape
    part = 768 if hidden % 768 == 0 else hidden
    once = pl.Buffered(1)
    whole = lambda *shape: pl.BlockSpec(shape, lambda e, f: (0,) * len(shape), pipeline_mode=once)
    wide = pl.BlockSpec((1, 2 * cap, part), lambda e, f: (e, k, f))
    slim = pl.BlockSpec((1, 2 * cap, width), lambda e, f: (e, k, 0))
    slots = blocks * 2 * cap
    shapes = [
        jax.ShapeDtypeStruct((rows, width), bf16), jax.ShapeDtypeStruct((rows, width), bf16),
        jax.ShapeDtypeStruct((rows + 16, width), bf16), jax.ShapeDtypeStruct((rows + 16, width), bf16),
        jax.ShapeDtypeStruct((local, slots, hidden), bf16), jax.ShapeDtypeStruct((local, slots, hidden), bf16),
        jax.ShapeDtypeStruct((local, slots, width), bf16), jax.ShapeDtypeStruct((local, slots, width), bf16),
    ]
    in_specs = [
        pl.BlockSpec(memory_space=pltpu.SMEM), whole(rows, width), whole(rows, width), whole(rows, width), whole(rows, width),
        whole(8, rows), whole(*router_t.shape),
        pl.BlockSpec((1, width, part), lambda e, f: (e, 0, f)), pl.BlockSpec((1, part, width), lambda e, f: (e, f, 0)),
    ]
    args = [first, n_a, n_b, g_a, g_b, info, router_t, w_in, w_out]
    alias = {}
    if kept is not None:
        alias = {len(args) + i: 4 + i for i in range(4)}
        in_specs += [pl.BlockSpec(memory_space=pl.ANY)] * 4
        args += list(kept)
    out = pl.pallas_call(
        expert_kernel,
        grid=(local, hidden // part),
        in_specs=in_specs,
        out_specs=[whole(rows, width), whole(rows, width), whole(rows + 16, width), whole(rows + 16, width), wide, wide, slim, slim],
        out_shape=shapes,
        scratch_shapes=[
            pltpu.VMEM((2, local * cap, rows), bf16),
            pltpu.VMEM((2 * cap, width), bf16), pltpu.VMEM((2 * cap, width), bf16), pltpu.VMEM((2 * cap, width), bf16),
            pltpu.VMEM((2 * cap, 1), f32),
            pltpu.VMEM((2 * cap, width), f32), pltpu.VMEM((2 * cap, width), f32),
            pltpu.VMEM((2, local * cap, width), bf16), pltpu.VMEM((2, local * cap, width), bf16),
            pltpu.VMEM((8, rows), f32),
        ],
        input_output_aliases=alias,
        compiler_params=pltpu.CompilerParams(vmem_limit_bytes=48 * 1024 * 1024),
        cost_estimate=pl.CostEstimate(flops=2 * local * cap * (8 * width * hidden + 8 * width * rows), bytes_accessed=60 * 1024 * 1024, transcendentals=2 * local * cap * hidden),
        name="expert_block",
    )(*args)
    return out[:4], out[4:]


def chip_ring(chips):
    return [0] + list(range(1, chips, 2)) + [z for z in range(chips - 1, 0, -1) if z % 2 == 0]


class Group:
    def __init__(self):
        self.size = lax.axis_size("grp")
        self.chips = self.size // 2
        self.order = chip_ring(self.chips)
        me = lax.axis_index("grp")
        self.me, self.chip, self.core = me, me // 2, me % 2

    def onward(self, x):
        pairs = []
        for i, z in enumerate(self.order):
            after = self.order[(i + 1) % self.chips]
            pairs += [(2 * z, 2 * after), (2 * z + 1, 2 * after + 1)]
        return lax.ppermute(x, "grp", pairs)

    def backward(self, x):
        pairs = []
        for i, z in enumerate(self.order):
            before = self.order[(i - 1) % self.chips]
            pairs += [(2 * z, 2 * before), (2 * z + 1, 2 * before + 1)]
        return lax.ppermute(x, "grp", pairs)

    def swap(self, x):
        return lax.ppermute(x, "grp", [(i, i ^ 1) for i in range(self.size)])

    def source_chip(self, k):
        table = [0] * self.chips
        for i, z in enumerate(self.order):
            table[z] = self.order[(i - k) % self.chips]
        return jnp.asarray(table, jnp.int32)[self.chip]


def pick_constant(table, index):
    value = jnp.int32(table[0])
    for i in range(1, len(table)):
        value = jnp.where(index == i, jnp.int32(table[i]), value)
    return value


def gather_kernel(chips, reps, stack, small, tally, stack_all, small_all, tally_all,
                  own_sem, ring_send, ring_recv, core_send, core_recv, own_send, own_recv,
                  plane_send, plane_recv, cross_send, cross_recv, rep_send, rep_recv, tally_in, tally_sum, tally_vmem):
    order = chip_ring(chips)
    mats, rows = stack.shape[0], stack.shape[1]
    rep, me = lax.axis_index("rep"), lax.axis_index("grp")
    chip, core = me // 2, me % 2
    mine = lax.rem(rep, mats)
    after_z, before_z = [0] * chips, [0] * chips
    for i, z in enumerate(order):
        after_z[z], before_z[z] = order[(i + 1) % chips], order[(i - 1) % chips]
    onward = 2 * pick_constant(after_z, chip) + core
    before = 2 * pick_constant(before_z, chip) + core
    sibling = 2 * chip + 1 - core
    mesh_id = pl.DeviceIdType.MESH
    plane = [(rep - mine) + lax.rem(mine + j, mats) for j in range(1, mats)]

    barrier = pltpu.get_barrier_semaphore()
    peers = [(rep, onward), (rep, before), (rep, sibling)] + [(lax.rem(rep + k, reps), me) for k in range(1, reps)]
    for peer in peers:
        pl.semaphore_signal(barrier, inc=1, device_id=peer, device_id_type=mesh_id)
    pl.semaphore_wait(barrier, len(peers))

    def remote(src, dst, send, recv, target):
        return pltpu.make_async_remote_copy(
            src_ref=src, dst_ref=dst, send_sem=send, recv_sem=recv, device_id=target, device_id_type=mesh_id
        )

    def owner_of(k, which_core):
        source = [0] * chips
        for i, z in enumerate(order):
            source[z] = order[(i - k) % chips]
        return 2 * pick_constant(source, chip) + which_core

    def shard(mat, owner):
        return stack_all.at[mat, pl.ds(pl.multiple_of(owner * rows, rows), rows), :]

    def places(k, which_core):
        owner = owner_of(k, which_core)
        return [shard(mine, owner), small_all.at[owner], tally_all.at[owner]]

    def matrix(j):
        return lax.rem(mine + j, mats)

    sent = []

    def start(copy):
        copy.start()
        sent.append(copy)
        return copy

    tallies = [
        start(remote(tally, tally_in.at[k - 1], rep_send.at[k - 1], rep_recv.at[k - 1], (lax.rem(rep + k, reps), me)))
        for k in range(1, reps)
    ]
    own = [
        pltpu.make_async_copy(stack, stack_all.at[:, pl.ds(pl.multiple_of(me * rows, rows), rows), :], own_sem.at[0]),
        pltpu.make_async_copy(small, small_all.at[me], own_sem.at[1]),
        pltpu.make_async_copy(tally, tally_vmem, own_sem.at[2]),
    ]
    for copy in own:
        copy.start()
    here = places(0, core)
    moved = [
        start(remote(stack.at[mine], here[0], ring_send.at[0, 0], ring_recv.at[0, 0], (rep, onward))),
        start(remote(small, here[1], ring_send.at[0, 1], ring_recv.at[0, 1], (rep, onward))),
    ]
    everywhere = stack_all.at[:, pl.ds(pl.multiple_of(me * rows, rows), rows), :]
    start(remote(small, here[1], core_send.at[0, 1], core_recv.at[0, 1], (rep, sibling)))
    start(remote(stack, everywhere, own_send, own_recv, (rep, sibling)))
    own[2].wait()
    total = tally_vmem[...]
    for k, copy in enumerate(tallies):
        copy.wait_recv()
        total = total + tally_in[k]
    tally_sum[...] = total
    keep = pltpu.make_async_copy(tally_sum, here[2], own_sem.at[3])
    keep.start()
    own = [own[0], own[1], keep]
    moved.append(start(remote(tally_sum, here[2], ring_send.at[0, 2], ring_recv.at[0, 2], (rep, onward))))
    start(remote(tally_sum, here[2], core_send.at[0, 2], core_recv.at[0, 2], (rep, sibling)))

    def pass_across(k):
        for j in range(1, mats):
            block = shard(matrix(j), owner_of(k, core))
            remote(block, block, plane_send.at[k, j - 1], plane_recv.at[k, mats - 1 - j], (plane[j - 1], me)).wait_recv()
            start(remote(block, block, cross_send.at[k, mats - 1 - j], cross_recv.at[k, j - 1], (rep, sibling)))

    for k in range(1, chips):
        here = places(k, core)
        for a in range(3):
            moved[a].wait_recv()
            if k < chips - 1:
                moved[a] = start(remote(here[a], here[a], ring_send.at[k, a], ring_recv.at[k, a], (rep, onward)))
            if a == 0:
                for j in range(1, mats):
                    start(remote(here[0], here[0], plane_send.at[k, j - 1], plane_recv.at[k, j - 1], (plane[j - 1], me)))
            start(remote(here[a], here[a], core_send.at[k, a], core_recv.at[k, a], (rep, sibling)))
        if k > 1:
            pass_across(k - 1)
    pass_across(chips - 1)
    for copy in sent:
        copy.wait_send()
    for copy in own:
        copy.wait()
    other = stack_all.at[:, pl.ds(pl.multiple_of(sibling * rows, rows), rows), :]
    remote(stack, other, own_send, own_recv, (rep, sibling)).wait_recv()
    for k in range(chips):
        there = places(k, 1 - core)
        for a in range(3):
            if a > 0 or k > 0:
                remote(there[a], there[a], core_send.at[k, a], core_recv.at[k, a], (rep, sibling)).wait_recv()
        if k > 0:
            for j in range(1, mats):
                block = shard(matrix(j), owner_of(k, 1 - core))
                remote(block, block, cross_send.at[k, j - 1], cross_recv.at[k, j - 1], (rep, sibling)).wait_recv()


def gather_group(stack, small, tally):
    size, reps = lax.axis_size("grp"), lax.axis_size("rep")
    chips = size // 2
    mats, rows, width = stack.shape
    hbm = pl.BlockSpec(memory_space=pl.ANY)
    dma = pltpu.SemaphoreType.DMA
    return pl.pallas_call(
        partial(gather_kernel, chips, reps),
        in_specs=[hbm] * 3,
        out_specs=[hbm] * 3,
        out_shape=[
            jax.ShapeDtypeStruct((mats, size * rows, width), stack.dtype),
            jax.ShapeDtypeStruct((size,) + small.shape, small.dtype),
            jax.ShapeDtypeStruct((size,) + tally.shape, f32),
        ],
        scratch_shapes=[
            dma((4,)), dma((chips, 3)), dma((chips, 3)), dma((chips, 3)), dma((chips, 3)), dma, dma,
            dma((chips, mats - 1)), dma((chips, mats - 1)), dma((chips, mats - 1)), dma((chips, mats - 1)),
            dma((reps,)), dma((reps,)),
            pltpu.VMEM((reps - 1,) + tally.shape, f32), pltpu.VMEM(tally.shape, f32), pltpu.VMEM(tally.shape, f32),
        ],
        compiler_params=pltpu.CompilerParams(collective_id=0, has_side_effects=True),
        cost_estimate=pl.CostEstimate(flops=0, bytes_accessed=16 * 1024 * 1024, transcendentals=0),
        name="gather_group",
    )(stack, small, tally)


def pack_small(gain_attn, gain_ffn, router, rel_bias, routes):
    def lanes(x):
        return jnp.pad(x, ((0, 0), (0, 128 - x.shape[1])))

    rows = jnp.concatenate([
        lanes(gain_attn[None]), lanes(gain_ffn[None]), lanes(rel_bias), lanes(router.T),
        routes.T.astype(bf16).reshape(-1, 128),
    ], axis=0)
    return jnp.pad(rows, ((0, -rows.shape[0] % 16), (0, 0)))


def unpack_small(packed, size, shard, bias_rows, heads, experts, tokens):
    blocks = packed.reshape(size, -1, 128)
    gain_one = blocks[:, 0, 0:shard].reshape(-1)
    gain_two = blocks[:, 1, 0:shard].reshape(-1)
    at = 2 + bias_rows
    table = blocks[:, 2:at, 0:heads].reshape(-1, heads)
    router_t = jnp.transpose(blocks[:, at:at + experts, 0:shard], (1, 0, 2)).reshape(experts, -1)
    at += experts
    routes = blocks[:, at:at + TOP * tokens // 128].reshape(size, TOP, tokens).astype(jnp.int32)
    return gain_one, gain_two, table, router_t, routes


def outer_sum(left_rows, right_rows):
    return lax.dot_general(
        left_rows, right_rows, (((0,), (0,)), ((), ())), preferred_element_type=jnp.float32
    )


def back_proj(grad_rows, weight):
    return lax.dot_general(
        grad_rows, weight, (((1,), (1,)), ((), ())), preferred_element_type=jnp.float32
    )


def reduce_steps(group, own, sibling, sent_as=bf16):
    moving, total = None, None
    for k in list(range(1, group.chips)) + [0]:
        pins = yield moving, total
        other = group.swap(sibling[k].astype(sent_as))
        if pins is not None:
            other, moving = after((other, moving), pins)
        total = own[k].astype(f32) + other.astype(f32)
        if moving is not None:
            total = total + moving.astype(f32)
        if k != 0:
            total = total.astype(sent_as)
            moving = group.onward(total)
    yield moving, total


def reduce_both_ways(group, own, sibling):
    half = group.chips // 2
    ahead, behind, total = None, None, None
    for k in list(range(half - 1, 0, -1)) + list(range(half, group.chips)) + [0]:
        pins = yield ahead, behind, total
        other = group.swap(sibling[k])
        if k >= half:
            other, ahead = after((other, ahead), pins)
            arrived = [ahead]
        elif k > 0:
            other, behind = after((other, behind), pins)
            arrived = [behind]
        else:
            other, ahead, behind = after((other, ahead, behind), pins)
            arrived = [ahead, behind]
        total = own[k].astype(f32) + other.astype(f32)
        for block in arrived:
            if block is not None:
                total = total + block.astype(f32)
        if k > 0:
            total = total.astype(bf16)
        if k >= half:
            ahead = group.onward(total)
        elif k > 0:
            behind = group.backward(total)
    yield ahead, behind, total


def local_slots(routes_all, first, local):
    ids = first + lax.iota(jnp.int32, local)
    hot = jnp.any(routes_all[:, None, :, :] == ids[None, :, None, None], axis=2).astype(jnp.int32)
    return jnp.where(hot != 0, jnp.cumsum(hot, axis=2) - hot, -1)


def shards(
    tokens,
    segments,
    routes,
    gain_attn,
    w_query,
    w_key,
    w_value,
    w_output,
    rel_bias,
    gain_ffn,
    router,
    w_in,
    w_out,
    cotangent,
):
    group = Group()
    tok_rows, width = tokens.shape
    exp_local = w_in.shape[0]
    groups = group.size
    experts = exp_local * groups
    capacity = 2 * tok_rows * TOP // experts
    choose = routes[:, :, None] == lax.iota(jnp.int32, experts)[None, None, :]
    tally = jnp.pad(jnp.sum(choose.astype(f32), axis=(0, 1))[None], ((0, 7), (0, 128 - experts)))
    small = pack_small(gain_attn, gain_ffn, router, rel_bias, routes)
    stack_all, small_all, tally_all = gather_group(jnp.stack([w_query, w_key, w_value, w_output]), small, tally)
    query_full, key_full, value_full, output_full = [stack_all[m] for m in range(4)]
    gain_one, gain_two, table_full, router_t, routes_all = unpack_small(
        small_all, groups, gain_attn.shape[0], rel_bias.shape[0], rel_bias.shape[1], experts, tok_rows
    )
    router_full = router_t.T
    counts = jnp.sum(tally_all[:, 0, 0:experts], axis=0)
    first = (group.me * exp_local).astype(jnp.int32)

    kept_grad = jnp.where((segments != 0)[:, None], cotangent, jnp.zeros_like(cotangent))
    grad_ring = [kept_grad]
    for k in range(1, group.chips - 1):
        grad_ring.append(group.onward(grad_ring[-1]))
    grad_ring.append(group.backward(after(kept_grad, small_all)))
    slots_all = local_slots(after(routes_all, grad_ring[1]), first, exp_local)

    inputs = tokens.astype(f32)
    scale_one = rms_scale(inputs)
    normed_one = (inputs * scale_one * gain_one.astype(f32)).astype(bf16)
    normed_one = after(normed_one, grad_ring[1])
    query_rows = jnp.dot(normed_one, query_full, preferred_element_type=f32).astype(bf16)
    key_rows = jnp.dot(normed_one, key_full, preferred_element_type=f32).astype(bf16)
    value_rows = jnp.dot(normed_one, value_full, preferred_element_type=f32).astype(bf16)
    base = bias_base(table_full)
    context, lse = attend(query_rows, key_rows, value_rows, after(segments, slots_all), base)
    context = after(context, grad_ring[-1])
    hidden_one = inputs + jnp.dot(context, output_full, preferred_element_type=f32)
    scale_two = rms_scale(hidden_one)
    normed_two = (hidden_one * scale_two * gain_two.astype(f32)).astype(bf16)

    kept = None
    results = []
    sibs = [group.swap(block) for block in grad_ring[:3]]
    ring = list(grad_ring)
    norm_ring = [normed_two]
    for k in range(group.chips):
        if k >= 3:
            sibs.append(group.swap(after(ring[k], results[k - 3][2])))
        norm_now = norm_ring[k]
        norm_sib = group.swap(norm_now)
        if k < group.chips - 1:
            moved = group.onward(norm_now)
        chip = group.source_chip(k)
        info = jnp.concatenate(
            [
                lax.dynamic_index_in_dim(rows, 2 * chip + core, 0, keepdims=False)
                for core in (group.core, 1 - group.core)
                for rows in (slots_all, routes_all)
            ],
            axis=0,
        )
        if k == 0:
            info = after(info, ring[2])
        if k == group.chips - 1:
            back_own, back_sib = [r[2] for r in results], [r[3] for r in results]
            back_steps = reduce_steps(group, back_own, back_sib)
            next(back_steps)
            sent = back_steps.send(None)[1]
            info = after(info, sent)
        outs, kept = expert_block(
            k, group.chips, first.reshape(1), norm_now, norm_sib, ring[k], sibs[k],
            info, router_t, w_in, w_out, capacity, kept,
        )
        results.append(outs)
        if k == group.chips - 1:
            back_own.append(outs[2])
            back_sib.append(outs[3])
        if k < group.chips - 1:
            norm_ring.append(after(moved, outs[2]))

    act_all, dpre_all, x_all, dy_all = kept
    chips = group.chips
    for k in range(2, chips - 1):
        sent = back_steps.send(outs[2])[1]
    up_grad = jnp.einsum("ekd,ekf->edf", after(x_all, sent), dpre_all, preferred_element_type=f32).astype(bf16)
    sent = back_steps.send(up_grad)[1]
    up_share = lax.psum_scatter(after(up_grad, sent), "rep", scatter_dimension=1, tiled=True)
    down_grad = jnp.einsum("ekf,ekd->efd", act_all, after(dy_all, sent), preferred_element_type=f32).astype(bf16)

    y_steps = reduce_both_ways(group, [r[0] for r in results], [r[1] for r in results])
    next(y_steps)
    sums = []
    for k in range(chips - 2):
        y_ahead, y_behind, sent = y_steps.send(down_grad)
        sums.append(sent)
    back = back_steps.send((down_grad, sums))[1]
    down_share = lax.psum_scatter(after(down_grad, back), "rep", scatter_dimension=1, tiled=True)

    logits = jnp.dot(normed_two, router_full, preferred_element_type=f32)
    router_prob = jax.nn.softmax(logits, axis=-1)
    picked_prob = jnp.sum(jnp.where(choose, router_prob[:, None, :], 0.0), axis=-1)
    prob_sum = jnp.sum(picked_prob, axis=-1, keepdims=True)
    all_tokens = tok_rows * lax.axis_size("rep") * groups
    fraction = counts / (TOP * all_tokens)

    grad_out = kept_grad.astype(f32)
    grad_gate = unpack_dgate(back[tok_rows:], tok_rows).T
    grad_norm_two = back[0:tok_rows]
    grad_picked = grad_gate / prob_sum - jnp.sum(
        grad_gate * picked_prob, axis=-1, keepdims=True
    ) / (prob_sum * prob_sum)
    grad_router_prob = (
        jnp.sum(jnp.where(choose, grad_picked[:, :, None], 0.0), axis=1)
        + aux_weight * experts * fraction / all_tokens
    )
    grad_logits = (
        router_prob
        * (grad_router_prob - jnp.sum(router_prob * grad_router_prob, axis=-1, keepdims=True))
    ).astype(jnp.bfloat16)
    router_grad = outer_sum(normed_two, grad_logits)
    grad_norm_two = grad_norm_two + back_proj(grad_logits, router_full)
    gain_two_grad = jnp.sum(grad_norm_two * (hidden_one * scale_two), axis=0)
    scaled_two = grad_norm_two * gain_two.astype(jnp.float32)
    grad_hidden_one = (
        grad_out
        + scale_two * scaled_two
        - hidden_one * scale_two**3 * jnp.mean(scaled_two * hidden_one, axis=-1, keepdims=True)
    )
    grad_attn = grad_hidden_one.astype(jnp.bfloat16)
    output_grad = outer_sum(context, grad_attn)
    grad_context = back_proj(grad_attn, output_full).astype(jnp.bfloat16)
    grad_query_rows, grad_key_rows, grad_value_rows, near_grad, far_grad = attend_back(
        query_rows, key_rows, value_rows, segments, base, context, grad_context, lse
    )
    grad_query_rows, grad_key_rows, grad_value_rows = after((grad_query_rows, grad_key_rows, grad_value_rows), y_behind)
    query_grad = outer_sum(normed_one, grad_query_rows)
    key_grad = outer_sum(normed_one, grad_key_rows)
    value_grad = outer_sum(normed_one, grad_value_rows)
    grad_norm_one = (
        back_proj(grad_query_rows, query_full)
        + back_proj(grad_key_rows, key_full)
        + back_proj(grad_value_rows, value_full)
    )
    gain_one_grad = jnp.sum(grad_norm_one * (inputs * scale_one), axis=0)
    scaled_one = grad_norm_one * gain_one.astype(jnp.float32)
    grad_input = (
        grad_hidden_one
        + scale_one * scaled_one
        - inputs * scale_one**3 * jnp.mean(scaled_one * inputs, axis=-1, keepdims=True)
    )
    table_grad = table_back(near_grad, far_grad, table_full.shape[0])
    def shares(x, rows):
        x = x.reshape(x.shape[:-2] + (groups, rows, x.shape[-1]))
        def one(k, core):
            return lax.dynamic_index_in_dim(x, 2 * group.source_chip(k) + core, x.ndim - 3, keepdims=False)
        return [one(k, group.core) for k in range(chips)], [one(k, 1 - group.core) for k in range(chips)]

    rows = width // groups
    dense = jnp.stack([query_grad, key_grad, value_grad, output_grad]).astype(bf16)
    dense_steps = reduce_steps(group, *shares(dense, rows))

    def lanes(x):
        return jnp.pad(x, ((0, 0), (0, 0), (0, 128 - x.shape[2])))

    heads = table_grad.shape[1]
    bias_rows = table_grad.shape[0] // groups
    prob_row = jnp.broadcast_to(jnp.sum(router_prob, axis=0), (groups, 1, experts))
    small = jnp.concatenate([
        lanes(gain_one_grad.reshape(groups, 1, rows)), lanes(gain_two_grad.reshape(groups, 1, rows)),
        lanes(prob_row), lanes(table_grad.reshape(groups, bias_rows, heads)),
        lanes(jnp.transpose(router_grad.T.reshape(experts, groups, rows), (1, 0, 2))),
    ], axis=1)
    small = jnp.pad(small, ((0, 0), (0, -small.shape[1] % 8), (0, 0)))
    small_steps = reduce_steps(group, *shares(small.reshape(-1, 128), small.shape[1]), f32)
    next(dense_steps)
    next(small_steps)
    up_share, down_share = up_share.astype(f32), down_share.astype(f32)
    pins = y_ahead
    for k in range(1, chips):
        dense_sum = dense_steps.send(pins)[1]
        small_sum = small_steps.send(dense_sum)[1]
        pins = (up_share, grad_input) if k == 1 else None
    y_steps.send(dense_sum)
    dense_sum = dense_steps.send(None)[1]
    small_sum = small_steps.send(dense_sum)[1]
    mixed = y_steps.send(dense_sum)[2]
    output = (hidden_one + mixed).astype(bf16)

    def over_rep(x):
        count = lax.axis_size("rep")
        return x.astype(f32), [lax.ppermute(x, "rep", [(i, i ^ k) for i in range(count)]) for k in range(1, count)]

    (dense, dense_moved), (small, small_moved) = over_rep(dense_sum.astype(bf16)), over_rep(small_sum)
    for got, also in zip(after(dense_moved, down_share), small_moved):
        dense, small = dense + got.astype(f32), small + also
    at = 3 + bias_rows
    balance_terms = experts * experts * fraction * (small[2, 0:experts] / all_tokens)
    loss = aux_weight / experts * jnp.sum(balance_terms)
    return (
        output,
        loss,
        balance_terms,
        grad_input,
        small[0, 0:rows],
        dense[0],
        dense[1],
        dense[2],
        dense[3],
        small[3:at, 0:heads],
        small[1, 0:rows],
        small[at:at + experts, 0:rows].T,
        up_share,
        down_share,
    )


def solution(mesh):
    return jax.shard_map(
        shards,
        mesh=mesh,
        in_specs=(
            P(("rep", "grp"), None),
            P(("rep", "grp")),
            P(("rep", "grp"), None),
            P("grp"),
            P("grp", None),
            P("grp", None),
            P("grp", None),
            P("grp", None),
            P("grp", None),
            P("grp"),
            P("grp", None),
            P("grp", None, None),
            P("grp", None, None),
            P(("rep", "grp"), None),
        ),
        out_specs=(
            P(("rep", "grp"), None),
            P(),
            P(),
            P(("rep", "grp"), None),
            P("grp"),
            P("grp", None),
            P("grp", None),
            P("grp", None),
            P("grp", None),
            P("grp", None),
            P("grp"),
            P("grp", None),
            P("grp", "rep", None),
            P("grp", "rep", None),
        ),
        check_vma=False,
    )
```

```python
from functools import partial

import jax
import jax.numpy as jnp
from jax import lax
from jax.experimental import pallas as pl
from jax.experimental.pallas import tpu as pltpu
from jax.sharding import PartitionSpec as P

TOP = 2
QB = 128
PAIR = 128
NEAR = 2 * QB
SPAN = 3 * QB
OUT_OF_DOC = -1e30
FAR_MARKS = (18, 20, 23, 26, 30, 34, 39, 45, 51, 58, 66, 76, 86, 98, 112)
norm_eps = 1e-06
aux_weight = 0.01
f32, bf16 = jnp.float32, jnp.bfloat16


def after(x, *earlier):
    return lax.optimization_barrier((x, earlier))[0]


def rms_scale(values):
    return lax.rsqrt(jnp.mean(values * values, axis=-1, keepdims=True) + norm_eps)


def bucket_of(distance):
    far_part = jnp.zeros_like(distance)
    for far_mark in FAR_MARKS:
        far_part = far_part + (distance >= far_mark).astype(jnp.int32)
    return jnp.minimum(distance, 16) + far_part


def band_hot(buckets):
    lane = lax.broadcasted_iota(jnp.int32, (8, SPAN), 1)
    row = lax.broadcasted_iota(jnp.int32, (8, SPAN), 0)
    turn = (lane - row + SPAN) % SPAN
    diff = jnp.where(turn < QB, turn, turn - SPAN) + QB
    bucket = bucket_of(jnp.maximum(diff, 0)).reshape(1, 8 * SPAN)
    return bucket == lax.iota(jnp.int32, buckets)[:, None]


def split_pair(rows, low_lanes):
    zero = jnp.zeros_like(rows)
    return jnp.concatenate(
        [jnp.where(low_lanes, rows, zero), jnp.where(low_lanes, zero, rows)], axis=0
    )


def fill_mask(seg_col, seg_row, mask):
    seq = mask.shape[0]
    for i in range(seq // QB):
        length = (i + 1) * QB
        sk = seg_col[0:length, :]
        sq = seg_row[:, i * QB:(i + 1) * QB]
        kp = lax.broadcasted_iota(jnp.int32, (length, QB), 0)
        qp = lax.broadcasted_iota(jnp.int32, (length, QB), 1) + i * QB
        ok = (sk == sq) & (kp <= qp) & ((sq != 0) | (kp == qp))
        mask[0:length, i * QB:(i + 1) * QB] = jnp.where(ok, 0.0, OUT_OF_DOC).astype(f32)


def fill_near(base, near):
    for head in range(2):
        rows = base[head]
        for a in range(NEAR // 8):
            turned = rows if a == 0 else pltpu.roll(rows, 8 * a, 1)
            near[8 * a:8 * a + 8, head * QB:(head + 1) * QB] = turned[:, 0:QB]


def scores_chunk(k, lo, hi, qcat, mask, near, i):
    s = lax.dot_general(k[lo:hi, :], qcat, (((1,), (1,)), ((), ())), preferred_element_type=f32)
    m = mask[lo:hi, i * QB:(i + 1) * QB]
    s = s + jnp.concatenate([m, m], axis=1)
    start = (i - 1) * QB
    if lo >= start:
        s = s + near[lo - start:hi - start, :]
    return s


def fwd_kernel(base, seg_col, seg_row, q, k, v, ctx, lse, mask, near, scores, probs, v_t):
    seq = q.shape[0]

    @pl.when(pl.program_id(0) == 0)
    def _():
        fill_mask(seg_col, seg_row, mask)

    fill_near(base, near)
    v_t[...] = v[...].T
    low_lanes = lax.broadcasted_iota(jnp.int32, (QB, PAIR), 1) < PAIR // 2
    scale = (PAIR // 2) ** -0.5
    for i in range(seq // QB):
        qs = slice(i * QB, (i + 1) * QB)
        qcat = split_pair(q[qs, :] * jnp.asarray(scale, bf16), low_lanes)
        top = None
        for c in range(i + 1):
            s = scores_chunk(k, c * QB, (c + 1) * QB, qcat, mask, near, i)
            scores[c * QB:(c + 1) * QB, :] = s
            here = jnp.max(s.reshape(QB // 8, 8, NEAR), axis=0)
            top = here if top is None else jnp.maximum(top, here)
        top = jnp.max(top, axis=0, keepdims=True)
        total = jnp.zeros((8, NEAR), f32)
        for c in range(i + 1):
            p = jnp.exp(scores[c * QB:(c + 1) * QB, :] - top)
            total = total + jnp.sum(p.reshape(QB // 8, 8, NEAR), axis=0)
            probs[c * QB:(c + 1) * QB, :] = p.astype(bf16)
        total = jnp.sum(total, axis=0, keepdims=True)
        length = (i + 1) * QB
        out = jnp.dot(v_t[:, 0:length], probs[0:length, :], preferred_element_type=f32) / total
        half = PAIR // 2
        both = jnp.concatenate([out[0:half, 0:QB], out[half:PAIR, QB:NEAR]], axis=0)
        ctx[qs, :] = both.T.astype(bf16)
        lse[0, i:i + 1, :] = top + jnp.log(total)


def attend(q, k, v, seg, base):
    seq, width = q.shape
    pairs = width // PAIR
    col = pl.BlockSpec((seq, PAIR), lambda h: (0, h))
    whole = lambda *shape: pl.BlockSpec(shape, lambda h: (0,) * len(shape))
    return pl.pallas_call(
        fwd_kernel,
        grid=(pairs,),
        in_specs=[pl.BlockSpec((2, 8, SPAN), lambda h: (h, 0, 0)), whole(seq, 1), whole(1, seq), col, col, col],
        out_specs=[col, pl.BlockSpec((1, seq // QB, NEAR), lambda h: (h, 0, 0))],
        out_shape=[
            jax.ShapeDtypeStruct((seq, width), bf16),
            jax.ShapeDtypeStruct((pairs, seq // QB, NEAR), f32),
        ],
        scratch_shapes=[
            pltpu.VMEM((seq, seq), f32),
            pltpu.VMEM((NEAR, NEAR), f32),
            pltpu.VMEM((seq, NEAR), f32),
            pltpu.VMEM((seq, NEAR), bf16),
            pltpu.VMEM((PAIR, seq), bf16),
        ],
        compiler_params=pltpu.CompilerParams(vmem_limit_bytes=32 * 1024 * 1024),
        cost_estimate=pl.CostEstimate(flops=1, bytes_accessed=1024, transcendentals=0),
        name="attend",
    )(base, seg.reshape(seq, 1), seg.reshape(1, seq), q, k, v)


def bwd_kernel(base, seg_col, seg_row, q, k, v, ctx, dctx, lse, dq, dk, dv, dnear, dfar,
               mask, near, ds_all, p_all, k_t, dk_sum, dv_sum, dnear_sum, dfar_sum):
    seq = q.shape[0]

    @pl.when(pl.program_id(0) == 0)
    def _():
        fill_mask(seg_col, seg_row, mask)

    fill_near(base, near)
    k_t[...] = k[...].T
    low_lanes = lax.broadcasted_iota(jnp.int32, (QB, PAIR), 1) < PAIR // 2
    half = PAIR // 2
    scale = half ** -0.5
    dnear_sum[...] = jnp.zeros_like(dnear_sum)
    dfar_sum[...] = jnp.zeros_like(dfar_sum)
    for i in reversed(range(seq // QB)):
        qs = slice(i * QB, (i + 1) * QB)
        length = (i + 1) * QB
        qcat = split_pair(q[qs, :] * jnp.asarray(scale, bf16), low_lanes)
        dcat = split_pair(dctx[qs, :], low_lanes)
        dots = (ctx[qs, :].astype(f32) * dctx[qs, :].astype(f32)).T
        centre = jnp.concatenate(
            [jnp.sum(dots[0:half], axis=0, keepdims=True), jnp.sum(dots[half:], axis=0, keepdims=True)], axis=1
        )
        norm = lse[0, i:i + 1, :]
        for c in range(i + 1):
            lo, hi = c * QB, (c + 1) * QB
            s = scores_chunk(k, lo, hi, qcat, mask, near, i)
            p = jnp.exp(s - norm)
            p_all[lo:hi, :] = p.astype(bf16)
            dp = lax.dot_general(v[lo:hi, :], dcat, (((1,), (1,)), ((), ())), preferred_element_type=f32)
            ds = p * (dp - centre)
            ds_all[lo:hi, :] = ds.astype(bf16)
            start = (i - 1) * QB
            if lo >= start:
                dnear_sum[lo - start:hi - start, :] += ds
            else:
                dfar_sum[...] += jnp.sum(ds.reshape(QB // 8, 8, NEAR), axis=0)
        out = jnp.dot(k_t[:, 0:length], ds_all[0:length, :], preferred_element_type=f32)
        both = jnp.concatenate([out[0:half, 0:QB], out[half:PAIR, QB:NEAR]], axis=0)
        dq[qs, :] = (both.T * scale).astype(bf16)
        dk_part = jnp.dot(ds_all[0:length, :], qcat, preferred_element_type=f32)
        dv_part = jnp.dot(p_all[0:length, :], dcat, preferred_element_type=f32)
        if i == seq // QB - 1:
            dk_sum[0:length, :] = dk_part
            dv_sum[0:length, :] = dv_part
        else:
            dk_sum[0:length, :] += dk_part
            dv_sum[0:length, :] += dv_part
    dk[...] = dk_sum[...].astype(bf16)
    dv[...] = dv_sum[...].astype(bf16)
    for head in range(2):
        total = jnp.zeros((8, SPAN), f32)
        for a in range(NEAR // 8):
            rows = dnear_sum[8 * a:8 * a + 8, head * QB:(head + 1) * QB]
            rows = jnp.concatenate([rows, jnp.zeros((8, SPAN - QB), f32)], axis=1)
            total = total + (rows if a == 0 else pltpu.roll(rows, SPAN - 8 * a, 1))
        dnear[head] = total
    dfar[0] = dfar_sum[...]


def attend_back(q, k, v, seg, base, ctx, dctx, lse):
    seq, width = q.shape
    pairs = width // PAIR
    col = pl.BlockSpec((seq, PAIR), lambda h: (0, h))
    band = pl.BlockSpec((2, 8, SPAN), lambda h: (h, 0, 0))
    whole = lambda *shape: pl.BlockSpec(shape, lambda h: (0,) * len(shape))
    rows = jax.ShapeDtypeStruct((seq, width), bf16)
    return pl.pallas_call(
        bwd_kernel,
        grid=(pairs,),
        in_specs=[band, whole(seq, 1), whole(1, seq), col, col, col, col, col,
                  pl.BlockSpec((1, seq // QB, NEAR), lambda h: (h, 0, 0))],
        out_specs=[col, col, col, band, pl.BlockSpec((1, 8, NEAR), lambda h: (h, 0, 0))],
        out_shape=[rows, rows, rows, jax.ShapeDtypeStruct((2 * pairs, 8, SPAN), f32),
                   jax.ShapeDtypeStruct((pairs, 8, NEAR), f32)],
        scratch_shapes=[
            pltpu.VMEM((seq, seq), f32),
            pltpu.VMEM((NEAR, NEAR), f32),
            pltpu.VMEM((seq, NEAR), bf16),
            pltpu.VMEM((seq, NEAR), bf16),
            pltpu.VMEM((PAIR, seq), bf16),
            pltpu.VMEM((seq, PAIR), f32),
            pltpu.VMEM((seq, PAIR), f32),
            pltpu.VMEM((NEAR, NEAR), f32),
            pltpu.VMEM((8, NEAR), f32),
        ],
        compiler_params=pltpu.CompilerParams(vmem_limit_bytes=40 * 1024 * 1024),
        cost_estimate=pl.CostEstimate(flops=1, bytes_accessed=1024, transcendentals=0),
        name="attend_back",
    )(base, seg.reshape(seq, 1), seg.reshape(1, seq), q, k, v, ctx, dctx, lse)


def bias_base(table):
    buckets, heads = table.shape
    hot = band_hot(buckets).astype(bf16)
    base = lax.dot_general(table, hot, (((0,), (0,)), ((), ())), preferred_element_type=f32)
    last = table[buckets - 1].astype(f32)
    return base.reshape(heads, 8, SPAN) - last[:, None, None]


def table_back(dnear, dfar, buckets):
    heads = dnear.shape[0]
    hot = band_hot(buckets).astype(f32)
    grad = lax.dot_general(hot, dnear.reshape(heads, 8 * SPAN), (((1,), (1,)), ((), ())),
                           preferred_element_type=f32, precision=lax.Precision.HIGHEST)
    far = jnp.sum(dfar.reshape(heads // 2, 8, 2, QB), axis=(1, 3)).reshape(1, heads)
    last = (lax.iota(jnp.int32, buckets) == buckets - 1)[:, None]
    return grad + jnp.where(last, far, 0.0)


def gelu_and_slope(u):
    root = (2.0 / jnp.pi) ** 0.5
    square = u * u
    bent = jnp.tanh(u * (root + (root * 0.044715) * square))
    rise = 0.5 + 0.5 * bent
    slope = rise + (0.5 * u) * (1.0 - bent * bent) * (root + (root * 3 * 0.044715) * square)
    return u * rise, slope


def expert_kernel(first, n_a, n_b, g_a, g_b, info, router_t, w_in, w_out, *rest):
    (y_a, y_b, r_a, r_b, act_out, dpre_out, x_out, dy_out,
     hot, x_s, g_s, dy_s, gate_s, y_sum, d_sum, y_all, d_all, dgate_c) = rest[-18:]
    e, f = pl.program_id(0), pl.program_id(1)
    rows, width = n_a.shape
    cap = x_s.shape[0] // 2
    expert = first[0] + e
    sources = ((n_a, g_a), (n_b, g_b))

    @pl.when((e == 0) & (f == 0))
    def _():
        dgate_c[...] = jnp.zeros_like(dgate_c)

    @pl.when(f == 0)
    def _():
        for s, (n_ref, g_ref) in enumerate(sources):
            logits = lax.dot_general(router_t[...], n_ref[...], (((1,), (1,)), ((), ())), preferred_element_type=f32)
            ids = lax.broadcasted_iota(jnp.int32, logits.shape, 0)
            power = jnp.exp(logits - jnp.max(logits, axis=0, keepdims=True))
            prob = power / jnp.sum(power, axis=0, keepdims=True)
            chosen = (ids == info[4 * s + 2:4 * s + 3, :]) | (ids == info[4 * s + 3:4 * s + 4, :])
            both = jnp.sum(jnp.where(chosen, prob, 0.0), axis=0, keepdims=True)
            gate_row = jnp.sum(jnp.where(ids == expert, prob, 0.0), axis=0, keepdims=True) / both
            slot_row = jnp.where(e == 0, info[4 * s:4 * s + 1, :], info[4 * s + 1:4 * s + 2, :])
            match = slot_row == lax.broadcasted_iota(jnp.int32, (cap, rows), 0)
            one_hot = jnp.where(match, 1.0, 0.0).astype(bf16)
            part = slice(s * cap, (s + 1) * cap)
            gate_s[part, :] = jnp.sum(jnp.where(match, gate_row, 0.0), axis=1, keepdims=True)
            hot[s, pl.ds(pl.multiple_of(e * cap, cap), cap), :] = one_hot
            x_s[part, :] = jnp.dot(one_hot, n_ref[...], preferred_element_type=f32).astype(bf16)
            g_rows = jnp.dot(one_hot, g_ref[...], preferred_element_type=f32)
            g_s[part, :] = g_rows.astype(bf16)
            dy_s[part, :] = (gate_s[part, :] * g_rows).astype(bf16)
        y_sum[...] = jnp.zeros_like(y_sum)
        d_sum[...] = jnp.zeros_like(d_sum)
        x_out[0] = x_s[...]
        dy_out[0] = dy_s[...]

    pre = jnp.dot(x_s[...], w_in[0], preferred_element_type=f32)
    dact = lax.dot_general(dy_s[...], w_out[0], (((1,), (1,)), ((), ())), preferred_element_type=f32)
    act, slope = gelu_and_slope(pre)
    act_out[0] = act.astype(bf16)
    dpre_out[0] = (dact * slope).astype(bf16)
    y_sum[...] += jnp.dot(act_out[0], w_out[0], preferred_element_type=f32)
    d_sum[...] += lax.dot_general(dpre_out[0], w_in[0], (((1,), (1,)), ((), ())), preferred_element_type=f32)

    @pl.when(f == pl.num_programs(1) - 1)
    def _():
        y_rows = y_sum[...].astype(bf16).astype(f32)
        dgate = jnp.sum(y_rows * g_s[...].astype(f32), axis=1, keepdims=True)
        y_rows = (gate_s[...] * y_rows).astype(bf16)
        d_rows = d_sum[...].astype(bf16)
        for s in range(2):
            part = slice(s * cap, (s + 1) * cap)
            here = pl.ds(pl.multiple_of(e * cap, cap), cap)
            y_all[s, here, :] = y_rows[part]
            d_all[s, here, :] = d_rows[part]
            slot_row = jnp.where(e == 0, info[4 * s:4 * s + 1, :], info[4 * s + 1:4 * s + 2, :])
            match = slot_row == lax.broadcasted_iota(jnp.int32, (cap, rows), 0)
            row = jnp.sum(jnp.where(match, dgate[part], 0.0), axis=0, keepdims=True)
            for c in range(TOP):
                routed = info[4 * s + 2 + c:4 * s + 3 + c, :] == expert
                dgate_c[TOP * s + c:TOP * s + c + 1, :] += jnp.where(routed, row, 0.0)

    @pl.when((e == pl.num_programs(0) - 1) & (f == pl.num_programs(1) - 1))
    def _():
        turn = (((0,), (0,)), ((), ()))
        for s, (y_ref, r_ref) in enumerate(((y_a, r_a), (y_b, r_b))):
            y_ref[...] = lax.dot_general(hot[s], y_all[s], turn, preferred_element_type=f32).astype(bf16)
            r_ref[0:rows, :] = lax.dot_general(hot[s], d_all[s], turn, preferred_element_type=f32).astype(bf16)
            value = dgate_c[TOP * s:TOP * s + TOP, :]
            high = value.astype(bf16)
            value = value - high.astype(f32)
            middle = value.astype(bf16)
            low = (value - middle.astype(f32)).astype(bf16)
            pieces = jnp.concatenate([high.astype(f32), middle.astype(f32), low.astype(f32), jnp.zeros((2, rows), f32)], axis=0)
            over = jnp.concatenate([pieces[:, width:], jnp.zeros((8, 2 * width - rows), f32)], axis=1)
            r_ref[rows:rows + 16, :] = jnp.concatenate([pieces[:, 0:width], over], axis=0).astype(bf16)


def unpack_dgate(tail, rows):
    tail = tail.astype(f32)
    pieces = jnp.concatenate([tail[0:8], tail[8:16]], axis=1)[:, 0:rows]
    return pieces[0:2] + pieces[2:4] + pieces[4:6]


def expert_block(k, blocks, first, n_a, n_b, g_a, g_b, info, router_t, w_in, w_out, cap, kept):
    rows, width = n_a.shape
    local, _, hidden = w_in.shape
    part = 768 if hidden % 768 == 0 else hidden
    once = pl.Buffered(1)
    whole = lambda *shape: pl.BlockSpec(shape, lambda e, f: (0,) * len(shape), pipeline_mode=once)
    wide = pl.BlockSpec((1, 2 * cap, part), lambda e, f: (e, k, f))
    slim = pl.BlockSpec((1, 2 * cap, width), lambda e, f: (e, k, 0))
    slots = blocks * 2 * cap
    shapes = [
        jax.ShapeDtypeStruct((rows, width), bf16), jax.ShapeDtypeStruct((rows, width), bf16),
        jax.ShapeDtypeStruct((rows + 16, width), bf16), jax.ShapeDtypeStruct((rows + 16, width), bf16),
        jax.ShapeDtypeStruct((local, slots, hidden), bf16), jax.ShapeDtypeStruct((local, slots, hidden), bf16),
        jax.ShapeDtypeStruct((local, slots, width), bf16), jax.ShapeDtypeStruct((local, slots, width), bf16),
    ]
    in_specs = [
        pl.BlockSpec(memory_space=pltpu.SMEM), whole(rows, width), whole(rows, width), whole(rows, width), whole(rows, width),
        whole(8, rows), whole(*router_t.shape),
        pl.BlockSpec((1, width, part), lambda e, f: (e, 0, f)), pl.BlockSpec((1, part, width), lambda e, f: (e, f, 0)),
    ]
    args = [first, n_a, n_b, g_a, g_b, info, router_t, w_in, w_out]
    alias = {}
    if kept is not None:
        alias = {len(args) + i: 4 + i for i in range(4)}
        in_specs += [pl.BlockSpec(memory_space=pl.ANY)] * 4
        args += list(kept)
    out = pl.pallas_call(
        expert_kernel,
        grid=(local, hidden // part),
        in_specs=in_specs,
        out_specs=[whole(rows, width), whole(rows, width), whole(rows + 16, width), whole(rows + 16, width), wide, wide, slim, slim],
        out_shape=shapes,
        scratch_shapes=[
            pltpu.VMEM((2, local * cap, rows), bf16),
            pltpu.VMEM((2 * cap, width), bf16), pltpu.VMEM((2 * cap, width), bf16), pltpu.VMEM((2 * cap, width), bf16),
            pltpu.VMEM((2 * cap, 1), f32),
            pltpu.VMEM((2 * cap, width), f32), pltpu.VMEM((2 * cap, width), f32),
            pltpu.VMEM((2, local * cap, width), bf16), pltpu.VMEM((2, local * cap, width), bf16),
            pltpu.VMEM((8, rows), f32),
        ],
        input_output_aliases=alias,
        compiler_params=pltpu.CompilerParams(vmem_limit_bytes=48 * 1024 * 1024),
        cost_estimate=pl.CostEstimate(flops=2 * local * cap * (8 * width * hidden + 8 * width * rows), bytes_accessed=60 * 1024 * 1024, transcendentals=2 * local * cap * hidden),
        name="expert_block",
    )(*args)
    return out[:4], out[4:]


def chip_ring(chips):
    return [0] + list(range(1, chips, 2)) + [z for z in range(chips - 1, 0, -1) if z % 2 == 0]


class Group:
    def __init__(self):
        self.size = lax.axis_size("grp")
        self.chips = self.size // 2
        self.order = chip_ring(self.chips)
        me = lax.axis_index("grp")
        self.me, self.chip, self.core = me, me // 2, me % 2

    def onward(self, x):
        pairs = []
        for i, z in enumerate(self.order):
            after = self.order[(i + 1) % self.chips]
            pairs += [(2 * z, 2 * after), (2 * z + 1, 2 * after + 1)]
        return lax.ppermute(x, "grp", pairs)

    def backward(self, x):
        pairs = []
        for i, z in enumerate(self.order):
            before = self.order[(i - 1) % self.chips]
            pairs += [(2 * z, 2 * before), (2 * z + 1, 2 * before + 1)]
        return lax.ppermute(x, "grp", pairs)

    def swap(self, x):
        return lax.ppermute(x, "grp", [(i, i ^ 1) for i in range(self.size)])

    def source_chip(self, k):
        table = [0] * self.chips
        for i, z in enumerate(self.order):
            table[z] = self.order[(i - k) % self.chips]
        return jnp.asarray(table, jnp.int32)[self.chip]


def pick_constant(table, index):
    value = jnp.int32(table[0])
    for i in range(1, len(table)):
        value = jnp.where(index == i, jnp.int32(table[i]), value)
    return value


def gather_kernel(chips, reps, stack, small, tally, stack_all, small_all, tally_all,
                  own_sem, ring_send, ring_recv, core_send, core_recv, own_send, own_recv,
                  plane_send, plane_recv, cross_send, cross_recv, rep_send, rep_recv, tally_in, tally_sum, tally_vmem):
    order = chip_ring(chips)
    mats, rows = stack.shape[0], stack.shape[1]
    rep, me = lax.axis_index("rep"), lax.axis_index("grp")
    chip, core = me // 2, me % 2
    mine = lax.rem(rep, mats)
    after_z, before_z = [0] * chips, [0] * chips
    for i, z in enumerate(order):
        after_z[z], before_z[z] = order[(i + 1) % chips], order[(i - 1) % chips]
    onward = 2 * pick_constant(after_z, chip) + core
    before = 2 * pick_constant(before_z, chip) + core
    sibling = 2 * chip + 1 - core
    mesh_id = pl.DeviceIdType.MESH
    plane = [(rep - mine) + lax.rem(mine + j, mats) for j in range(1, mats)]

    barrier = pltpu.get_barrier_semaphore()
    peers = [(rep, onward), (rep, before), (rep, sibling)] + [(lax.rem(rep + k, reps), me) for k in range(1, reps)]
    for peer in peers:
        pl.semaphore_signal(barrier, inc=1, device_id=peer, device_id_type=mesh_id)
    pl.semaphore_wait(barrier, len(peers))

    def remote(src, dst, send, recv, target):
        return pltpu.make_async_remote_copy(
            src_ref=src, dst_ref=dst, send_sem=send, recv_sem=recv, device_id=target, device_id_type=mesh_id
        )

    def owner_of(k, which_core):
        source = [0] * chips
        for i, z in enumerate(order):
            source[z] = order[(i - k) % chips]
        return 2 * pick_constant(source, chip) + which_core

    def shard(mat, owner):
        return stack_all.at[mat, pl.ds(pl.multiple_of(owner * rows, rows), rows), :]

    def places(k, which_core):
        owner = owner_of(k, which_core)
        return [shard(mine, owner), small_all.at[owner], tally_all.at[owner]]

    def matrix(j):
        return lax.rem(mine + j, mats)

    sent = []

    def start(copy):
        copy.start()
        sent.append(copy)
        return copy

    tallies = [
        start(remote(tally, tally_in.at[k - 1], rep_send.at[k - 1], rep_recv.at[k - 1], (lax.rem(rep + k, reps), me)))
        for k in range(1, reps)
    ]
    own = [
        pltpu.make_async_copy(stack, stack_all.at[:, pl.ds(pl.multiple_of(me * rows, rows), rows), :], own_sem.at[0]),
        pltpu.make_async_copy(small, small_all.at[me], own_sem.at[1]),
        pltpu.make_async_copy(tally, tally_vmem, own_sem.at[2]),
    ]
    for copy in own:
        copy.start()
    here = places(0, core)
    moved = [
        start(remote(stack.at[mine], here[0], ring_send.at[0, 0], ring_recv.at[0, 0], (rep, onward))),
        start(remote(small, here[1], ring_send.at[0, 1], ring_recv.at[0, 1], (rep, onward))),
    ]
    everywhere = stack_all.at[:, pl.ds(pl.multiple_of(me * rows, rows), rows), :]
    start(remote(small, here[1], core_send.at[0, 1], core_recv.at[0, 1], (rep, sibling)))
    start(remote(stack, everywhere, own_send, own_recv, (rep, sibling)))
    own[2].wait()
    total = tally_vmem[...]
    for k, copy in enumerate(tallies):
        copy.wait_recv()
        total = total + tally_in[k]
    tally_sum[...] = total
    keep = pltpu.make_async_copy(tally_sum, here[2], own_sem.at[3])
    keep.start()
    own = [own[0], own[1], keep]
    moved.append(start(remote(tally_sum, here[2], ring_send.at[0, 2], ring_recv.at[0, 2], (rep, onward))))
    start(remote(tally_sum, here[2], core_send.at[0, 2], core_recv.at[0, 2], (rep, sibling)))

    def pass_across(k):
        for j in range(1, mats):
            block = shard(matrix(j), owner_of(k, core))
            remote(block, block, plane_send.at[k, j - 1], plane_recv.at[k, mats - 1 - j], (plane[j - 1], me)).wait_recv()
            start(remote(block, block, cross_send.at[k, mats - 1 - j], cross_recv.at[k, j - 1], (rep, sibling)))

    for k in range(1, chips):
        here = places(k, core)
        for a in range(3):
            moved[a].wait_recv()
            if k < chips - 1:
                moved[a] = start(remote(here[a], here[a], ring_send.at[k, a], ring_recv.at[k, a], (rep, onward)))
            if a == 0:
                for j in range(1, mats):
                    start(remote(here[0], here[0], plane_send.at[k, j - 1], plane_recv.at[k, j - 1], (plane[j - 1], me)))
            start(remote(here[a], here[a], core_send.at[k, a], core_recv.at[k, a], (rep, sibling)))
        if k > 1:
            pass_across(k - 1)
    pass_across(chips - 1)
    for copy in sent:
        copy.wait_send()
    for copy in own:
        copy.wait()
    other = stack_all.at[:, pl.ds(pl.multiple_of(sibling * rows, rows), rows), :]
    remote(stack, other, own_send, own_recv, (rep, sibling)).wait_recv()
    for k in range(chips):
        there = places(k, 1 - core)
        for a in range(3):
            if a > 0 or k > 0:
                remote(there[a], there[a], core_send.at[k, a], core_recv.at[k, a], (rep, sibling)).wait_recv()
        if k > 0:
            for j in range(1, mats):
                block = shard(matrix(j), owner_of(k, 1 - core))
                remote(block, block, cross_send.at[k, j - 1], cross_recv.at[k, j - 1], (rep, sibling)).wait_recv()


def gather_group(stack, small, tally):
    size, reps = lax.axis_size("grp"), lax.axis_size("rep")
    chips = size // 2
    mats, rows, width = stack.shape
    hbm = pl.BlockSpec(memory_space=pl.ANY)
    dma = pltpu.SemaphoreType.DMA
    return pl.pallas_call(
        partial(gather_kernel, chips, reps),
        in_specs=[hbm] * 3,
        out_specs=[hbm] * 3,
        out_shape=[
            jax.ShapeDtypeStruct((mats, size * rows, width), stack.dtype),
            jax.ShapeDtypeStruct((size,) + small.shape, small.dtype),
            jax.ShapeDtypeStruct((size,) + tally.shape, f32),
        ],
        scratch_shapes=[
            dma((4,)), dma((chips, 3)), dma((chips, 3)), dma((chips, 3)), dma((chips, 3)), dma, dma,
            dma((chips, mats - 1)), dma((chips, mats - 1)), dma((chips, mats - 1)), dma((chips, mats - 1)),
            dma((reps,)), dma((reps,)),
            pltpu.VMEM((reps - 1,) + tally.shape, f32), pltpu.VMEM(tally.shape, f32), pltpu.VMEM(tally.shape, f32),
        ],
        compiler_params=pltpu.CompilerParams(collective_id=0, has_side_effects=True),
        cost_estimate=pl.CostEstimate(flops=0, bytes_accessed=16 * 1024 * 1024, transcendentals=0),
        name="gather_group",
    )(stack, small, tally)


def pack_small(gain_attn, gain_ffn, router, rel_bias, routes):
    def lanes(x):
        return jnp.pad(x, ((0, 0), (0, 128 - x.shape[1])))

    rows = jnp.concatenate([
        lanes(gain_attn[None]), lanes(gain_ffn[None]), lanes(rel_bias), lanes(router.T),
        routes.T.astype(bf16).reshape(-1, 128),
    ], axis=0)
    return jnp.pad(rows, ((0, -rows.shape[0] % 16), (0, 0)))


def unpack_small(packed, size, shard, bias_rows, heads, experts, tokens):
    blocks = packed.reshape(size, -1, 128)
    gain_one = blocks[:, 0, 0:shard].reshape(-1)
    gain_two = blocks[:, 1, 0:shard].reshape(-1)
    at = 2 + bias_rows
    table = blocks[:, 2:at, 0:heads].reshape(-1, heads)
    router_t = jnp.transpose(blocks[:, at:at + experts, 0:shard], (1, 0, 2)).reshape(experts, -1)
    at += experts
    routes = blocks[:, at:at + TOP * tokens // 128].reshape(size, TOP, tokens).astype(jnp.int32)
    return gain_one, gain_two, table, router_t, routes


def outer_sum(left_rows, right_rows):
    return lax.dot_general(
        left_rows, right_rows, (((0,), (0,)), ((), ())), preferred_element_type=jnp.float32
    )


def back_proj(grad_rows, weight):
    return lax.dot_general(
        grad_rows, weight, (((1,), (1,)), ((), ())), preferred_element_type=jnp.float32
    )


def reduce_steps(group, own, sibling, sent_as=bf16):
    moving, total = None, None
    for k in list(range(1, group.chips)) + [0]:
        pins = yield moving, total
        other = group.swap(sibling[k].astype(sent_as))
        if pins is not None:
            other, moving = after((other, moving), pins)
        total = own[k].astype(f32) + other.astype(f32)
        if moving is not None:
            total = total + moving.astype(f32)
        if k != 0:
            total = total.astype(sent_as)
            moving = group.onward(total)
    yield moving, total


def reduce_both_ways(group, own, sibling):
    half = group.chips // 2
    ahead, behind, total = None, None, None
    for k in list(range(half - 1, 0, -1)) + list(range(half, group.chips)) + [0]:
        pins = yield ahead, behind, total
        other = group.swap(sibling[k])
        if k >= half:
            other, ahead = after((other, ahead), pins)
            arrived = [ahead]
        elif k > 0:
            other, behind = after((other, behind), pins)
            arrived = [behind]
        else:
            other, ahead, behind = after((other, ahead, behind), pins)
            arrived = [ahead, behind]
        total = own[k].astype(f32) + other.astype(f32)
        for block in arrived:
            if block is not None:
                total = total + block.astype(f32)
        if k > 0:
            total = total.astype(bf16)
        if k >= half:
            ahead = group.onward(total)
        elif k > 0:
            behind = group.backward(total)
    yield ahead, behind, total


def local_slots(routes_all, first, local):
    ids = first + lax.iota(jnp.int32, local)
    hot = jnp.any(routes_all[:, None, :, :] == ids[None, :, None, None], axis=2).astype(jnp.int32)
    return jnp.where(hot != 0, jnp.cumsum(hot, axis=2) - hot, -1)


def shards(
    tokens,
    segments,
    routes,
    gain_attn,
    w_query,
    w_key,
    w_value,
    w_output,
    rel_bias,
    gain_ffn,
    router,
    w_in,
    w_out,
    cotangent,
):
    group = Group()
    tok_rows, width = tokens.shape
    exp_local = w_in.shape[0]
    groups = group.size
    experts = exp_local * groups
    capacity = 2 * tok_rows * TOP // experts
    choose = routes[:, :, None] == lax.iota(jnp.int32, experts)[None, None, :]
    tally = jnp.pad(jnp.sum(choose.astype(f32), axis=(0, 1))[None], ((0, 7), (0, 128 - experts)))
    small = pack_small(gain_attn, gain_ffn, router, rel_bias, routes)
    stack_all, small_all, tally_all = gather_group(jnp.stack([w_query, w_key, w_value, w_output]), small, tally)
    query_full, key_full, value_full, output_full = [stack_all[m] for m in range(4)]
    gain_one, gain_two, table_full, router_t, routes_all = unpack_small(
        small_all, groups, gain_attn.shape[0], rel_bias.shape[0], rel_bias.shape[1], experts, tok_rows
    )
    router_full = router_t.T
    counts = jnp.sum(tally_all[:, 0, 0:experts], axis=0)
    first = (group.me * exp_local).astype(jnp.int32)

    kept_grad = jnp.where((segments != 0)[:, None], cotangent, jnp.zeros_like(cotangent))
    grad_ring = [kept_grad]
    for k in range(1, group.chips - 1):
        grad_ring.append(group.onward(grad_ring[-1]))
    grad_ring.append(group.backward(after(kept_grad, small_all)))
    slots_all = local_slots(after(routes_all, grad_ring[1]), first, exp_local)

    inputs = tokens.astype(f32)
    scale_one = rms_scale(inputs)
    normed_one = (inputs * scale_one * gain_one.astype(f32)).astype(bf16)
    normed_one = after(normed_one, grad_ring[1])
    query_rows = jnp.dot(normed_one, query_full, preferred_element_type=f32).astype(bf16)
    key_rows = jnp.dot(normed_one, key_full, preferred_element_type=f32).astype(bf16)
    value_rows = jnp.dot(normed_one, value_full, preferred_element_type=f32).astype(bf16)
    base = bias_base(table_full)
    context, lse = attend(query_rows, key_rows, value_rows, after(segments, slots_all), base)
    context = after(context, grad_ring[-1])
    hidden_one = inputs + jnp.dot(context, output_full, preferred_element_type=f32)
    scale_two = rms_scale(hidden_one)
    normed_two = (hidden_one * scale_two * gain_two.astype(f32)).astype(bf16)

    kept = None
    results = []
    sibs = [group.swap(block) for block in grad_ring[:3]]
    ring = list(grad_ring)
    norm_ring = [normed_two]
    for k in range(group.chips):
        if k >= 3:
            sibs.append(group.swap(after(ring[k], results[k - 3][2])))
        norm_now = norm_ring[k]
        norm_sib = group.swap(norm_now)
        if k < group.chips - 1:
            moved = group.onward(norm_now)
        chip = group.source_chip(k)
        info = jnp.concatenate(
            [
                lax.dynamic_index_in_dim(rows, 2 * chip + core, 0, keepdims=False)
                for core in (group.core, 1 - group.core)
                for rows in (slots_all, routes_all)
            ],
            axis=0,
        )
        if k == 0:
            info = after(info, ring[2])
        if k == group.chips - 1:
            back_own, back_sib = [r[2] for r in results], [r[3] for r in results]
            back_steps = reduce_steps(group, back_own, back_sib)
            next(back_steps)
            sent = back_steps.send(None)[1]
            info = after(info, sent)
        outs, kept = expert_block(
            k, group.chips, first.reshape(1), norm_now, norm_sib, ring[k], sibs[k],
            info, router_t, w_in, w_out, capacity, kept,
        )
        results.append(outs)
        if k == group.chips - 1:
            back_own.append(outs[2])
            back_sib.append(outs[3])
        if k < group.chips - 1:
            norm_ring.append(after(moved, outs[2]))

    act_all, dpre_all, x_all, dy_all = kept
    chips = group.chips
    for k in range(2, chips - 1):
        sent = back_steps.send(outs[2])[1]
    up_grad = jnp.einsum("ekd,ekf->edf", after(x_all, sent), dpre_all, preferred_element_type=f32).astype(bf16)
    sent = back_steps.send(up_grad)[1]
    up_share = lax.psum_scatter(after(up_grad, sent), "rep", scatter_dimension=1, tiled=True)
    down_grad = jnp.einsum("ekf,ekd->efd", act_all, after(dy_all, sent), preferred_element_type=f32).astype(bf16)

    y_steps = reduce_both_ways(group, [r[0] for r in results], [r[1] for r in results])
    next(y_steps)
    sums = []
    for k in range(chips - 2):
        y_ahead, y_behind, sent = y_steps.send(down_grad)
        sums.append(sent)
    back = back_steps.send((down_grad, sums))[1]
    down_share = lax.psum_scatter(after(down_grad, back), "rep", scatter_dimension=1, tiled=True)

    logits = jnp.dot(normed_two, router_full, preferred_element_type=f32)
    router_prob = jax.nn.softmax(logits, axis=-1)
    picked_prob = jnp.sum(jnp.where(choose, router_prob[:, None, :], 0.0), axis=-1)
    prob_sum = jnp.sum(picked_prob, axis=-1, keepdims=True)
    all_tokens = tok_rows * lax.axis_size("rep") * groups
    fraction = counts / (TOP * all_tokens)

    grad_out = kept_grad.astype(f32)
    grad_gate = unpack_dgate(back[tok_rows:], tok_rows).T
    grad_norm_two = back[0:tok_rows]
    grad_picked = grad_gate / prob_sum - jnp.sum(
        grad_gate * picked_prob, axis=-1, keepdims=True
    ) / (prob_sum * prob_sum)
    grad_router_prob = (
        jnp.sum(jnp.where(choose, grad_picked[:, :, None], 0.0), axis=1)
        + aux_weight * experts * fraction / all_tokens
    )
    grad_logits = (
        router_prob
        * (grad_router_prob - jnp.sum(router_prob * grad_router_prob, axis=-1, keepdims=True))
    ).astype(jnp.bfloat16)
    router_grad = outer_sum(normed_two, grad_logits)
    grad_norm_two = grad_norm_two + back_proj(grad_logits, router_full)
    gain_two_grad = jnp.sum(grad_norm_two * (hidden_one * scale_two), axis=0)
    scaled_two = grad_norm_two * gain_two.astype(jnp.float32)
    grad_hidden_one = (
        grad_out
        + scale_two * scaled_two
        - hidden_one * scale_two**3 * jnp.mean(scaled_two * hidden_one, axis=-1, keepdims=True)
    )
    grad_attn = grad_hidden_one.astype(jnp.bfloat16)
    output_grad = outer_sum(context, grad_attn)
    grad_context = back_proj(grad_attn, output_full).astype(jnp.bfloat16)
    grad_query_rows, grad_key_rows, grad_value_rows, near_grad, far_grad = attend_back(
        query_rows, key_rows, value_rows, segments, base, context, grad_context, lse
    )
    grad_query_rows, grad_key_rows, grad_value_rows = after((grad_query_rows, grad_key_rows, grad_value_rows), y_behind)
    query_grad = outer_sum(normed_one, grad_query_rows)
    key_grad = outer_sum(normed_one, grad_key_rows)
    value_grad = outer_sum(normed_one, grad_value_rows)
    grad_norm_one = (
        back_proj(grad_query_rows, query_full)
        + back_proj(grad_key_rows, key_full)
        + back_proj(grad_value_rows, value_full)
    )
    gain_one_grad = jnp.sum(grad_norm_one * (inputs * scale_one), axis=0)
    scaled_one = grad_norm_one * gain_one.astype(jnp.float32)
    grad_input = (
        grad_hidden_one
        + scale_one * scaled_one
        - inputs * scale_one**3 * jnp.mean(scaled_one * inputs, axis=-1, keepdims=True)
    )
    table_grad = table_back(near_grad, far_grad, table_full.shape[0])
    def shares(x, rows):
        x = x.reshape(x.shape[:-2] + (groups, rows, x.shape[-1]))
        def one(k, core):
            return lax.dynamic_index_in_dim(x, 2 * group.source_chip(k) + core, x.ndim - 3, keepdims=False)
        return [one(k, group.core) for k in range(chips)], [one(k, 1 - group.core) for k in range(chips)]

    rows = width // groups
    dense = jnp.stack([query_grad, key_grad, value_grad, output_grad]).astype(bf16)
    dense_own, dense_sib = shares(dense, rows)

    def lanes(x):
        return jnp.pad(x, ((0, 0), (0, 0), (0, 128 - x.shape[2])))

    heads = table_grad.shape[1]
    bias_rows = table_grad.shape[0] // groups
    prob_row = jnp.broadcast_to(jnp.sum(router_prob, axis=0), (groups, 1, experts))
    small = jnp.concatenate([
        lanes(gain_one_grad.reshape(groups, 1, rows)), lanes(gain_two_grad.reshape(groups, 1, rows)),
        lanes(prob_row), lanes(table_grad.reshape(groups, bias_rows, heads)),
        lanes(jnp.transpose(router_grad.T.reshape(experts, groups, rows), (1, 0, 2))),
    ], axis=1)
    small = jnp.pad(small, ((0, 0), (0, -small.shape[1] % 8), (0, 0)))
    small_own, small_sib = shares(small.reshape(-1, 128), small.shape[1])
    lines = -(-small_own[0].size // width)

    def pack_sums(matrices, rest):
        rest = jnp.pad(rest.reshape(-1), (0, lines * width - rest.size)).reshape(lines, width)
        high = lax.reduce_precision(rest, 8, 7)
        parts = (matrices.reshape(-1, width), high, rest - high)
        return jnp.concatenate([part.astype(bf16) for part in parts], axis=0)

    def unpack_sums(block):
        block = block.astype(f32)
        rest = block[-2 * lines:-lines] + block[-lines:]
        return block[:-2 * lines].reshape(dense_own[0].shape), rest.reshape(-1)[:small_own[0].size].reshape(small_own[0].shape)

    up_share, down_share = up_share.astype(f32), down_share.astype(f32)
    arriving, pins = None, y_ahead
    for k in list(range(1, chips)) + [0]:
        other, rest = group.swap(dense_sib[k]), group.swap(small_sib[k])
        if pins is not None:
            other = after(other, pins)
        dense_sum = dense_own[k].astype(f32) + other.astype(f32)
        small_sum = small_own[k] + rest
        if arriving is not None:
            more, rest = unpack_sums(arriving)
            dense_sum, small_sum = dense_sum + more, small_sum + rest
        if k > 0:
            block = pack_sums(dense_sum, small_sum)
            arriving = group.onward(block)
        pins = (up_share, grad_input) if k == 1 else None
        if k == chips - 1:
            y_steps.send(block)
    mixed = y_steps.send(dense_sum)[2]
    output = (hidden_one + mixed).astype(bf16)

    def over_rep(x):
        count = lax.axis_size("rep")
        return x.astype(f32), [lax.ppermute(x, "rep", [(i, i ^ k) for i in range(count)]) for k in range(1, count)]

    reps = lax.axis_size("rep")
    small, small_moved = over_rep(small_sum)
    if reps == dense_sum.shape[0]:
        me = lax.axis_index("rep")
        sent = dense_sum.astype(bf16)

        def swap_with(k, x):
            return lax.ppermute(x, "rep", [(i, i ^ k) for i in range(reps)])

        mine = lax.dynamic_index_in_dim(dense_sum, me, 0, keepdims=False)
        for k in range(1, reps):
            mine = mine + swap_with(k, lax.dynamic_index_in_dim(sent, me ^ k, 0, keepdims=False)).astype(f32)
        mine = mine.astype(bf16)
        whole = jnp.stack([mine] + after([swap_with(k, mine) for k in range(1, reps)], output))
        dense = [lax.dynamic_index_in_dim(whole, me ^ m, 0, keepdims=False).astype(f32) for m in range(reps)]
    else:
        dense, dense_moved = over_rep(dense_sum.astype(bf16))
        for got in after(dense_moved, output):
            dense = dense + got.astype(f32)
    for also in small_moved:
        small = small + also
    at = 3 + bias_rows
    balance_terms = experts * experts * fraction * (small[2, 0:experts] / all_tokens)
    loss = aux_weight / experts * jnp.sum(balance_terms)
    return (
        output,
        loss,
        balance_terms,
        grad_input,
        small[0, 0:rows],
        dense[0],
        dense[1],
        dense[2],
        dense[3],
        small[3:at, 0:heads],
        small[1, 0:rows],
        small[at:at + experts, 0:rows].T,
        up_share,
        down_share,
    )


def solution(mesh):
    return jax.shard_map(
        shards,
        mesh=mesh,
        in_specs=(
            P(("rep", "grp"), None),
            P(("rep", "grp")),
            P(("rep", "grp"), None),
            P("grp"),
            P("grp", None),
            P("grp", None),
            P("grp", None),
            P("grp", None),
            P("grp", None),
            P("grp"),
            P("grp", None),
            P("grp", None, None),
            P("grp", None, None),
            P(("rep", "grp"), None),
        ),
        out_specs=(
            P(("rep", "grp"), None),
            P(),
            P(),
            P(("rep", "grp"), None),
            P("grp"),
            P("grp", None),
            P("grp", None),
            P("grp", None),
            P("grp", None),
            P("grp", None),
            P("grp"),
            P("grp", None),
            P("grp", "rep", None),
            P("grp", "rep", None),
        ),
        check_vma=False,
    )
```

```python
from functools import partial

import jax
import jax.numpy as jnp
from jax import lax
from jax.experimental import pallas as pl
from jax.experimental.pallas import tpu as pltpu
from jax.sharding import PartitionSpec as P

TOP = 2
QB = 128
PAIR = 128
NEAR = 2 * QB
SPAN = 3 * QB
OUT_OF_DOC = -1e30
FAR_MARKS = (18, 20, 23, 26, 30, 34, 39, 45, 51, 58, 66, 76, 86, 98, 112)
norm_eps = 1e-06
aux_weight = 0.01
f32, bf16 = jnp.float32, jnp.bfloat16


def after(x, *earlier):
    return lax.optimization_barrier((x, earlier))[0]


def rms_scale(values):
    return lax.rsqrt(jnp.mean(values * values, axis=-1, keepdims=True) + norm_eps)


def bucket_of(distance):
    far_part = jnp.zeros_like(distance)
    for far_mark in FAR_MARKS:
        far_part = far_part + (distance >= far_mark).astype(jnp.int32)
    return jnp.minimum(distance, 16) + far_part


def band_hot(buckets):
    lane = lax.broadcasted_iota(jnp.int32, (8, SPAN), 1)
    row = lax.broadcasted_iota(jnp.int32, (8, SPAN), 0)
    turn = (lane - row + SPAN) % SPAN
    diff = jnp.where(turn < QB, turn, turn - SPAN) + QB
    bucket = bucket_of(jnp.maximum(diff, 0)).reshape(1, 8 * SPAN)
    return bucket == lax.iota(jnp.int32, buckets)[:, None]


def split_pair(rows, low_lanes):
    zero = jnp.zeros_like(rows)
    return jnp.concatenate(
        [jnp.where(low_lanes, rows, zero), jnp.where(low_lanes, zero, rows)], axis=0
    )


def fill_mask(seg_col, seg_row, mask):
    seq = mask.shape[0]
    for i in range(seq // QB):
        length = (i + 1) * QB
        sk = seg_col[0:length, :]
        sq = seg_row[:, i * QB:(i + 1) * QB]
        kp = lax.broadcasted_iota(jnp.int32, (length, QB), 0)
        qp = lax.broadcasted_iota(jnp.int32, (length, QB), 1) + i * QB
        ok = (sk == sq) & (kp <= qp) & ((sq != 0) | (kp == qp))
        mask[0:length, i * QB:(i + 1) * QB] = jnp.where(ok, 0.0, OUT_OF_DOC).astype(f32)


def fill_near(base, near):
    for head in range(2):
        rows = base[head]
        for a in range(NEAR // 8):
            turned = rows if a == 0 else pltpu.roll(rows, 8 * a, 1)
            near[8 * a:8 * a + 8, head * QB:(head + 1) * QB] = turned[:, 0:QB]


def scores_chunk(k, lo, hi, qcat, mask, near, i):
    s = lax.dot_general(k[lo:hi, :], qcat, (((1,), (1,)), ((), ())), preferred_element_type=f32)
    m = mask[lo:hi, i * QB:(i + 1) * QB]
    s = s + jnp.concatenate([m, m], axis=1)
    start = (i - 1) * QB
    if lo >= start:
        s = s + near[lo - start:hi - start, :]
    return s


def fwd_kernel(base, seg_col, seg_row, q, k, v, ctx, lse, mask, near, scores, probs, v_t):
    seq = q.shape[0]

    @pl.when(pl.program_id(0) == 0)
    def _():
        fill_mask(seg_col, seg_row, mask)

    fill_near(base, near)
    v_t[...] = v[...].T
    low_lanes = lax.broadcasted_iota(jnp.int32, (QB, PAIR), 1) < PAIR // 2
    scale = (PAIR // 2) ** -0.5
    for i in range(seq // QB):
        qs = slice(i * QB, (i + 1) * QB)
        qcat = split_pair(q[qs, :] * jnp.asarray(scale, bf16), low_lanes)
        top = None
        for c in range(i + 1):
            s = scores_chunk(k, c * QB, (c + 1) * QB, qcat, mask, near, i)
            scores[c * QB:(c + 1) * QB, :] = s
            here = jnp.max(s.reshape(QB // 8, 8, NEAR), axis=0)
            top = here if top is None else jnp.maximum(top, here)
        top = jnp.max(top, axis=0, keepdims=True)
        total = jnp.zeros((8, NEAR), f32)
        for c in range(i + 1):
            p = jnp.exp(scores[c * QB:(c + 1) * QB, :] - top)
            total = total + jnp.sum(p.reshape(QB // 8, 8, NEAR), axis=0)
            probs[c * QB:(c + 1) * QB, :] = p.astype(bf16)
        total = jnp.sum(total, axis=0, keepdims=True)
        length = (i + 1) * QB
        out = jnp.dot(v_t[:, 0:length], probs[0:length, :], preferred_element_type=f32) / total
        half = PAIR // 2
        both = jnp.concatenate([out[0:half, 0:QB], out[half:PAIR, QB:NEAR]], axis=0)
        ctx[qs, :] = both.T.astype(bf16)
        lse[0, i:i + 1, :] = top + jnp.log(total)


def attend(q, k, v, seg, base):
    seq, width = q.shape
    pairs = width // PAIR
    col = pl.BlockSpec((seq, PAIR), lambda h: (0, h))
    whole = lambda *shape: pl.BlockSpec(shape, lambda h: (0,) * len(shape))
    return pl.pallas_call(
        fwd_kernel,
        grid=(pairs,),
        in_specs=[pl.BlockSpec((2, 8, SPAN), lambda h: (h, 0, 0)), whole(seq, 1), whole(1, seq), col, col, col],
        out_specs=[col, pl.BlockSpec((1, seq // QB, NEAR), lambda h: (h, 0, 0))],
        out_shape=[
            jax.ShapeDtypeStruct((seq, width), bf16),
            jax.ShapeDtypeStruct((pairs, seq // QB, NEAR), f32),
        ],
        scratch_shapes=[
            pltpu.VMEM((seq, seq), f32),
            pltpu.VMEM((NEAR, NEAR), f32),
            pltpu.VMEM((seq, NEAR), f32),
            pltpu.VMEM((seq, NEAR), bf16),
            pltpu.VMEM((PAIR, seq), bf16),
        ],
        compiler_params=pltpu.CompilerParams(vmem_limit_bytes=32 * 1024 * 1024),
        cost_estimate=pl.CostEstimate(flops=1, bytes_accessed=1024, transcendentals=0),
        name="attend",
    )(base, seg.reshape(seq, 1), seg.reshape(1, seq), q, k, v)


def bwd_kernel(base, seg_col, seg_row, q, k, v, ctx, dctx, lse, dq, dk, dv, dnear, dfar,
               mask, near, ds_all, p_all, k_t, dk_sum, dv_sum, dnear_sum, dfar_sum):
    seq = q.shape[0]

    @pl.when(pl.program_id(0) == 0)
    def _():
        fill_mask(seg_col, seg_row, mask)

    fill_near(base, near)
    k_t[...] = k[...].T
    low_lanes = lax.broadcasted_iota(jnp.int32, (QB, PAIR), 1) < PAIR // 2
    half = PAIR // 2
    scale = half ** -0.5
    dnear_sum[...] = jnp.zeros_like(dnear_sum)
    dfar_sum[...] = jnp.zeros_like(dfar_sum)
    for i in reversed(range(seq // QB)):
        qs = slice(i * QB, (i + 1) * QB)
        length = (i + 1) * QB
        qcat = split_pair(q[qs, :] * jnp.asarray(scale, bf16), low_lanes)
        dcat = split_pair(dctx[qs, :], low_lanes)
        dots = (ctx[qs, :].astype(f32) * dctx[qs, :].astype(f32)).T
        centre = jnp.concatenate(
            [jnp.sum(dots[0:half], axis=0, keepdims=True), jnp.sum(dots[half:], axis=0, keepdims=True)], axis=1
        )
        norm = lse[0, i:i + 1, :]
        for c in range(i + 1):
            lo, hi = c * QB, (c + 1) * QB
            s = scores_chunk(k, lo, hi, qcat, mask, near, i)
            p = jnp.exp(s - norm)
            p_all[lo:hi, :] = p.astype(bf16)
            dp = lax.dot_general(v[lo:hi, :], dcat, (((1,), (1,)), ((), ())), preferred_element_type=f32)
            ds = p * (dp - centre)
            ds_all[lo:hi, :] = ds.astype(bf16)
            start = (i - 1) * QB
            if lo >= start:
                dnear_sum[lo - start:hi - start, :] += ds
            else:
                dfar_sum[...] += jnp.sum(ds.reshape(QB // 8, 8, NEAR), axis=0)
        out = jnp.dot(k_t[:, 0:length], ds_all[0:length, :], preferred_element_type=f32)
        both = jnp.concatenate([out[0:half, 0:QB], out[half:PAIR, QB:NEAR]], axis=0)
        dq[qs, :] = (both.T * scale).astype(bf16)
        dk_part = jnp.dot(ds_all[0:length, :], qcat, preferred_element_type=f32)
        dv_part = jnp.dot(p_all[0:length, :], dcat, preferred_element_type=f32)
        if i == seq // QB - 1:
            dk_sum[0:length, :] = dk_part
            dv_sum[0:length, :] = dv_part
        else:
            dk_sum[0:length, :] += dk_part
            dv_sum[0:length, :] += dv_part
    dk[...] = dk_sum[...].astype(bf16)
    dv[...] = dv_sum[...].astype(bf16)
    for head in range(2):
        total = jnp.zeros((8, SPAN), f32)
        for a in range(NEAR // 8):
            rows = dnear_sum[8 * a:8 * a + 8, head * QB:(head + 1) * QB]
            rows = jnp.concatenate([rows, jnp.zeros((8, SPAN - QB), f32)], axis=1)
            total = total + (rows if a == 0 else pltpu.roll(rows, SPAN - 8 * a, 1))
        dnear[head] = total
    dfar[0] = dfar_sum[...]


def attend_back(q, k, v, seg, base, ctx, dctx, lse):
    seq, width = q.shape
    pairs = width // PAIR
    col = pl.BlockSpec((seq, PAIR), lambda h: (0, h))
    band = pl.BlockSpec((2, 8, SPAN), lambda h: (h, 0, 0))
    whole = lambda *shape: pl.BlockSpec(shape, lambda h: (0,) * len(shape))
    rows = jax.ShapeDtypeStruct((seq, width), bf16)
    return pl.pallas_call(
        bwd_kernel,
        grid=(pairs,),
        in_specs=[band, whole(seq, 1), whole(1, seq), col, col, col, col, col,
                  pl.BlockSpec((1, seq // QB, NEAR), lambda h: (h, 0, 0))],
        out_specs=[col, col, col, band, pl.BlockSpec((1, 8, NEAR), lambda h: (h, 0, 0))],
        out_shape=[rows, rows, rows, jax.ShapeDtypeStruct((2 * pairs, 8, SPAN), f32),
                   jax.ShapeDtypeStruct((pairs, 8, NEAR), f32)],
        scratch_shapes=[
            pltpu.VMEM((seq, seq), f32),
            pltpu.VMEM((NEAR, NEAR), f32),
            pltpu.VMEM((seq, NEAR), bf16),
            pltpu.VMEM((seq, NEAR), bf16),
            pltpu.VMEM((PAIR, seq), bf16),
            pltpu.VMEM((seq, PAIR), f32),
            pltpu.VMEM((seq, PAIR), f32),
            pltpu.VMEM((NEAR, NEAR), f32),
            pltpu.VMEM((8, NEAR), f32),
        ],
        compiler_params=pltpu.CompilerParams(vmem_limit_bytes=40 * 1024 * 1024),
        cost_estimate=pl.CostEstimate(flops=1, bytes_accessed=1024, transcendentals=0),
        name="attend_back",
    )(base, seg.reshape(seq, 1), seg.reshape(1, seq), q, k, v, ctx, dctx, lse)


def bias_base(table):
    buckets, heads = table.shape
    hot = band_hot(buckets).astype(bf16)
    base = lax.dot_general(table, hot, (((0,), (0,)), ((), ())), preferred_element_type=f32)
    last = table[buckets - 1].astype(f32)
    return base.reshape(heads, 8, SPAN) - last[:, None, None]


def table_back(dnear, dfar, buckets):
    heads = dnear.shape[0]
    hot = band_hot(buckets).astype(f32)
    grad = lax.dot_general(hot, dnear.reshape(heads, 8 * SPAN), (((1,), (1,)), ((), ())),
                           preferred_element_type=f32, precision=lax.Precision.HIGHEST)
    far = jnp.sum(dfar.reshape(heads // 2, 8, 2, QB), axis=(1, 3)).reshape(1, heads)
    last = (lax.iota(jnp.int32, buckets) == buckets - 1)[:, None]
    return grad + jnp.where(last, far, 0.0)


def gelu_and_slope(u):
    root = (2.0 / jnp.pi) ** 0.5
    square = u * u
    bent = jnp.tanh(u * (root + (root * 0.044715) * square))
    rise = 0.5 + 0.5 * bent
    slope = rise + (0.5 * u) * (1.0 - bent * bent) * (root + (root * 3 * 0.044715) * square)
    return u * rise, slope


def expert_kernel(first, n_a, n_b, g_a, g_b, info, router_t, w_in, w_out, *rest):
    (y_a, y_b, r_a, r_b, act_out, dpre_out, x_out, dy_out,
     hot, x_s, g_s, dy_s, gate_s, y_sum, d_sum, yd_all, gates, dgate_c) = rest[-18:]
    e, f = pl.program_id(0), pl.program_id(1)
    rows, width = n_a.shape
    cap = x_s.shape[0] // 2
    expert = first[0] + e
    sources = ((n_a, g_a), (n_b, g_b))

    @pl.when((e == 0) & (f == 0))
    def _():
        dgate_c[...] = jnp.zeros_like(dgate_c)
        for s, (n_ref, g_ref) in enumerate(sources):
            logits = lax.dot_general(router_t[...], n_ref[...], (((1,), (1,)), ((), ())), preferred_element_type=f32)
            ids = lax.broadcasted_iota(jnp.int32, logits.shape, 0)
            power = jnp.exp(logits - jnp.max(logits, axis=0, keepdims=True))
            prob = power / jnp.sum(power, axis=0, keepdims=True)
            chosen = (ids == info[4 * s + 2:4 * s + 3, :]) | (ids == info[4 * s + 3:4 * s + 4, :])
            both = jnp.sum(jnp.where(chosen, prob, 0.0), axis=0, keepdims=True)
            gates[s] = prob / both

    @pl.when(f == 0)
    def _():
        for s, (n_ref, g_ref) in enumerate(sources):
            ids = lax.broadcasted_iota(jnp.int32, gates.shape[1:], 0)
            gate_row = jnp.sum(jnp.where(ids == expert, gates[s], 0.0), axis=0, keepdims=True)
            slot_row = jnp.where(e == 0, info[4 * s:4 * s + 1, :], info[4 * s + 1:4 * s + 2, :])
            match = slot_row == lax.broadcasted_iota(jnp.int32, (cap, rows), 0)
            one_hot = jnp.where(match, 1.0, 0.0).astype(bf16)
            part = slice(s * cap, (s + 1) * cap)
            gate_s[part, :] = jnp.sum(jnp.where(match, gate_row, 0.0), axis=1, keepdims=True)
            hot[s, pl.ds(pl.multiple_of(e * cap, cap), cap), :] = one_hot
            x_s[part, :] = jnp.dot(one_hot, n_ref[...], preferred_element_type=f32).astype(bf16)
            g_rows = jnp.dot(one_hot, g_ref[...], preferred_element_type=f32)
            g_s[part, :] = g_rows.astype(bf16)
            dy_s[part, :] = (gate_s[part, :] * g_rows).astype(bf16)
        y_sum[...] = jnp.zeros_like(y_sum)
        d_sum[...] = jnp.zeros_like(d_sum)
        x_out[0] = x_s[...]
        dy_out[0] = dy_s[...]

    pre = jnp.dot(x_s[...], w_in[0], preferred_element_type=f32)
    dact = lax.dot_general(dy_s[...], w_out[0], (((1,), (1,)), ((), ())), preferred_element_type=f32)
    act, slope = gelu_and_slope(pre)
    act_out[0] = act.astype(bf16)
    dpre_out[0] = (dact * slope).astype(bf16)
    y_sum[...] += jnp.dot(act_out[0], w_out[0], preferred_element_type=f32)
    d_sum[...] += lax.dot_general(dpre_out[0], w_in[0], (((1,), (1,)), ((), ())), preferred_element_type=f32)

    @pl.when(f == pl.num_programs(1) - 1)
    def _():
        y_rows = y_sum[...].astype(bf16).astype(f32)
        dgate = jnp.sum(y_rows * g_s[...].astype(f32), axis=1, keepdims=True)
        y_rows = (gate_s[...] * y_rows).astype(bf16)
        d_rows = d_sum[...].astype(bf16)
        for s in range(2):
            part = slice(s * cap, (s + 1) * cap)
            here = pl.ds(pl.multiple_of(e * cap, cap), cap)
            yd_all[s, here, 0:width] = y_rows[part]
            yd_all[s, here, width:] = d_rows[part]
            slot_row = jnp.where(e == 0, info[4 * s:4 * s + 1, :], info[4 * s + 1:4 * s + 2, :])
            match = slot_row == lax.broadcasted_iota(jnp.int32, (cap, rows), 0)
            row = jnp.sum(jnp.where(match, dgate[part], 0.0), axis=0, keepdims=True)
            for c in range(TOP):
                routed = info[4 * s + 2 + c:4 * s + 3 + c, :] == expert
                dgate_c[TOP * s + c:TOP * s + c + 1, :] += jnp.where(routed, row, 0.0)

    @pl.when((e == pl.num_programs(0) - 1) & (f == pl.num_programs(1) - 1))
    def _():
        turn = (((0,), (0,)), ((), ()))
        for s, (y_ref, r_ref) in enumerate(((y_a, r_a), (y_b, r_b))):
            sums = lax.dot_general(hot[s], yd_all[s], turn, preferred_element_type=f32).astype(bf16)
            y_ref[...] = sums[:, 0:width]
            r_ref[0:rows, :] = sums[:, width:]
            value = dgate_c[TOP * s:TOP * s + TOP, :]
            high = value.astype(bf16)
            value = value - high.astype(f32)
            middle = value.astype(bf16)
            low = (value - middle.astype(f32)).astype(bf16)
            pieces = jnp.concatenate([high.astype(f32), middle.astype(f32), low.astype(f32), jnp.zeros((2, rows), f32)], axis=0)
            over = jnp.concatenate([pieces[:, width:], jnp.zeros((8, 2 * width - rows), f32)], axis=1)
            r_ref[rows:rows + 16, :] = jnp.concatenate([pieces[:, 0:width], over], axis=0).astype(bf16)


def unpack_dgate(tail, rows):
    tail = tail.astype(f32)
    pieces = jnp.concatenate([tail[0:8], tail[8:16]], axis=1)[:, 0:rows]
    return pieces[0:2] + pieces[2:4] + pieces[4:6]


def expert_block(k, blocks, first, n_a, n_b, g_a, g_b, info, router_t, w_in, w_out, cap, kept):
    rows, width = n_a.shape
    local, _, hidden = w_in.shape
    part = 768 if hidden % 768 == 0 else hidden
    once = pl.Buffered(1)
    whole = lambda *shape: pl.BlockSpec(shape, lambda e, f: (0,) * len(shape), pipeline_mode=once)
    wide = pl.BlockSpec((1, 2 * cap, part), lambda e, f: (e, k, f))
    slim = pl.BlockSpec((1, 2 * cap, width), lambda e, f: (e, k, 0))
    slots = blocks * 2 * cap
    shapes = [
        jax.ShapeDtypeStruct((rows, width), bf16), jax.ShapeDtypeStruct((rows, width), bf16),
        jax.ShapeDtypeStruct((rows + 16, width), bf16), jax.ShapeDtypeStruct((rows + 16, width), bf16),
        jax.ShapeDtypeStruct((local, slots, hidden), bf16), jax.ShapeDtypeStruct((local, slots, hidden), bf16),
        jax.ShapeDtypeStruct((local, slots, width), bf16), jax.ShapeDtypeStruct((local, slots, width), bf16),
    ]
    in_specs = [
        pl.BlockSpec(memory_space=pltpu.SMEM), whole(rows, width), whole(rows, width), whole(rows, width), whole(rows, width),
        whole(8, rows), whole(*router_t.shape),
        pl.BlockSpec((1, width, part), lambda e, f: (e, 0, f)), pl.BlockSpec((1, part, width), lambda e, f: (e, f, 0)),
    ]
    args = [first, n_a, n_b, g_a, g_b, info, router_t, w_in, w_out]
    alias = {}
    if kept is not None:
        alias = {len(args) + i: 4 + i for i in range(4)}
        in_specs += [pl.BlockSpec(memory_space=pl.ANY)] * 4
        args += list(kept)
    out = pl.pallas_call(
        expert_kernel,
        grid=(local, hidden // part),
        in_specs=in_specs,
        out_specs=[whole(rows, width), whole(rows, width), whole(rows + 16, width), whole(rows + 16, width), wide, wide, slim, slim],
        out_shape=shapes,
        scratch_shapes=[
            pltpu.VMEM((2, local * cap, rows), bf16),
            pltpu.VMEM((2 * cap, width), bf16), pltpu.VMEM((2 * cap, width), bf16), pltpu.VMEM((2 * cap, width), bf16),
            pltpu.VMEM((2 * cap, 1), f32),
            pltpu.VMEM((2 * cap, width), f32), pltpu.VMEM((2 * cap, width), f32),
            pltpu.VMEM((2, local * cap, 2 * width), bf16), pltpu.VMEM((2,) + (router_t.shape[0], rows), f32),
            pltpu.VMEM((8, rows), f32),
        ],
        input_output_aliases=alias,
        compiler_params=pltpu.CompilerParams(vmem_limit_bytes=48 * 1024 * 1024),
        cost_estimate=pl.CostEstimate(flops=2 * local * cap * (8 * width * hidden + 8 * width * rows), bytes_accessed=60 * 1024 * 1024, transcendentals=2 * local * cap * hidden),
        name="expert_block",
    )(*args)
    return out[:4], out[4:]


def chip_ring(chips):
    return [0] + list(range(1, chips, 2)) + [z for z in range(chips - 1, 0, -1) if z % 2 == 0]


class Group:
    def __init__(self):
        self.size = lax.axis_size("grp")
        self.chips = self.size // 2
        self.order = chip_ring(self.chips)
        me = lax.axis_index("grp")
        self.me, self.chip, self.core = me, me // 2, me % 2

    def onward(self, x):
        pairs = []
        for i, z in enumerate(self.order):
            after = self.order[(i + 1) % self.chips]
            pairs += [(2 * z, 2 * after), (2 * z + 1, 2 * after + 1)]
        return lax.ppermute(x, "grp", pairs)

    def backward(self, x):
        pairs = []
        for i, z in enumerate(self.order):
            before = self.order[(i - 1) % self.chips]
            pairs += [(2 * z, 2 * before), (2 * z + 1, 2 * before + 1)]
        return lax.ppermute(x, "grp", pairs)

    def swap(self, x):
        return lax.ppermute(x, "grp", [(i, i ^ 1) for i in range(self.size)])

    def source_chip(self, k):
        table = [0] * self.chips
        for i, z in enumerate(self.order):
            table[z] = self.order[(i - k) % self.chips]
        return jnp.asarray(table, jnp.int32)[self.chip]


def pick_constant(table, index):
    value = jnp.int32(table[0])
    for i in range(1, len(table)):
        value = jnp.where(index == i, jnp.int32(table[i]), value)
    return value


def gather_kernel(chips, reps, stack, small, tally, stack_all, small_all, tally_all,
                  own_sem, ring_send, ring_recv, core_send, core_recv, own_send, own_recv,
                  plane_send, plane_recv, cross_send, cross_recv, rep_send, rep_recv, tally_in, tally_sum, tally_vmem):
    order = chip_ring(chips)
    mats, rows = stack.shape[0], stack.shape[1]
    rep, me = lax.axis_index("rep"), lax.axis_index("grp")
    chip, core = me // 2, me % 2
    mine = lax.rem(rep, mats)
    after_z, before_z = [0] * chips, [0] * chips
    for i, z in enumerate(order):
        after_z[z], before_z[z] = order[(i + 1) % chips], order[(i - 1) % chips]
    onward = 2 * pick_constant(after_z, chip) + core
    before = 2 * pick_constant(before_z, chip) + core
    sibling = 2 * chip + 1 - core
    mesh_id = pl.DeviceIdType.MESH
    plane = [(rep - mine) + lax.rem(mine + j, mats) for j in range(1, mats)]

    barrier = pltpu.get_barrier_semaphore()
    peers = [(rep, onward), (rep, before), (rep, sibling)] + [(lax.rem(rep + k, reps), me) for k in range(1, reps)]
    for peer in peers:
        pl.semaphore_signal(barrier, inc=1, device_id=peer, device_id_type=mesh_id)
    pl.semaphore_wait(barrier, len(peers))

    def remote(src, dst, send, recv, target):
        return pltpu.make_async_remote_copy(
            src_ref=src, dst_ref=dst, send_sem=send, recv_sem=recv, device_id=target, device_id_type=mesh_id
        )

    def owner_of(k, which_core):
        source = [0] * chips
        for i, z in enumerate(order):
            source[z] = order[(i - k) % chips]
        return 2 * pick_constant(source, chip) + which_core

    def shard(mat, owner):
        return stack_all.at[mat, pl.ds(pl.multiple_of(owner * rows, rows), rows), :]

    def places(k, which_core):
        owner = owner_of(k, which_core)
        return [shard(mine, owner), small_all.at[owner], tally_all.at[owner]]

    def matrix(j):
        return lax.rem(mine + j, mats)

    sent = []

    def start(copy):
        copy.start()
        sent.append(copy)
        return copy

    tallies = [
        start(remote(tally, tally_in.at[k - 1], rep_send.at[k - 1], rep_recv.at[k - 1], (lax.rem(rep + k, reps), me)))
        for k in range(1, reps)
    ]
    own = [
        pltpu.make_async_copy(stack, stack_all.at[:, pl.ds(pl.multiple_of(me * rows, rows), rows), :], own_sem.at[0]),
        pltpu.make_async_copy(small, small_all.at[me], own_sem.at[1]),
        pltpu.make_async_copy(tally, tally_vmem, own_sem.at[2]),
    ]
    for copy in own:
        copy.start()
    here = places(0, core)
    moved = [
        start(remote(stack.at[mine], here[0], ring_send.at[0, 0], ring_recv.at[0, 0], (rep, onward))),
        start(remote(small, here[1], ring_send.at[0, 1], ring_recv.at[0, 1], (rep, onward))),
    ]
    everywhere = stack_all.at[:, pl.ds(pl.multiple_of(me * rows, rows), rows), :]
    start(remote(small, here[1], core_send.at[0, 1], core_recv.at[0, 1], (rep, sibling)))
    start(remote(stack, everywhere, own_send, own_recv, (rep, sibling)))
    own[2].wait()
    total = tally_vmem[...]
    for k, copy in enumerate(tallies):
        copy.wait_recv()
        total = total + tally_in[k]
    tally_sum[...] = total
    keep = pltpu.make_async_copy(tally_sum, here[2], own_sem.at[3])
    keep.start()
    own = [own[0], own[1], keep]
    moved.append(start(remote(tally_sum, here[2], ring_send.at[0, 2], ring_recv.at[0, 2], (rep, onward))))
    start(remote(tally_sum, here[2], core_send.at[0, 2], core_recv.at[0, 2], (rep, sibling)))

    def pass_across(k):
        for j in range(1, mats):
            block = shard(matrix(j), owner_of(k, core))
            remote(block, block, plane_send.at[k, j - 1], plane_recv.at[k, mats - 1 - j], (plane[j - 1], me)).wait_recv()
            start(remote(block, block, cross_send.at[k, mats - 1 - j], cross_recv.at[k, j - 1], (rep, sibling)))

    for k in range(1, chips):
        here = places(k, core)
        for a in range(3):
            moved[a].wait_recv()
            if k < chips - 1:
                moved[a] = start(remote(here[a], here[a], ring_send.at[k, a], ring_recv.at[k, a], (rep, onward)))
            if a == 0:
                for j in range(1, mats):
                    start(remote(here[0], here[0], plane_send.at[k, j - 1], plane_recv.at[k, j - 1], (plane[j - 1], me)))
            start(remote(here[a], here[a], core_send.at[k, a], core_recv.at[k, a], (rep, sibling)))
        if k > 1:
            pass_across(k - 1)
    pass_across(chips - 1)
    for copy in sent:
        copy.wait_send()
    for copy in own:
        copy.wait()
    other = stack_all.at[:, pl.ds(pl.multiple_of(sibling * rows, rows), rows), :]
    remote(stack, other, own_send, own_recv, (rep, sibling)).wait_recv()
    for k in range(chips):
        there = places(k, 1 - core)
        for a in range(3):
            if a > 0 or k > 0:
                remote(there[a], there[a], core_send.at[k, a], core_recv.at[k, a], (rep, sibling)).wait_recv()
        if k > 0:
            for j in range(1, mats):
                block = shard(matrix(j), owner_of(k, 1 - core))
                remote(block, block, cross_send.at[k, j - 1], cross_recv.at[k, j - 1], (rep, sibling)).wait_recv()


def gather_group(stack, small, tally):
    size, reps = lax.axis_size("grp"), lax.axis_size("rep")
    chips = size // 2
    mats, rows, width = stack.shape
    hbm = pl.BlockSpec(memory_space=pl.ANY)
    dma = pltpu.SemaphoreType.DMA
    return pl.pallas_call(
        partial(gather_kernel, chips, reps),
        in_specs=[hbm] * 3,
        out_specs=[hbm] * 3,
        out_shape=[
            jax.ShapeDtypeStruct((mats, size * rows, width), stack.dtype),
            jax.ShapeDtypeStruct((size,) + small.shape, small.dtype),
            jax.ShapeDtypeStruct((size,) + tally.shape, f32),
        ],
        scratch_shapes=[
            dma((4,)), dma((chips, 3)), dma((chips, 3)), dma((chips, 3)), dma((chips, 3)), dma, dma,
            dma((chips, mats - 1)), dma((chips, mats - 1)), dma((chips, mats - 1)), dma((chips, mats - 1)),
            dma((reps,)), dma((reps,)),
            pltpu.VMEM((reps - 1,) + tally.shape, f32), pltpu.VMEM(tally.shape, f32), pltpu.VMEM(tally.shape, f32),
        ],
        compiler_params=pltpu.CompilerParams(collective_id=0, has_side_effects=True),
        cost_estimate=pl.CostEstimate(flops=0, bytes_accessed=16 * 1024 * 1024, transcendentals=0),
        name="gather_group",
    )(stack, small, tally)


def pack_small(gain_attn, gain_ffn, router, rel_bias, routes):
    def lanes(x):
        return jnp.pad(x, ((0, 0), (0, 128 - x.shape[1])))

    rows = jnp.concatenate([
        lanes(gain_attn[None]), lanes(gain_ffn[None]), lanes(rel_bias), lanes(router.T),
        routes.T.astype(bf16).reshape(-1, 128),
    ], axis=0)
    return jnp.pad(rows, ((0, -rows.shape[0] % 16), (0, 0)))


def unpack_small(packed, size, shard, bias_rows, heads, experts, tokens):
    blocks = packed.reshape(size, -1, 128)
    gain_one = blocks[:, 0, 0:shard].reshape(-1)
    gain_two = blocks[:, 1, 0:shard].reshape(-1)
    at = 2 + bias_rows
    table = blocks[:, 2:at, 0:heads].reshape(-1, heads)
    router_t = jnp.transpose(blocks[:, at:at + experts, 0:shard], (1, 0, 2)).reshape(experts, -1)
    at += experts
    routes = blocks[:, at:at + TOP * tokens // 128].reshape(size, TOP, tokens).astype(jnp.int32)
    return gain_one, gain_two, table, router_t, routes


def outer_sum(left_rows, right_rows):
    return lax.dot_general(
        left_rows, right_rows, (((0,), (0,)), ((), ())), preferred_element_type=jnp.float32
    )


def back_proj(grad_rows, weight):
    return lax.dot_general(
        grad_rows, weight, (((1,), (1,)), ((), ())), preferred_element_type=jnp.float32
    )


def reduce_steps(group, own, sibling, sent_as=bf16):
    moving, total = None, None
    for k in list(range(1, group.chips)) + [0]:
        pins = yield moving, total
        other = group.swap(sibling[k].astype(sent_as))
        if pins is not None:
            other, moving = after((other, moving), pins)
        total = own[k].astype(f32) + other.astype(f32)
        if moving is not None:
            total = total + moving.astype(f32)
        if k != 0:
            total = total.astype(sent_as)
            moving = group.onward(total)
    yield moving, total


def reduce_both_ways(group, own, sibling):
    half = group.chips // 2
    ahead, behind, total = None, None, None
    for k in list(range(half - 1, 0, -1)) + list(range(half, group.chips)) + [0]:
        pins = yield ahead, behind, total
        other = group.swap(sibling[k])
        if k >= half:
            other, ahead = after((other, ahead), pins)
            arrived = [ahead]
        elif k > 0:
            other, behind = after((other, behind), pins)
            arrived = [behind]
        else:
            other, ahead, behind = after((other, ahead, behind), pins)
            arrived = [ahead, behind]
        total = own[k].astype(f32) + other.astype(f32)
        for block in arrived:
            if block is not None:
                total = total + block.astype(f32)
        if k > 0:
            total = total.astype(bf16)
        if k >= half:
            ahead = group.onward(total)
        elif k > 0:
            behind = group.backward(total)
    yield ahead, behind, total


def local_slots(routes_all, first, local):
    ids = first + lax.iota(jnp.int32, local)
    hot = jnp.any(routes_all[:, None, :, :] == ids[None, :, None, None], axis=2).astype(jnp.int32)
    return jnp.where(hot != 0, jnp.cumsum(hot, axis=2) - hot, -1)


def shards(
    tokens,
    segments,
    routes,
    gain_attn,
    w_query,
    w_key,
    w_value,
    w_output,
    rel_bias,
    gain_ffn,
    router,
    w_in,
    w_out,
    cotangent,
):
    group = Group()
    tok_rows, width = tokens.shape
    exp_local = w_in.shape[0]
    groups = group.size
    experts = exp_local * groups
    capacity = 2 * tok_rows * TOP // experts
    choose = routes[:, :, None] == lax.iota(jnp.int32, experts)[None, None, :]
    tally = jnp.pad(jnp.sum(choose.astype(f32), axis=(0, 1))[None], ((0, 7), (0, 128 - experts)))
    small = pack_small(gain_attn, gain_ffn, router, rel_bias, routes)
    stack_all, small_all, tally_all = gather_group(jnp.stack([w_query, w_key, w_value, w_output]), small, tally)
    query_full, key_full, value_full, output_full = [stack_all[m] for m in range(4)]
    gain_one, gain_two, table_full, router_t, routes_all = unpack_small(
        small_all, groups, gain_attn.shape[0], rel_bias.shape[0], rel_bias.shape[1], experts, tok_rows
    )
    router_full = router_t.T
    counts = jnp.sum(tally_all[:, 0, 0:experts], axis=0)
    first = (group.me * exp_local).astype(jnp.int32)

    kept_grad = jnp.where((segments != 0)[:, None], cotangent, jnp.zeros_like(cotangent))
    grad_ring = [kept_grad]
    for k in range(1, group.chips - 1):
        grad_ring.append(group.onward(grad_ring[-1]))
    grad_ring.append(group.backward(after(kept_grad, small_all)))
    slots_all = local_slots(after(routes_all, grad_ring[1]), first, exp_local)

    inputs = tokens.astype(f32)
    scale_one = rms_scale(inputs)
    normed_one = (inputs * scale_one * gain_one.astype(f32)).astype(bf16)
    normed_one = after(normed_one, grad_ring[1])
    query_rows = jnp.dot(normed_one, query_full, preferred_element_type=f32).astype(bf16)
    key_rows = jnp.dot(normed_one, key_full, preferred_element_type=f32).astype(bf16)
    value_rows = jnp.dot(normed_one, value_full, preferred_element_type=f32).astype(bf16)
    base = bias_base(table_full)
    context, lse = attend(query_rows, key_rows, value_rows, after(segments, slots_all), base)
    context = after(context, grad_ring[-1])
    hidden_one = inputs + jnp.dot(context, output_full, preferred_element_type=f32)
    scale_two = rms_scale(hidden_one)
    normed_two = (hidden_one * scale_two * gain_two.astype(f32)).astype(bf16)

    kept = None
    results = []
    sibs = [group.swap(block) for block in grad_ring[:3]]
    ring = list(grad_ring)
    norm_ring = [normed_two]
    for k in range(group.chips):
        if k >= 3:
            sibs.append(group.swap(after(ring[k], results[k - 3][2])))
        norm_now = norm_ring[k]
        norm_sib = group.swap(norm_now)
        if k < group.chips - 1:
            moved = group.onward(norm_now)
        chip = group.source_chip(k)
        info = jnp.concatenate(
            [
                lax.dynamic_index_in_dim(rows, 2 * chip + core, 0, keepdims=False)
                for core in (group.core, 1 - group.core)
                for rows in (slots_all, routes_all)
            ],
            axis=0,
        )
        if k == 0:
            info = after(info, ring[2])
        if k == group.chips - 1:
            back_own, back_sib = [r[2] for r in results], [r[3] for r in results]
            back_steps = reduce_steps(group, back_own, back_sib)
            next(back_steps)
            sent = back_steps.send(None)[1]
            info = after(info, sent)
        outs, kept = expert_block(
            k, group.chips, first.reshape(1), norm_now, norm_sib, ring[k], sibs[k],
            info, router_t, w_in, w_out, capacity, kept,
        )
        results.append(outs)
        if k == group.chips - 1:
            back_own.append(outs[2])
            back_sib.append(outs[3])
        if k < group.chips - 1:
            norm_ring.append(after(moved, outs[2]))

    act_all, dpre_all, x_all, dy_all = kept
    chips = group.chips
    for k in range(2, chips - 1):
        sent = back_steps.send(outs[2])[1]
    up_grad = jnp.einsum("ekd,ekf->edf", after(x_all, sent), dpre_all, preferred_element_type=f32).astype(bf16)
    sent = back_steps.send(up_grad)[1]
    up_share = lax.psum_scatter(after(up_grad, sent), "rep", scatter_dimension=1, tiled=True)
    down_grad = jnp.einsum("ekf,ekd->efd", act_all, after(dy_all, sent), preferred_element_type=f32).astype(bf16)

    y_steps = reduce_both_ways(group, [r[0] for r in results], [r[1] for r in results])
    next(y_steps)
    sums = []
    for k in range(chips - 2):
        y_ahead, y_behind, sent = y_steps.send(down_grad)
        sums.append(sent)
    back = back_steps.send((down_grad, sums))[1]
    down_share = lax.psum_scatter(after(down_grad, back), "rep", scatter_dimension=1, tiled=True)

    logits = jnp.dot(normed_two, router_full, preferred_element_type=f32)
    router_prob = jax.nn.softmax(logits, axis=-1)
    picked_prob = jnp.sum(jnp.where(choose, router_prob[:, None, :], 0.0), axis=-1)
    prob_sum = jnp.sum(picked_prob, axis=-1, keepdims=True)
    all_tokens = tok_rows * lax.axis_size("rep") * groups
    fraction = counts / (TOP * all_tokens)

    grad_out = kept_grad.astype(f32)
    grad_gate = unpack_dgate(back[tok_rows:], tok_rows).T
    grad_norm_two = back[0:tok_rows]
    grad_picked = grad_gate / prob_sum - jnp.sum(
        grad_gate * picked_prob, axis=-1, keepdims=True
    ) / (prob_sum * prob_sum)
    grad_router_prob = (
        jnp.sum(jnp.where(choose, grad_picked[:, :, None], 0.0), axis=1)
        + aux_weight * experts * fraction / all_tokens
    )
    grad_logits = (
        router_prob
        * (grad_router_prob - jnp.sum(router_prob * grad_router_prob, axis=-1, keepdims=True))
    ).astype(jnp.bfloat16)
    router_grad = outer_sum(normed_two, grad_logits)
    grad_norm_two = grad_norm_two + back_proj(grad_logits, router_full)
    gain_two_grad = jnp.sum(grad_norm_two * (hidden_one * scale_two), axis=0)
    scaled_two = grad_norm_two * gain_two.astype(jnp.float32)
    grad_hidden_one = (
        grad_out
        + scale_two * scaled_two
        - hidden_one * scale_two**3 * jnp.mean(scaled_two * hidden_one, axis=-1, keepdims=True)
    )
    grad_attn = grad_hidden_one.astype(jnp.bfloat16)
    output_grad = outer_sum(context, grad_attn)
    grad_context = back_proj(grad_attn, output_full).astype(jnp.bfloat16)
    grad_query_rows, grad_key_rows, grad_value_rows, near_grad, far_grad = attend_back(
        query_rows, key_rows, value_rows, segments, base, context, grad_context, lse
    )
    grad_query_rows, grad_key_rows, grad_value_rows = after((grad_query_rows, grad_key_rows, grad_value_rows), y_behind)
    query_grad = outer_sum(normed_one, grad_query_rows)
    key_grad = outer_sum(normed_one, grad_key_rows)
    value_grad = outer_sum(normed_one, grad_value_rows)
    grad_norm_one = (
        back_proj(grad_query_rows, query_full)
        + back_proj(grad_key_rows, key_full)
        + back_proj(grad_value_rows, value_full)
    )
    gain_one_grad = jnp.sum(grad_norm_one * (inputs * scale_one), axis=0)
    scaled_one = grad_norm_one * gain_one.astype(jnp.float32)
    grad_input = (
        grad_hidden_one
        + scale_one * scaled_one
        - inputs * scale_one**3 * jnp.mean(scaled_one * inputs, axis=-1, keepdims=True)
    )
    table_grad = table_back(near_grad, far_grad, table_full.shape[0])
    def shares(x, rows):
        x = x.reshape(x.shape[:-2] + (groups, rows, x.shape[-1]))
        def one(k, core):
            return lax.dynamic_index_in_dim(x, 2 * group.source_chip(k) + core, x.ndim - 3, keepdims=False)
        return [one(k, group.core) for k in range(chips)], [one(k, 1 - group.core) for k in range(chips)]

    rows = width // groups
    dense = jnp.stack([query_grad, key_grad, value_grad, output_grad]).astype(bf16)
    dense_own, dense_sib = shares(dense, rows)

    def lanes(x):
        return jnp.pad(x, ((0, 0), (0, 0), (0, 128 - x.shape[2])))

    heads = table_grad.shape[1]
    bias_rows = table_grad.shape[0] // groups
    prob_row = jnp.broadcast_to(jnp.sum(router_prob, axis=0), (groups, 1, experts))
    small = jnp.concatenate([
        lanes(gain_one_grad.reshape(groups, 1, rows)), lanes(gain_two_grad.reshape(groups, 1, rows)),
        lanes(prob_row), lanes(table_grad.reshape(groups, bias_rows, heads)),
        lanes(jnp.transpose(router_grad.T.reshape(experts, groups, rows), (1, 0, 2))),
    ], axis=1)
    small = jnp.pad(small, ((0, 0), (0, -small.shape[1] % 8), (0, 0)))
    small_own, small_sib = shares(small.reshape(-1, 128), small.shape[1])
    lines = -(-small_own[0].size // width)

    def pack_sums(matrices, rest):
        rest = jnp.pad(rest.reshape(-1), (0, lines * width - rest.size)).reshape(lines, width)
        high = lax.reduce_precision(rest, 8, 7)
        parts = (matrices.reshape(-1, width), high, rest - high)
        return jnp.concatenate([part.astype(bf16) for part in parts], axis=0)

    def unpack_sums(block):
        block = block.astype(f32)
        rest = block[-2 * lines:-lines] + block[-lines:]
        return block[:-2 * lines].reshape(dense_own[0].shape), rest.reshape(-1)[:small_own[0].size].reshape(small_own[0].shape)

    up_share, down_share = up_share.astype(f32), down_share.astype(f32)
    arriving, pins = None, y_ahead
    for k in list(range(1, chips)) + [0]:
        other, rest = group.swap(dense_sib[k]), group.swap(small_sib[k])
        if pins is not None:
            other = after(other, pins)
        dense_sum = dense_own[k].astype(f32) + other.astype(f32)
        small_sum = small_own[k] + rest
        if arriving is not None:
            more, rest = unpack_sums(arriving)
            dense_sum, small_sum = dense_sum + more, small_sum + rest
        if k > 0:
            block = pack_sums(dense_sum, small_sum)
            arriving = group.onward(block)
        pins = (up_share, grad_input) if k == 1 else None
        if k == chips - 1:
            y_steps.send(block)
    mixed = y_steps.send(dense_sum)[2]
    output = (hidden_one + mixed).astype(bf16)

    def over_rep(x):
        count = lax.axis_size("rep")
        return x.astype(f32), [lax.ppermute(x, "rep", [(i, i ^ k) for i in range(count)]) for k in range(1, count)]

    reps = lax.axis_size("rep")
    small, small_moved = over_rep(small_sum)
    if reps == dense_sum.shape[0]:
        me = lax.axis_index("rep")
        sent = dense_sum.astype(bf16)

        def swap_with(k, x):
            return lax.ppermute(x, "rep", [(i, i ^ k) for i in range(reps)])

        mine = lax.dynamic_index_in_dim(dense_sum, me, 0, keepdims=False)
        for k in range(1, reps):
            mine = mine + swap_with(k, lax.dynamic_index_in_dim(sent, me ^ k, 0, keepdims=False)).astype(f32)
        mine = mine.astype(bf16)
        whole = jnp.stack([mine] + after([swap_with(k, mine) for k in range(1, reps)], output))
        dense = [lax.dynamic_index_in_dim(whole, me ^ m, 0, keepdims=False).astype(f32) for m in range(reps)]
    else:
        dense, dense_moved = over_rep(dense_sum.astype(bf16))
        for got in after(dense_moved, output):
            dense = dense + got.astype(f32)
    for also in small_moved:
        small = small + also
    at = 3 + bias_rows
    balance_terms = experts * experts * fraction * (small[2, 0:experts] / all_tokens)
    loss = aux_weight / experts * jnp.sum(balance_terms)
    return (
        output,
        loss,
        balance_terms,
        grad_input,
        small[0, 0:rows],
        dense[0],
        dense[1],
        dense[2],
        dense[3],
        small[3:at, 0:heads],
        small[1, 0:rows],
        small[at:at + experts, 0:rows].T,
        up_share,
        down_share,
    )


def solution(mesh):
    return jax.shard_map(
        shards,
        mesh=mesh,
        in_specs=(
            P(("rep", "grp"), None),
            P(("rep", "grp")),
            P(("rep", "grp"), None),
            P("grp"),
            P("grp", None),
            P("grp", None),
            P("grp", None),
            P("grp", None),
            P("grp", None),
            P("grp"),
            P("grp", None),
            P("grp", None, None),
            P("grp", None, None),
            P(("rep", "grp"), None),
        ),
        out_specs=(
            P(("rep", "grp"), None),
            P(),
            P(),
            P(("rep", "grp"), None),
            P("grp"),
            P("grp", None),
            P("grp", None),
            P("grp", None),
            P("grp", None),
            P("grp", None),
            P("grp"),
            P("grp", None),
            P("grp", "rep", None),
            P("grp", "rep", None),
        ),
        check_vma=False,
    )
```

```python
from functools import partial

import jax
import jax.numpy as jnp
from jax import lax
from jax.experimental import pallas as pl
from jax.experimental.pallas import tpu as pltpu
from jax.sharding import PartitionSpec as P

TOP = 2
QB = 128
PAIR = 128
NEAR = 2 * QB
SPAN = 3 * QB
OUT_OF_DOC = -1e30
FAR_MARKS = (18, 20, 23, 26, 30, 34, 39, 45, 51, 58, 66, 76, 86, 98, 112)
norm_eps = 1e-06
aux_weight = 0.01
f32, bf16 = jnp.float32, jnp.bfloat16


def after(x, *earlier):
    return lax.optimization_barrier((x, earlier))[0]


def rms_scale(values):
    return lax.rsqrt(jnp.mean(values * values, axis=-1, keepdims=True) + norm_eps)


def bucket_of(distance):
    far_part = jnp.zeros_like(distance)
    for far_mark in FAR_MARKS:
        far_part = far_part + (distance >= far_mark).astype(jnp.int32)
    return jnp.minimum(distance, 16) + far_part


def band_hot(buckets):
    lane = lax.broadcasted_iota(jnp.int32, (8, SPAN), 1)
    row = lax.broadcasted_iota(jnp.int32, (8, SPAN), 0)
    turn = (lane - row + SPAN) % SPAN
    diff = jnp.where(turn < QB, turn, turn - SPAN) + QB
    bucket = bucket_of(jnp.maximum(diff, 0)).reshape(1, 8 * SPAN)
    return bucket == lax.iota(jnp.int32, buckets)[:, None]


def split_pair(rows, low_lanes):
    zero = jnp.zeros_like(rows)
    return jnp.concatenate(
        [jnp.where(low_lanes, rows, zero), jnp.where(low_lanes, zero, rows)], axis=0
    )


def fill_mask(seg_col, seg_row, mask):
    seq = mask.shape[0]
    for i in range(seq // QB):
        length = (i + 1) * QB
        sk = seg_col[0:length, :]
        sq = seg_row[:, i * QB:(i + 1) * QB]
        kp = lax.broadcasted_iota(jnp.int32, (length, QB), 0)
        qp = lax.broadcasted_iota(jnp.int32, (length, QB), 1) + i * QB
        ok = (sk == sq) & (kp <= qp) & ((sq != 0) | (kp == qp))
        mask[0:length, i * QB:(i + 1) * QB] = jnp.where(ok, 0.0, OUT_OF_DOC).astype(f32)


def fill_near(base, near):
    for head in range(2):
        rows = base[head]
        for a in range(NEAR // 8):
            turned = rows if a == 0 else pltpu.roll(rows, 8 * a, 1)
            near[8 * a:8 * a + 8, head * QB:(head + 1) * QB] = turned[:, 0:QB]


def scores_chunk(k, lo, hi, qcat, mask, near, i):
    s = lax.dot_general(k[lo:hi, :], qcat, (((1,), (1,)), ((), ())), preferred_element_type=f32)
    m = mask[lo:hi, i * QB:(i + 1) * QB]
    s = s + jnp.concatenate([m, m], axis=1)
    start = (i - 1) * QB
    if lo >= start:
        s = s + near[lo - start:hi - start, :]
    return s


def fwd_kernel(base, seg_col, seg_row, q, k, v, ctx, lse, mask, near, scores, probs, v_t):
    seq = q.shape[0]

    @pl.when(pl.program_id(0) == 0)
    def _():
        fill_mask(seg_col, seg_row, mask)

    fill_near(base, near)
    v_t[...] = v[...].T
    low_lanes = lax.broadcasted_iota(jnp.int32, (QB, PAIR), 1) < PAIR // 2
    scale = (PAIR // 2) ** -0.5
    for i in range(seq // QB):
        qs = slice(i * QB, (i + 1) * QB)
        qcat = split_pair(q[qs, :] * jnp.asarray(scale, bf16), low_lanes)
        top = None
        for c in range(i + 1):
            s = scores_chunk(k, c * QB, (c + 1) * QB, qcat, mask, near, i)
            scores[c * QB:(c + 1) * QB, :] = s
            here = jnp.max(s.reshape(QB // 8, 8, NEAR), axis=0)
            top = here if top is None else jnp.maximum(top, here)
        top = jnp.max(top, axis=0, keepdims=True)
        total = jnp.zeros((8, NEAR), f32)
        for c in range(i + 1):
            p = jnp.exp(scores[c * QB:(c + 1) * QB, :] - top)
            total = total + jnp.sum(p.reshape(QB // 8, 8, NEAR), axis=0)
            probs[c * QB:(c + 1) * QB, :] = p.astype(bf16)
        total = jnp.sum(total, axis=0, keepdims=True)
        length = (i + 1) * QB
        out = jnp.dot(v_t[:, 0:length], probs[0:length, :], preferred_element_type=f32) / total
        half = PAIR // 2
        both = jnp.concatenate([out[0:half, 0:QB], out[half:PAIR, QB:NEAR]], axis=0)
        ctx[qs, :] = both.T.astype(bf16)
        lse[0, i:i + 1, :] = top + jnp.log(total)


def attend(q, k, v, seg, base):
    seq, width = q.shape
    pairs = width // PAIR
    col = pl.BlockSpec((seq, PAIR), lambda h: (0, h))
    whole = lambda *shape: pl.BlockSpec(shape, lambda h: (0,) * len(shape))
    return pl.pallas_call(
        fwd_kernel,
        grid=(pairs,),
        in_specs=[pl.BlockSpec((2, 8, SPAN), lambda h: (h, 0, 0)), whole(seq, 1), whole(1, seq), col, col, col],
        out_specs=[col, pl.BlockSpec((1, seq // QB, NEAR), lambda h: (h, 0, 0))],
        out_shape=[
            jax.ShapeDtypeStruct((seq, width), bf16),
            jax.ShapeDtypeStruct((pairs, seq // QB, NEAR), f32),
        ],
        scratch_shapes=[
            pltpu.VMEM((seq, seq), f32),
            pltpu.VMEM((NEAR, NEAR), f32),
            pltpu.VMEM((seq, NEAR), f32),
            pltpu.VMEM((seq, NEAR), bf16),
            pltpu.VMEM((PAIR, seq), bf16),
        ],
        compiler_params=pltpu.CompilerParams(vmem_limit_bytes=32 * 1024 * 1024),
        cost_estimate=pl.CostEstimate(flops=1, bytes_accessed=1024, transcendentals=0),
        name="attend",
    )(base, seg.reshape(seq, 1), seg.reshape(1, seq), q, k, v)


def bwd_kernel(base, seg_col, seg_row, q, k, v, ctx, dctx, lse, dq, dk, dv, dnear, dfar,
               mask, near, ds_all, p_all, k_t, dk_sum, dv_sum, dnear_sum, dfar_sum):
    seq = q.shape[0]

    @pl.when(pl.program_id(0) == 0)
    def _():
        fill_mask(seg_col, seg_row, mask)

    fill_near(base, near)
    k_t[...] = k[...].T
    low_lanes = lax.broadcasted_iota(jnp.int32, (QB, PAIR), 1) < PAIR // 2
    half = PAIR // 2
    scale = half ** -0.5
    dnear_sum[...] = jnp.zeros_like(dnear_sum)
    dfar_sum[...] = jnp.zeros_like(dfar_sum)
    for i in reversed(range(seq // QB)):
        qs = slice(i * QB, (i + 1) * QB)
        length = (i + 1) * QB
        qcat = split_pair(q[qs, :] * jnp.asarray(scale, bf16), low_lanes)
        dcat = split_pair(dctx[qs, :], low_lanes)
        dots = (ctx[qs, :].astype(f32) * dctx[qs, :].astype(f32)).T
        centre = jnp.concatenate(
            [jnp.sum(dots[0:half], axis=0, keepdims=True), jnp.sum(dots[half:], axis=0, keepdims=True)], axis=1
        )
        norm = lse[0, i:i + 1, :]
        for c in range(i + 1):
            lo, hi = c * QB, (c + 1) * QB
            s = scores_chunk(k, lo, hi, qcat, mask, near, i)
            p = jnp.exp(s - norm)
            p_all[lo:hi, :] = p.astype(bf16)
            dp = lax.dot_general(v[lo:hi, :], dcat, (((1,), (1,)), ((), ())), preferred_element_type=f32)
            ds = p * (dp - centre)
            ds_all[lo:hi, :] = ds.astype(bf16)
            start = (i - 1) * QB
            if lo >= start:
                dnear_sum[lo - start:hi - start, :] += ds
            else:
                dfar_sum[...] += jnp.sum(ds.reshape(QB // 8, 8, NEAR), axis=0)
        out = jnp.dot(k_t[:, 0:length], ds_all[0:length, :], preferred_element_type=f32)
        both = jnp.concatenate([out[0:half, 0:QB], out[half:PAIR, QB:NEAR]], axis=0)
        dq[qs, :] = (both.T * scale).astype(bf16)
        dk_part = jnp.dot(ds_all[0:length, :], qcat, preferred_element_type=f32)
        dv_part = jnp.dot(p_all[0:length, :], dcat, preferred_element_type=f32)
        if i == seq // QB - 1:
            dk_sum[0:length, :] = dk_part
            dv_sum[0:length, :] = dv_part
        else:
            dk_sum[0:length, :] += dk_part
            dv_sum[0:length, :] += dv_part
    dk[...] = dk_sum[...].astype(bf16)
    dv[...] = dv_sum[...].astype(bf16)
    for head in range(2):
        total = jnp.zeros((8, SPAN), f32)
        for a in range(NEAR // 8):
            rows = dnear_sum[8 * a:8 * a + 8, head * QB:(head + 1) * QB]
            rows = jnp.concatenate([rows, jnp.zeros((8, SPAN - QB), f32)], axis=1)
            total = total + (rows if a == 0 else pltpu.roll(rows, SPAN - 8 * a, 1))
        dnear[head] = total
    dfar[0] = dfar_sum[...]


def attend_back(q, k, v, seg, base, ctx, dctx, lse):
    seq, width = q.shape
    pairs = width // PAIR
    col = pl.BlockSpec((seq, PAIR), lambda h: (0, h))
    band = pl.BlockSpec((2, 8, SPAN), lambda h: (h, 0, 0))
    whole = lambda *shape: pl.BlockSpec(shape, lambda h: (0,) * len(shape))
    rows = jax.ShapeDtypeStruct((seq, width), bf16)
    return pl.pallas_call(
        bwd_kernel,
        grid=(pairs,),
        in_specs=[band, whole(seq, 1), whole(1, seq), col, col, col, col, col,
                  pl.BlockSpec((1, seq // QB, NEAR), lambda h: (h, 0, 0))],
        out_specs=[col, col, col, band, pl.BlockSpec((1, 8, NEAR), lambda h: (h, 0, 0))],
        out_shape=[rows, rows, rows, jax.ShapeDtypeStruct((2 * pairs, 8, SPAN), f32),
                   jax.ShapeDtypeStruct((pairs, 8, NEAR), f32)],
        scratch_shapes=[
            pltpu.VMEM((seq, seq), f32),
            pltpu.VMEM((NEAR, NEAR), f32),
            pltpu.VMEM((seq, NEAR), bf16),
            pltpu.VMEM((seq, NEAR), bf16),
            pltpu.VMEM((PAIR, seq), bf16),
            pltpu.VMEM((seq, PAIR), f32),
            pltpu.VMEM((seq, PAIR), f32),
            pltpu.VMEM((NEAR, NEAR), f32),
            pltpu.VMEM((8, NEAR), f32),
        ],
        compiler_params=pltpu.CompilerParams(vmem_limit_bytes=40 * 1024 * 1024),
        cost_estimate=pl.CostEstimate(flops=1, bytes_accessed=1024, transcendentals=0),
        name="attend_back",
    )(base, seg.reshape(seq, 1), seg.reshape(1, seq), q, k, v, ctx, dctx, lse)


def bias_base(table):
    buckets, heads = table.shape
    hot = band_hot(buckets).astype(bf16)
    base = lax.dot_general(table, hot, (((0,), (0,)), ((), ())), preferred_element_type=f32)
    last = table[buckets - 1].astype(f32)
    return base.reshape(heads, 8, SPAN) - last[:, None, None]


def table_back(dnear, dfar, buckets):
    heads = dnear.shape[0]
    hot = band_hot(buckets).astype(f32)
    grad = lax.dot_general(hot, dnear.reshape(heads, 8 * SPAN), (((1,), (1,)), ((), ())),
                           preferred_element_type=f32, precision=lax.Precision.HIGHEST)
    far = jnp.sum(dfar.reshape(heads // 2, 8, 2, QB), axis=(1, 3)).reshape(1, heads)
    last = (lax.iota(jnp.int32, buckets) == buckets - 1)[:, None]
    return grad + jnp.where(last, far, 0.0)


def gelu_and_slope(u):
    root = (2.0 / jnp.pi) ** 0.5
    square = u * u
    bent = jnp.tanh(u * (root + (root * 0.044715) * square))
    rise = 0.5 + 0.5 * bent
    slope = rise + (0.5 * u) * (1.0 - bent * bent) * (root + (root * 3 * 0.044715) * square)
    return u * rise, slope


def expert_kernel(first, n_a, n_b, g_a, g_b, info, router_t, w_in, w_out, *rest):
    (y_a, y_b, r_a, r_b, act_out, dpre_out, x_out, dy_out,
     hot, x_s, g_s, dy_s, gate_s, y_sum, d_sum, yd_all, gates, dgate_c) = rest[-18:]
    e, f = pl.program_id(0), pl.program_id(1)
    rows, width = n_a.shape
    cap = x_s.shape[0] // 2
    expert = first[0] + e
    sources = ((n_a, g_a), (n_b, g_b))

    @pl.when((e == 0) & (f == 0))
    def _():
        dgate_c[...] = jnp.zeros_like(dgate_c)
        for s, (n_ref, g_ref) in enumerate(sources):
            logits = lax.dot_general(router_t[...], n_ref[...], (((1,), (1,)), ((), ())), preferred_element_type=f32)
            ids = lax.broadcasted_iota(jnp.int32, logits.shape, 0)
            power = jnp.exp(logits - jnp.max(logits, axis=0, keepdims=True))
            prob = power / jnp.sum(power, axis=0, keepdims=True)
            chosen = (ids == info[4 * s + 2:4 * s + 3, :]) | (ids == info[4 * s + 3:4 * s + 4, :])
            both = jnp.sum(jnp.where(chosen, prob, 0.0), axis=0, keepdims=True)
            gates[s] = prob / both

    @pl.when(f == 0)
    def _():
        for s, (n_ref, g_ref) in enumerate(sources):
            ids = lax.broadcasted_iota(jnp.int32, gates.shape[1:], 0)
            gate_row = jnp.sum(jnp.where(ids == expert, gates[s], 0.0), axis=0, keepdims=True)
            slot_row = jnp.where(e == 0, info[4 * s:4 * s + 1, :], info[4 * s + 1:4 * s + 2, :])
            match = slot_row == lax.broadcasted_iota(jnp.int32, (cap, rows), 0)
            one_hot = jnp.where(match, 1.0, 0.0).astype(bf16)
            part = slice(s * cap, (s + 1) * cap)
            gate_s[part, :] = jnp.sum(jnp.where(match, gate_row, 0.0), axis=1, keepdims=True)
            hot[s, pl.ds(pl.multiple_of(e * cap, cap), cap), :] = one_hot
            x_s[part, :] = jnp.dot(one_hot, n_ref[...], preferred_element_type=f32).astype(bf16)
            g_rows = jnp.dot(one_hot, g_ref[...], preferred_element_type=f32)
            g_s[part, :] = g_rows.astype(bf16)
            dy_s[part, :] = (gate_s[part, :] * g_rows).astype(bf16)
        y_sum[...] = jnp.zeros_like(y_sum)
        d_sum[...] = jnp.zeros_like(d_sum)
        x_out[0] = x_s[...]
        dy_out[0] = dy_s[...]

    pre = jnp.dot(x_s[...], w_in[0], preferred_element_type=f32)
    dact = lax.dot_general(dy_s[...], w_out[0], (((1,), (1,)), ((), ())), preferred_element_type=f32)
    act, slope = gelu_and_slope(pre)
    act_out[0] = act.astype(bf16)
    dpre_out[0] = (dact * slope).astype(bf16)
    y_sum[...] += jnp.dot(act_out[0], w_out[0], preferred_element_type=f32)
    d_sum[...] += lax.dot_general(dpre_out[0], w_in[0], (((1,), (1,)), ((), ())), preferred_element_type=f32)

    @pl.when(f == pl.num_programs(1) - 1)
    def _():
        y_rows = y_sum[...].astype(bf16).astype(f32)
        dgate = jnp.sum(y_rows * g_s[...].astype(f32), axis=1, keepdims=True)
        y_rows = (gate_s[...] * y_rows).astype(bf16)
        d_rows = d_sum[...].astype(bf16)
        for s in range(2):
            part = slice(s * cap, (s + 1) * cap)
            here = pl.ds(pl.multiple_of(e * cap, cap), cap)
            yd_all[s, here, 0:width] = y_rows[part]
            yd_all[s, here, width:] = d_rows[part]
            slot_row = jnp.where(e == 0, info[4 * s:4 * s + 1, :], info[4 * s + 1:4 * s + 2, :])
            match = slot_row == lax.broadcasted_iota(jnp.int32, (cap, rows), 0)
            row = jnp.sum(jnp.where(match, dgate[part], 0.0), axis=0, keepdims=True)
            for c in range(TOP):
                routed = info[4 * s + 2 + c:4 * s + 3 + c, :] == expert
                dgate_c[TOP * s + c:TOP * s + c + 1, :] += jnp.where(routed, row, 0.0)

    @pl.when((e == pl.num_programs(0) - 1) & (f == pl.num_programs(1) - 1))
    def _():
        turn = (((0,), (0,)), ((), ()))
        for s, (y_ref, r_ref) in enumerate(((y_a, r_a), (y_b, r_b))):
            sums = lax.dot_general(hot[s], yd_all[s], turn, preferred_element_type=f32).astype(bf16)
            y_ref[...] = sums[:, 0:width]
            r_ref[0:rows, :] = sums[:, width:]
            value = dgate_c[TOP * s:TOP * s + TOP, :]
            high = value.astype(bf16)
            value = value - high.astype(f32)
            middle = value.astype(bf16)
            low = (value - middle.astype(f32)).astype(bf16)
            pieces = jnp.concatenate([high.astype(f32), middle.astype(f32), low.astype(f32), jnp.zeros((2, rows), f32)], axis=0)
            over = jnp.concatenate([pieces[:, width:], jnp.zeros((8, 2 * width - rows), f32)], axis=1)
            r_ref[rows:rows + 16, :] = jnp.concatenate([pieces[:, 0:width], over], axis=0).astype(bf16)


def unpack_dgate(tail, rows):
    tail = tail.astype(f32)
    pieces = jnp.concatenate([tail[0:8], tail[8:16]], axis=1)[:, 0:rows]
    return pieces[0:2] + pieces[2:4] + pieces[4:6]


def expert_block(k, blocks, first, n_a, n_b, g_a, g_b, info, router_t, w_in, w_out, cap, kept):
    rows, width = n_a.shape
    local, _, hidden = w_in.shape
    part = 768 if hidden % 768 == 0 else hidden
    once = pl.Buffered(1)
    whole = lambda *shape: pl.BlockSpec(shape, lambda e, f: (0,) * len(shape), pipeline_mode=once)
    wide = pl.BlockSpec((1, 2 * cap, part), lambda e, f: (e, k, f))
    slim = pl.BlockSpec((1, 2 * cap, width), lambda e, f: (e, k, 0))
    slots = blocks * 2 * cap
    shapes = [
        jax.ShapeDtypeStruct((rows, width), bf16), jax.ShapeDtypeStruct((rows, width), bf16),
        jax.ShapeDtypeStruct((rows + 16, width), bf16), jax.ShapeDtypeStruct((rows + 16, width), bf16),
        jax.ShapeDtypeStruct((local, slots, hidden), bf16), jax.ShapeDtypeStruct((local, slots, hidden), bf16),
        jax.ShapeDtypeStruct((local, slots, width), bf16), jax.ShapeDtypeStruct((local, slots, width), bf16),
    ]
    in_specs = [
        pl.BlockSpec(memory_space=pltpu.SMEM), whole(rows, width), whole(rows, width), whole(rows, width), whole(rows, width),
        whole(8, rows), whole(*router_t.shape),
        pl.BlockSpec((1, width, part), lambda e, f: (e, 0, f)), pl.BlockSpec((1, part, width), lambda e, f: (e, f, 0)),
    ]
    args = [first, n_a, n_b, g_a, g_b, info, router_t, w_in, w_out]
    alias = {}
    if kept is not None:
        alias = {len(args) + i: 4 + i for i in range(4)}
        in_specs += [pl.BlockSpec(memory_space=pl.ANY)] * 4
        args += list(kept)
    out = pl.pallas_call(
        expert_kernel,
        grid=(local, hidden // part),
        in_specs=in_specs,
        out_specs=[whole(rows, width), whole(rows, width), whole(rows + 16, width), whole(rows + 16, width), wide, wide, slim, slim],
        out_shape=shapes,
        scratch_shapes=[
            pltpu.VMEM((2, local * cap, rows), bf16),
            pltpu.VMEM((2 * cap, width), bf16), pltpu.VMEM((2 * cap, width), bf16), pltpu.VMEM((2 * cap, width), bf16),
            pltpu.VMEM((2 * cap, 1), f32),
            pltpu.VMEM((2 * cap, width), f32), pltpu.VMEM((2 * cap, width), f32),
            pltpu.VMEM((2, local * cap, 2 * width), bf16), pltpu.VMEM((2,) + (router_t.shape[0], rows), f32),
            pltpu.VMEM((8, rows), f32),
        ],
        input_output_aliases=alias,
        compiler_params=pltpu.CompilerParams(vmem_limit_bytes=48 * 1024 * 1024),
        cost_estimate=pl.CostEstimate(flops=2 * local * cap * (8 * width * hidden + 8 * width * rows), bytes_accessed=60 * 1024 * 1024, transcendentals=2 * local * cap * hidden),
        name="expert_block",
    )(*args)
    return out[:4], out[4:]


def chip_ring(chips):
    return [0] + list(range(1, chips, 2)) + [z for z in range(chips - 1, 0, -1) if z % 2 == 0]


class Group:
    def __init__(self):
        self.size = lax.axis_size("grp")
        self.chips = self.size // 2
        self.order = chip_ring(self.chips)
        me = lax.axis_index("grp")
        self.me, self.chip, self.core = me, me // 2, me % 2

    def onward(self, x):
        pairs = []
        for i, z in enumerate(self.order):
            after = self.order[(i + 1) % self.chips]
            pairs += [(2 * z, 2 * after), (2 * z + 1, 2 * after + 1)]
        return lax.ppermute(x, "grp", pairs)

    def backward(self, x):
        pairs = []
        for i, z in enumerate(self.order):
            before = self.order[(i - 1) % self.chips]
            pairs += [(2 * z, 2 * before), (2 * z + 1, 2 * before + 1)]
        return lax.ppermute(x, "grp", pairs)

    def swap(self, x):
        return lax.ppermute(x, "grp", [(i, i ^ 1) for i in range(self.size)])

    def source_chip(self, k):
        table = [0] * self.chips
        for i, z in enumerate(self.order):
            table[z] = self.order[(i - k) % self.chips]
        return jnp.asarray(table, jnp.int32)[self.chip]


def pick_constant(table, index):
    value = jnp.int32(table[0])
    for i in range(1, len(table)):
        value = jnp.where(index == i, jnp.int32(table[i]), value)
    return value


def gather_kernel(chips, reps, stack, small, tally, stack_all, small_all, tally_all,
                  own_sem, ring_send, ring_recv, core_send, core_recv, own_send, own_recv,
                  plane_send, plane_recv, cross_send, cross_recv, rep_send, rep_recv, tally_in, tally_sum, tally_vmem):
    order = chip_ring(chips)
    mats, rows = stack.shape[0], stack.shape[1]
    rep, me = lax.axis_index("rep"), lax.axis_index("grp")
    chip, core = me // 2, me % 2
    mine = lax.rem(rep, mats)
    after_z, before_z = [0] * chips, [0] * chips
    for i, z in enumerate(order):
        after_z[z], before_z[z] = order[(i + 1) % chips], order[(i - 1) % chips]
    onward = 2 * pick_constant(after_z, chip) + core
    before = 2 * pick_constant(before_z, chip) + core
    sibling = 2 * chip + 1 - core
    mesh_id = pl.DeviceIdType.MESH
    plane = [(rep - mine) + lax.rem(mine + j, mats) for j in range(1, mats)]

    barrier = pltpu.get_barrier_semaphore()
    peers = [(rep, onward), (rep, before), (rep, sibling)] + [(lax.rem(rep + k, reps), me) for k in range(1, reps)]
    for peer in peers:
        pl.semaphore_signal(barrier, inc=1, device_id=peer, device_id_type=mesh_id)
    pl.semaphore_wait(barrier, len(peers))

    def remote(src, dst, send, recv, target):
        return pltpu.make_async_remote_copy(
            src_ref=src, dst_ref=dst, send_sem=send, recv_sem=recv, device_id=target, device_id_type=mesh_id
        )

    def owner_of(k, which_core):
        source = [0] * chips
        for i, z in enumerate(order):
            source[z] = order[(i - k) % chips]
        return 2 * pick_constant(source, chip) + which_core

    def shard(mat, owner):
        return stack_all.at[mat, pl.ds(pl.multiple_of(owner * rows, rows), rows), :]

    def places(k, which_core):
        owner = owner_of(k, which_core)
        return [shard(mine, owner), small_all.at[owner], tally_all.at[owner]]

    def matrix(j):
        return lax.rem(mine + j, mats)

    sent = []

    def start(copy):
        copy.start()
        sent.append(copy)
        return copy

    tallies = [
        start(remote(tally, tally_in.at[k - 1], rep_send.at[k - 1], rep_recv.at[k - 1], (lax.rem(rep + k, reps), me)))
        for k in range(1, reps)
    ]
    own = [
        pltpu.make_async_copy(stack, stack_all.at[:, pl.ds(pl.multiple_of(me * rows, rows), rows), :], own_sem.at[0]),
        pltpu.make_async_copy(small, small_all.at[me], own_sem.at[1]),
        pltpu.make_async_copy(tally, tally_vmem, own_sem.at[2]),
    ]
    for copy in own:
        copy.start()
    here = places(0, core)
    moved = [
        start(remote(stack.at[mine], here[0], ring_send.at[0, 0], ring_recv.at[0, 0], (rep, onward))),
        start(remote(small, here[1], ring_send.at[0, 1], ring_recv.at[0, 1], (rep, onward))),
    ]
    everywhere = stack_all.at[:, pl.ds(pl.multiple_of(me * rows, rows), rows), :]
    start(remote(small, here[1], core_send.at[0, 1], core_recv.at[0, 1], (rep, sibling)))
    start(remote(stack, everywhere, own_send, own_recv, (rep, sibling)))
    own[2].wait()
    total = tally_vmem[...]
    for k, copy in enumerate(tallies):
        copy.wait_recv()
        total = total + tally_in[k]
    tally_sum[...] = total
    keep = pltpu.make_async_copy(tally_sum, here[2], own_sem.at[3])
    keep.start()
    own = [own[0], own[1], keep]
    moved.append(start(remote(tally_sum, here[2], ring_send.at[0, 2], ring_recv.at[0, 2], (rep, onward))))
    start(remote(tally_sum, here[2], core_send.at[0, 2], core_recv.at[0, 2], (rep, sibling)))

    def pass_across(k):
        for j in range(1, mats):
            block = shard(matrix(j), owner_of(k, core))
            remote(block, block, plane_send.at[k, j - 1], plane_recv.at[k, mats - 1 - j], (plane[j - 1], me)).wait_recv()
            start(remote(block, block, cross_send.at[k, mats - 1 - j], cross_recv.at[k, j - 1], (rep, sibling)))

    for k in range(1, chips):
        here = places(k, core)
        for a in range(3):
            moved[a].wait_recv()
            if k < chips - 1:
                moved[a] = start(remote(here[a], here[a], ring_send.at[k, a], ring_recv.at[k, a], (rep, onward)))
            if a == 0:
                for j in range(1, mats):
                    start(remote(here[0], here[0], plane_send.at[k, j - 1], plane_recv.at[k, j - 1], (plane[j - 1], me)))
            start(remote(here[a], here[a], core_send.at[k, a], core_recv.at[k, a], (rep, sibling)))
        if k > 1:
            pass_across(k - 1)
    pass_across(chips - 1)
    for copy in sent:
        copy.wait_send()
    for copy in own:
        copy.wait()
    other = stack_all.at[:, pl.ds(pl.multiple_of(sibling * rows, rows), rows), :]
    remote(stack, other, own_send, own_recv, (rep, sibling)).wait_recv()
    for k in range(chips):
        there = places(k, 1 - core)
        for a in range(3):
            if a > 0 or k > 0:
                remote(there[a], there[a], core_send.at[k, a], core_recv.at[k, a], (rep, sibling)).wait_recv()
        if k > 0:
            for j in range(1, mats):
                block = shard(matrix(j), owner_of(k, 1 - core))
                remote(block, block, cross_send.at[k, j - 1], cross_recv.at[k, j - 1], (rep, sibling)).wait_recv()


def gather_group(stack, small, tally):
    size, reps = lax.axis_size("grp"), lax.axis_size("rep")
    chips = size // 2
    mats, rows, width = stack.shape
    hbm = pl.BlockSpec(memory_space=pl.ANY)
    dma = pltpu.SemaphoreType.DMA
    return pl.pallas_call(
        partial(gather_kernel, chips, reps),
        in_specs=[hbm] * 3,
        out_specs=[hbm] * 3,
        out_shape=[
            jax.ShapeDtypeStruct((mats, size * rows, width), stack.dtype),
            jax.ShapeDtypeStruct((size,) + small.shape, small.dtype),
            jax.ShapeDtypeStruct((size,) + tally.shape, f32),
        ],
        scratch_shapes=[
            dma((4,)), dma((chips, 3)), dma((chips, 3)), dma((chips, 3)), dma((chips, 3)), dma, dma,
            dma((chips, mats - 1)), dma((chips, mats - 1)), dma((chips, mats - 1)), dma((chips, mats - 1)),
            dma((reps,)), dma((reps,)),
            pltpu.VMEM((reps - 1,) + tally.shape, f32), pltpu.VMEM(tally.shape, f32), pltpu.VMEM(tally.shape, f32),
        ],
        compiler_params=pltpu.CompilerParams(collective_id=0, has_side_effects=True),
        cost_estimate=pl.CostEstimate(flops=0, bytes_accessed=16 * 1024 * 1024, transcendentals=0),
        name="gather_group",
    )(stack, small, tally)


def pack_small(gain_attn, gain_ffn, router, rel_bias, routes):
    def lanes(x):
        return jnp.pad(x, ((0, 0), (0, 128 - x.shape[1])))

    rows = jnp.concatenate([
        lanes(gain_attn[None]), lanes(gain_ffn[None]), lanes(rel_bias), lanes(router.T),
        routes.T.astype(bf16).reshape(-1, 128),
    ], axis=0)
    return jnp.pad(rows, ((0, -rows.shape[0] % 16), (0, 0)))


def unpack_small(packed, size, shard, bias_rows, heads, experts, tokens):
    blocks = packed.reshape(size, -1, 128)
    gain_one = blocks[:, 0, 0:shard].reshape(-1)
    gain_two = blocks[:, 1, 0:shard].reshape(-1)
    at = 2 + bias_rows
    table = blocks[:, 2:at, 0:heads].reshape(-1, heads)
    router_t = jnp.transpose(blocks[:, at:at + experts, 0:shard], (1, 0, 2)).reshape(experts, -1)
    at += experts
    routes = blocks[:, at:at + TOP * tokens // 128].reshape(size, TOP, tokens).astype(jnp.int32)
    return gain_one, gain_two, table, router_t, routes


def outer_sum(left_rows, right_rows):
    return lax.dot_general(
        left_rows, right_rows, (((0,), (0,)), ((), ())), preferred_element_type=jnp.float32
    )


def back_proj(grad_rows, weight):
    return lax.dot_general(
        grad_rows, weight, (((1,), (1,)), ((), ())), preferred_element_type=jnp.float32
    )


def reduce_steps(group, own, sibling, sent_as=bf16):
    moving, total = None, None
    for k in list(range(1, group.chips)) + [0]:
        pins = yield moving, total
        other = group.swap(sibling[k].astype(sent_as))
        if pins is not None:
            other, moving = after((other, moving), pins)
        total = own[k].astype(f32) + other.astype(f32)
        if moving is not None:
            total = total + moving.astype(f32)
        if k != 0:
            total = total.astype(sent_as)
            moving = group.onward(total)
    yield moving, total


def reduce_both_ways(group, own, sibling):
    half = group.chips // 2
    ahead, behind, total = None, None, None
    for k in list(range(half - 1, 0, -1)) + list(range(half, group.chips)) + [0]:
        pins = yield ahead, behind, total
        other = group.swap(sibling[k])
        if k >= half:
            other, ahead = after((other, ahead), pins)
            arrived = [ahead]
        elif k > 0:
            other, behind = after((other, behind), pins)
            arrived = [behind]
        else:
            other, ahead, behind = after((other, ahead, behind), pins)
            arrived = [ahead, behind]
        total = own[k].astype(f32) + other.astype(f32)
        for block in arrived:
            if block is not None:
                total = total + block.astype(f32)
        if k > 0:
            total = total.astype(bf16)
        if k >= half:
            ahead = group.onward(total)
        elif k > 0:
            behind = group.backward(total)
    yield ahead, behind, total


def local_slots(routes_all, first, local):
    ids = first + lax.iota(jnp.int32, local)
    hot = jnp.any(routes_all[:, None, :, :] == ids[None, :, None, None], axis=2).astype(jnp.int32)
    return jnp.where(hot != 0, jnp.cumsum(hot, axis=2) - hot, -1)


def shards(
    tokens,
    segments,
    routes,
    gain_attn,
    w_query,
    w_key,
    w_value,
    w_output,
    rel_bias,
    gain_ffn,
    router,
    w_in,
    w_out,
    cotangent,
):
    group = Group()
    tok_rows, width = tokens.shape
    exp_local = w_in.shape[0]
    groups = group.size
    experts = exp_local * groups
    capacity = 2 * tok_rows * TOP // experts
    choose = routes[:, :, None] == lax.iota(jnp.int32, experts)[None, None, :]
    tally = jnp.pad(jnp.sum(choose.astype(f32), axis=(0, 1))[None], ((0, 7), (0, 128 - experts)))
    small = pack_small(gain_attn, gain_ffn, router, rel_bias, routes)
    stack_all, small_all, tally_all = gather_group(jnp.stack([w_query, w_key, w_value, w_output]), small, tally)
    query_full, key_full, value_full, output_full = [stack_all[m] for m in range(4)]
    gain_one, gain_two, table_full, router_t, routes_all = unpack_small(
        small_all, groups, gain_attn.shape[0], rel_bias.shape[0], rel_bias.shape[1], experts, tok_rows
    )
    router_full = router_t.T
    counts = jnp.sum(tally_all[:, 0, 0:experts], axis=0)
    first = (group.me * exp_local).astype(jnp.int32)

    kept_grad = jnp.where((segments != 0)[:, None], cotangent, jnp.zeros_like(cotangent))
    grad_ring = [kept_grad]
    for k in range(1, group.chips - 1):
        grad_ring.append(group.onward(grad_ring[-1]))
    grad_ring.append(group.backward(after(kept_grad, small_all)))
    slots_all = local_slots(after(routes_all, grad_ring[1]), first, exp_local)

    inputs = tokens.astype(f32)
    scale_one = rms_scale(inputs)
    normed_one = (inputs * scale_one * gain_one.astype(f32)).astype(bf16)
    normed_one = after(normed_one, grad_ring[1])
    query_rows = jnp.dot(normed_one, query_full, preferred_element_type=f32).astype(bf16)
    key_rows = jnp.dot(normed_one, key_full, preferred_element_type=f32).astype(bf16)
    value_rows = jnp.dot(normed_one, value_full, preferred_element_type=f32).astype(bf16)
    base = bias_base(table_full)
    context, lse = attend(query_rows, key_rows, value_rows, after(segments, slots_all), base)
    context = after(context, grad_ring[-1])
    hidden_one = inputs + jnp.dot(context, output_full, preferred_element_type=f32)
    scale_two = rms_scale(hidden_one)
    normed_two = (hidden_one * scale_two * gain_two.astype(f32)).astype(bf16)

    kept = None
    results = []
    sibs = [group.swap(block) for block in grad_ring[:3]]
    ring = list(grad_ring)
    norm_ring = [normed_two]
    for k in range(group.chips):
        if k >= 3:
            sibs.append(group.swap(after(ring[k], results[k - 3][2])))
        norm_now = norm_ring[k]
        norm_sib = group.swap(norm_now)
        if k < group.chips - 1:
            moved = group.onward(norm_now)
        chip = group.source_chip(k)
        info = jnp.concatenate(
            [
                lax.dynamic_index_in_dim(rows, 2 * chip + core, 0, keepdims=False)
                for core in (group.core, 1 - group.core)
                for rows in (slots_all, routes_all)
            ],
            axis=0,
        )
        if k == 1:
            info = after(info, ring[2])
        if k == group.chips - 1:
            back_own, back_sib = [r[2] for r in results], [r[3] for r in results]
            back_steps = reduce_steps(group, back_own, back_sib)
            next(back_steps)
            sent = back_steps.send(None)[1]
            info = after(info, sent)
        outs, kept = expert_block(
            k, group.chips, first.reshape(1), norm_now, norm_sib, ring[k], sibs[k],
            info, router_t, w_in, w_out, capacity, kept,
        )
        results.append(outs)
        if k == group.chips - 1:
            back_own.append(outs[2])
            back_sib.append(outs[3])
        if k < group.chips - 1:
            norm_ring.append(after(moved, outs[2]))

    act_all, dpre_all, x_all, dy_all = kept
    chips = group.chips
    for k in range(2, chips - 1):
        sent = back_steps.send(outs[2])[1]
    up_grad = jnp.einsum("ekd,ekf->edf", after(x_all, sent), dpre_all, preferred_element_type=f32).astype(bf16)
    sent = back_steps.send(up_grad)[1]
    up_share = lax.psum_scatter(after(up_grad, sent), "rep", scatter_dimension=1, tiled=True)
    down_grad = jnp.einsum("ekf,ekd->efd", act_all, after(dy_all, sent), preferred_element_type=f32).astype(bf16)

    y_steps = reduce_both_ways(group, [r[0] for r in results], [r[1] for r in results])
    next(y_steps)
    sums = []
    for k in range(chips - 2):
        y_ahead, y_behind, sent = y_steps.send(down_grad)
        sums.append(sent)
    back = back_steps.send((down_grad, sums))[1]
    down_share = lax.psum_scatter(after(down_grad, back), "rep", scatter_dimension=1, tiled=True)

    logits = jnp.dot(normed_two, router_full, preferred_element_type=f32)
    router_prob = jax.nn.softmax(logits, axis=-1)
    picked_prob = jnp.sum(jnp.where(choose, router_prob[:, None, :], 0.0), axis=-1)
    prob_sum = jnp.sum(picked_prob, axis=-1, keepdims=True)
    all_tokens = tok_rows * lax.axis_size("rep") * groups
    fraction = counts / (TOP * all_tokens)

    grad_out = kept_grad.astype(f32)
    grad_gate = unpack_dgate(back[tok_rows:], tok_rows).T
    grad_norm_two = back[0:tok_rows]
    grad_picked = grad_gate / prob_sum - jnp.sum(
        grad_gate * picked_prob, axis=-1, keepdims=True
    ) / (prob_sum * prob_sum)
    grad_router_prob = (
        jnp.sum(jnp.where(choose, grad_picked[:, :, None], 0.0), axis=1)
        + aux_weight * experts * fraction / all_tokens
    )
    grad_logits = (
        router_prob
        * (grad_router_prob - jnp.sum(router_prob * grad_router_prob, axis=-1, keepdims=True))
    ).astype(jnp.bfloat16)
    router_grad = outer_sum(normed_two, grad_logits)
    grad_norm_two = grad_norm_two + back_proj(grad_logits, router_full)
    gain_two_grad = jnp.sum(grad_norm_two * (hidden_one * scale_two), axis=0)
    scaled_two = grad_norm_two * gain_two.astype(jnp.float32)
    grad_hidden_one = (
        grad_out
        + scale_two * scaled_two
        - hidden_one * scale_two**3 * jnp.mean(scaled_two * hidden_one, axis=-1, keepdims=True)
    )
    grad_attn = grad_hidden_one.astype(jnp.bfloat16)
    output_grad = outer_sum(context, grad_attn)
    grad_context = back_proj(grad_attn, output_full).astype(jnp.bfloat16)
    grad_query_rows, grad_key_rows, grad_value_rows, near_grad, far_grad = attend_back(
        query_rows, key_rows, value_rows, segments, base, context, grad_context, lse
    )
    grad_query_rows, grad_key_rows, grad_value_rows = after((grad_query_rows, grad_key_rows, grad_value_rows), y_behind)
    query_grad = outer_sum(normed_one, grad_query_rows)
    key_grad = outer_sum(normed_one, grad_key_rows)
    value_grad = outer_sum(normed_one, grad_value_rows)
    grad_norm_one = (
        back_proj(grad_query_rows, query_full)
        + back_proj(grad_key_rows, key_full)
        + back_proj(grad_value_rows, value_full)
    )
    gain_one_grad = jnp.sum(grad_norm_one * (inputs * scale_one), axis=0)
    scaled_one = grad_norm_one * gain_one.astype(jnp.float32)
    grad_input = (
        grad_hidden_one
        + scale_one * scaled_one
        - inputs * scale_one**3 * jnp.mean(scaled_one * inputs, axis=-1, keepdims=True)
    )
    table_grad = table_back(near_grad, far_grad, table_full.shape[0])
    def shares(x, rows):
        x = x.reshape(x.shape[:-2] + (groups, rows, x.shape[-1]))
        def one(k, core):
            return lax.dynamic_index_in_dim(x, 2 * group.source_chip(k) + core, x.ndim - 3, keepdims=False)
        return [one(k, group.core) for k in range(chips)], [one(k, 1 - group.core) for k in range(chips)]

    rows = width // groups
    dense = jnp.stack([query_grad, key_grad, value_grad, output_grad]).astype(bf16)
    dense_own, dense_sib = shares(dense, rows)

    def lanes(x):
        return jnp.pad(x, ((0, 0), (0, 0), (0, 128 - x.shape[2])))

    heads = table_grad.shape[1]
    bias_rows = table_grad.shape[0] // groups
    prob_row = jnp.broadcast_to(jnp.sum(router_prob, axis=0), (groups, 1, experts))
    small = jnp.concatenate([
        lanes(gain_one_grad.reshape(groups, 1, rows)), lanes(gain_two_grad.reshape(groups, 1, rows)),
        lanes(prob_row), lanes(table_grad.reshape(groups, bias_rows, heads)),
        lanes(jnp.transpose(router_grad.T.reshape(experts, groups, rows), (1, 0, 2))),
    ], axis=1)
    small = jnp.pad(small, ((0, 0), (0, -small.shape[1] % 8), (0, 0)))
    small_own, small_sib = shares(small.reshape(-1, 128), small.shape[1])
    lines = -(-small_own[0].size // width)

    def pack_sums(matrices, rest):
        rest = jnp.pad(rest.reshape(-1), (0, lines * width - rest.size)).reshape(lines, width)
        high = lax.reduce_precision(rest, 8, 7)
        parts = (matrices.reshape(-1, width), high, rest - high)
        return jnp.concatenate([part.astype(bf16) for part in parts], axis=0)

    def unpack_sums(block):
        block = block.astype(f32)
        rest = block[-2 * lines:-lines] + block[-lines:]
        return block[:-2 * lines].reshape(dense_own[0].shape), rest.reshape(-1)[:small_own[0].size].reshape(small_own[0].shape)

    up_share, down_share = up_share.astype(f32), down_share.astype(f32)
    arriving, pins = None, y_ahead
    for k in list(range(1, chips)) + [0]:
        other, rest = group.swap(dense_sib[k]), group.swap(small_sib[k])
        if pins is not None:
            other = after(other, pins)
        dense_sum = dense_own[k].astype(f32) + other.astype(f32)
        small_sum = small_own[k] + rest
        if arriving is not None:
            more, rest = unpack_sums(arriving)
            dense_sum, small_sum = dense_sum + more, small_sum + rest
        if k > 0:
            block = pack_sums(dense_sum, small_sum)
            arriving = group.onward(block)
        pins = (up_share, grad_input) if k == 1 else None
        if k == chips - 1:
            y_steps.send(block)
    mixed = y_steps.send(dense_sum)[2]
    output = (hidden_one + mixed).astype(bf16)

    def over_rep(x):
        count = lax.axis_size("rep")
        return x.astype(f32), [lax.ppermute(x, "rep", [(i, i ^ k) for i in range(count)]) for k in range(1, count)]

    reps = lax.axis_size("rep")
    small, small_moved = over_rep(small_sum)
    if reps == dense_sum.shape[0]:
        me = lax.axis_index("rep")
        sent = dense_sum.astype(bf16)

        def swap_with(k, x):
            return lax.ppermute(x, "rep", [(i, i ^ k) for i in range(reps)])

        mine = lax.dynamic_index_in_dim(dense_sum, me, 0, keepdims=False)
        for k in range(1, reps):
            mine = mine + swap_with(k, lax.dynamic_index_in_dim(sent, me ^ k, 0, keepdims=False)).astype(f32)
        mine = mine.astype(bf16)
        whole = jnp.stack([mine] + after([swap_with(k, mine) for k in range(1, reps)], output))
        dense = [lax.dynamic_index_in_dim(whole, me ^ m, 0, keepdims=False).astype(f32) for m in range(reps)]
    else:
        dense, dense_moved = over_rep(dense_sum.astype(bf16))
        for got in after(dense_moved, output):
            dense = dense + got.astype(f32)
    for also in small_moved:
        small = small + also
    at = 3 + bias_rows
    balance_terms = experts * experts * fraction * (small[2, 0:experts] / all_tokens)
    loss = aux_weight / experts * jnp.sum(balance_terms)
    return (
        output,
        loss,
        balance_terms,
        grad_input,
        small[0, 0:rows],
        dense[0],
        dense[1],
        dense[2],
        dense[3],
        small[3:at, 0:heads],
        small[1, 0:rows],
        small[at:at + experts, 0:rows].T,
        up_share,
        down_share,
    )


def solution(mesh):
    return jax.shard_map(
        shards,
        mesh=mesh,
        in_specs=(
            P(("rep", "grp"), None),
            P(("rep", "grp")),
            P(("rep", "grp"), None),
            P("grp"),
            P("grp", None),
            P("grp", None),
            P("grp", None),
            P("grp", None),
            P("grp", None),
            P("grp"),
            P("grp", None),
            P("grp", None, None),
            P("grp", None, None),
            P(("rep", "grp"), None),
        ),
        out_specs=(
            P(("rep", "grp"), None),
            P(),
            P(),
            P(("rep", "grp"), None),
            P("grp"),
            P("grp", None),
            P("grp", None),
            P("grp", None),
            P("grp", None),
            P("grp", None),
            P("grp"),
            P("grp", None),
            P("grp", "rep", None),
            P("grp", "rep", None),
        ),
        check_vma=False,
    )
```
